128 devices in a mesh: lat: 8 (over x, core), lon: 16 (over z, y).
Axes of the slice: x: 4, y: 4, z: 4, core: 2. Of those that a mesh axis runs over, the one named last changes fastest.
Arguments:
- node_latents: bfloat16 [32768, 512], P(('lat', 'lon')), may hold values from -6 to 6
- edge_latents: bfloat16 [262144, 512], P(('lat', 'lon')), may hold values from -6 to 6
- edge_count: int32 [128], P(('lat', 'lon')), may hold values from 256 to 2048, as said below
- receiver: int32 [262144], P(('lat', 'lon')), may hold values from 0 to 255, as said below
- sender: int32 [262144], P(('lat', 'lon')), may hold values from 0 to 639, as said below
- halo_send: int32 [128, 4, 32], P(('lat', 'lon')), may hold values from 0 to 255
- far_send: int32 [128, 128, 2], P(('lat', 'lon')), may hold values from 0 to 255
- edge_weight_in: bfloat16 [1536, 512], replicated, may hold values from -0.15625 to 0.15625
- edge_bias: float32 [512], replicated, may hold values from -3 to 3
- edge_weight_out: bfloat16 [512, 512], replicated, may hold values from -0.25 to 0.25
- edge_gain: float32 [512], replicated, may hold values from 0.25 to 1.75
- node_weight_in: bfloat16 [1024, 512], replicated, may hold values from -0.1875 to 0.1875
- node_bias: float32 [512], replicated, may hold values from -3 to 3
- node_weight_out: bfloat16 [512, 512], replicated, may hold values from -0.25 to 0.25
- node_gain: float32 [512], replicated, may hold values from 0.25 to 1.75
- cot_nodes: bfloat16 [32768, 512], P(('lat', 'lon')), may hold values from -6 to 6
- cot_edges: bfloat16 [262144, 512], P(('lat', 'lon')), may hold values from -6 to 6
Outputs:
- node_out: bfloat16 [32768, 512], P(('lat', 'lon'))
- edge_out: bfloat16 [262144, 512], P(('lat', 'lon'))
- grad_nodes: bfloat16 [32768, 512], P(('lat', 'lon'))
- grad_edges: bfloat16 [262144, 512], P(('lat', 'lon'))
- grad_edge_weight_in: float32 [1536, 512], replicated
- grad_edge_bias: float32 [512], replicated
- grad_edge_weight_out: float32 [512, 512], replicated
- grad_edge_gain: float32 [512], replicated
- grad_node_weight_in: float32 [1024, 512], replicated
- grad_node_bias: float32 [512], replicated
- grad_node_weight_out: float32 [512, 512], replicated
- grad_node_gain: float32 [512], replicated
The draws below stay inside these ranges and needn't reach their ends.
Inputs may be any that keep to these rules, and one draw needn't show every extreme that they name: `edge_count`: edge slots of a device past its count are padding; some device has all 2048 slots live in every draw. `receiver`: nondecreasing within each device's 2048 edge slots. `sender`: rows below 256 are the device's own nodes, the next 128 the four neighbours' halo rows, the rest the 2 rows from each peer in device order; halo rows from a band that does not exist are never named.
All inputs are finite; a program needn't handle non-finite values.
Results may differ from the reference program's by a relative error of at most 0.017.
Values may be sent and summed in bfloat16 or wider, within the bound.
A program may use at most 128 MiB of HBM per device.

```python
from functools import partial
import jax
import jax.numpy as jnp
from jax import lax

D = 512
NODE_DEV = 256
BORDER = 32
CAP = 2
EDGE_DEV = 2048
NODES = 32768
EDGES = 262144
BANDS = 8
TILES = 16
N_LAT = 8
N_LON = 16
DEVICES = 128


def live_counts(key):
    key_one, key_two = jax.random.split(key)
    level_draw = jax.random.randint(key_one, (DEVICES,), 0, 64, dtype=jnp.int32)
    least_count = EDGE_DEV // 8
    counts = least_count + level_draw * level_draw * (EDGE_DEV - least_count) // 3969
    busiest = jax.random.randint(key_two, (), 0, DEVICES, dtype=jnp.int32)
    return counts.at[busiest].set(EDGE_DEV).astype(jnp.int32)


def draw_edge_count(key, part):
    return live_counts(key)


def draw_receiver(key, part):
    counts = live_counts(key)
    key = jax.random.fold_in(key, 2)
    drawn = jax.random.randint(key, (DEVICES, EDGE_DEV), 0, NODE_DEV, dtype=jnp.int32)
    position = jnp.arange(EDGE_DEV, dtype=jnp.int32)[None, :]
    drawn = jnp.where(position < counts[:, None], drawn, NODE_DEV)
    ordered = jnp.minimum(jnp.sort(drawn, axis=1), NODE_DEV - 1)
    return ordered.reshape(-1).astype(jnp.int32)


def draw_sender(key, part):
    key = jax.random.fold_in(key, 3)
    keys = jax.random.split(key, 5)
    grid_shape = (DEVICES, EDGE_DEV)
    category = jax.random.randint(keys[0], grid_shape, 0, 20, dtype=jnp.int32)
    own_index = jax.random.randint(keys[1], grid_shape, 0, NODE_DEV, dtype=jnp.int32)
    direction = jax.random.randint(keys[2], grid_shape, 0, 4, dtype=jnp.int32)
    band_index = (jnp.arange(DEVICES, dtype=jnp.int32) // TILES)[:, None]
    direction = jnp.where((band_index == 0) & (direction == 0), 1, direction)
    direction = jnp.where((band_index == BANDS - 1) & (direction == 1), 0, direction)
    position = jax.random.randint(keys[3], grid_shape, 0, BORDER, dtype=jnp.int32)
    offset = jax.random.randint(keys[4], (DEVICES, 1), 0, DEVICES * CAP, dtype=jnp.int32)
    edge_position = jnp.arange(EDGE_DEV, dtype=jnp.int32)[None, :]
    far_slot = (edge_position + offset) % (DEVICES * CAP)
    picked = jnp.where(category < 10, own_index, jnp.where(category < 15, NODE_DEV + direction * BORDER + position, NODE_DEV + 4 * BORDER + far_slot))
    return picked.reshape(-1).astype(jnp.int32)


def place_ends(values, own_key, least, largest):
    extent = values.shape
    spot = [jax.random.randint(jax.random.fold_in(own_key, axis), (), 0, extent[axis]) for axis in range(len(extent))]
    values = values.at[tuple(spot)].set(least)
    longest = extent.index(max(extent))
    spot[longest] = (spot[longest] + 1) % extent[longest]
    return values.at[tuple(spot)].set(largest)


def block_scale(rng, dims, cuts, least, largest):
    level, own = 1.0, jax.random.fold_in(rng, 6)
    for dim, blocks in cuts:
        draws = jnp.exp(jax.random.uniform(jax.random.fold_in(own, dim), (blocks,), jnp.float32, least / len(cuts), largest / len(cuts)))
        level = level * jnp.repeat(draws, dims[dim] // blocks).reshape([-1 if axis == dim else 1 for axis in range(len(dims))])
    return level


def scatter_about(key, shape, width, reach, cuts=(), kind=jnp.bfloat16):
    array = jax.random.normal(key, shape, jnp.float32) * width
    if len(cuts) > 0:
        array = block_scale(key, shape, cuts, -0.22, 0.18) * array
    return jnp.clip(array, min=-reach, max=reach).astype(kind)


def setup_inputs(seed: int = 0) -> dict:
    streams_of = jax.random.split(jax.random.key(seed), 18)
    return {
        "node_latents": scatter_about(streams_of[0], (NODES, D), 1.0, 6.0, ((0, 128),)),
        "edge_latents": scatter_about(streams_of[1], (EDGES, D), 1.0, 6.0, ((0, 128),)),
        "edge_count": draw_edge_count(jax.random.fold_in(streams_of[17], 71), 0),
        "receiver": draw_receiver(jax.random.fold_in(streams_of[17], 71), 0),
        "sender": draw_sender(jax.random.fold_in(streams_of[17], 71), 0),
        "halo_send": place_ends(jax.random.randint(streams_of[5], (DEVICES, 4, BORDER), 0, NODE_DEV), jax.random.fold_in(streams_of[5], 1), 0, NODE_DEV - 1).astype(jnp.int32),
        "far_send": place_ends(jax.random.randint(streams_of[6], (DEVICES, DEVICES, CAP), 0, NODE_DEV), jax.random.fold_in(streams_of[6], 1), 0, NODE_DEV - 1).astype(jnp.int32),
        "edge_weight_in": scatter_about(streams_of[7], (3 * D, D), (3 * D) ** -0.5, 0.15625),
        "edge_bias": scatter_about(streams_of[8], (D,), 0.5, 3.0, (), jnp.float32),
        "edge_weight_out": scatter_about(streams_of[9], (D, D), D ** -0.5, 0.25),
        "edge_gain": jnp.clip(1.0 + 0.15 * jax.random.normal(streams_of[10], (D,), jnp.float32), 0.25, 1.75),
        "node_weight_in": scatter_about(streams_of[11], (2 * D, D), (2 * D) ** -0.5, 0.1875),
        "node_bias": scatter_about(streams_of[12], (D,), 0.5, 3.0, (), jnp.float32),
        "node_weight_out": scatter_about(streams_of[13], (D, D), D ** -0.5, 0.25),
        "node_gain": jnp.clip(1.0 + 0.15 * jax.random.normal(streams_of[14], (D,), jnp.float32), 0.25, 1.75),
        "cot_nodes": scatter_about(streams_of[15], (NODES, D), 1.0, 6.0, ((0, 128),)),
        "cot_edges": scatter_about(streams_of[16], (EDGES, D), 1.0, 6.0, ((0, 128),)),
    }


EPSILON = 1e-05

def layer_norm(values, gain_out):
    row_mean = lax.optimization_barrier(jnp.mean(values, axis=-1, keepdims=True))
    centered = values - row_mean
    variance = lax.optimization_barrier(jnp.mean(centered * centered, axis=-1, keepdims=True))
    return centered * lax.rsqrt(variance + EPSILON) * gain_out

def edge_update(params, edge_rows, sender_rows, receiver_rows, live_mask):
    weight_in, bias_in, weight_out, gain_out = params
    joined = jnp.concatenate([edge_rows, sender_rows, receiver_rows], axis=1)
    first_layer = jnp.dot(joined, weight_in, preferred_element_type=jnp.float32) + bias_in
    active = jax.nn.silu(first_layer).astype(jnp.bfloat16)
    second = jnp.dot(active, weight_out, preferred_element_type=jnp.float32)
    message = layer_norm(second, gain_out) * live_mask[:, None]
    updated = (edge_rows.astype(jnp.float32) + message).astype(jnp.bfloat16)
    return (updated, message)

def node_update(params, node_rows, gathered):
    weight_in, bias_in, weight_out, gain_out = params
    joined = jnp.concatenate([node_rows, gathered], axis=1)
    first_layer = jnp.dot(joined, weight_in, preferred_element_type=jnp.float32) + bias_in
    active = jax.nn.silu(first_layer).astype(jnp.bfloat16)
    second = jnp.dot(active, weight_out, preferred_element_type=jnp.float32)
    return (node_rows.astype(jnp.float32) + layer_norm(second, gain_out)).astype(jnp.bfloat16)

def global_senders(sender_block, halo_send, far_send):
    device_count = N_LAT * N_LON
    device_ids = jnp.arange(device_count, dtype=jnp.int32)[:, None]
    band_index = device_ids // N_LON
    tile_index = device_ids % N_LON
    halo_part = sender_block - NODE_DEV
    far_part = sender_block - NODE_DEV - 4 * BORDER
    direction = jnp.clip(halo_part // BORDER, 0, 3).astype(jnp.int32)
    position = jnp.clip(halo_part, 0, 4 * BORDER - 1) % BORDER
    band_step = jnp.where(direction == 0, -1, jnp.where(direction == 1, 1, 0))
    tile_step = jnp.where(direction == 2, -1, jnp.where(direction == 3, 1, 0))
    near_band = band_index + band_step
    near_tile = (tile_index + tile_step) % N_LON
    inside = (near_band >= 0) & (near_band < N_LAT)
    neighbour = (jnp.clip(near_band, 0, N_LAT - 1) * N_LON + near_tile).astype(jnp.int32)
    list_index = jnp.bitwise_xor(direction, 1).astype(jnp.int32)
    halo_row = halo_send[neighbour, list_index, position]
    halo_global = jnp.where(inside, neighbour * NODE_DEV + halo_row, NODES)
    peer_index = jnp.clip(far_part // CAP, 0, device_count - 1).astype(jnp.int32)
    slot_index = (jnp.clip(far_part, 0, device_count * CAP - 1) % CAP).astype(jnp.int32)
    far_row = far_send[peer_index, jnp.broadcast_to(device_ids, peer_index.shape), slot_index]
    far_global = peer_index * NODE_DEV + far_row
    own_global = device_ids * NODE_DEV + sender_block
    picked = jnp.where(sender_block < NODE_DEV, own_global, jnp.where(far_part < 0, halo_global, far_global))
    return picked.astype(jnp.int32)

def reference(node_latents, edge_latents, edge_count, receiver, sender, halo_send, far_send, edge_weight_in, edge_bias, edge_weight_out, edge_gain, node_weight_in, node_bias, node_weight_out, node_gain, cot_nodes, cot_edges):
    device_count = N_LAT * N_LON
    feature_width = node_latents.shape[1]
    sender_index = global_senders(sender.reshape(device_count, EDGE_DEV), halo_send, far_send)
    padded = jnp.concatenate([node_latents, jnp.zeros((1, feature_width), jnp.bfloat16)], axis=0)
    edge_params = (edge_weight_in, edge_bias, edge_weight_out, edge_gain)
    node_params = (node_weight_in, node_bias, node_weight_out, node_gain)

    def one_device(accumulated, device_item):
        param_sums, spread = accumulated
        own_nodes, own_edges, live_count, receiver_block, sender_block, node_cot, edge_cot_in = device_item
        live_mask = (lax.iota(jnp.int32, EDGE_DEV) < live_count).astype(jnp.float32)
        sent_rows = padded[sender_block]
        received_rows = own_nodes[receiver_block]
        (new_edges, message), edge_back = jax.vjp(partial(edge_update, live_mask=live_mask), edge_params, own_edges, sent_rows, received_rows)
        gathered = jax.ops.segment_sum(message, receiver_block, NODE_DEV, indices_are_sorted=True).astype(jnp.bfloat16)
        new_nodes, node_back = jax.vjp(node_update, node_params, own_nodes, gathered)
        node_grads, from_node, from_gathered = node_back(node_cot)
        edge_grads, edge_grad, from_send, from_receive = edge_back((edge_cot_in, from_gathered.astype(jnp.float32)[receiver_block]))
        local_totals = from_node.astype(jnp.float32) + jax.ops.segment_sum(from_receive.astype(jnp.float32), receiver_block, NODE_DEV, indices_are_sorted=True)
        spread = spread.at[sender_block].add(from_send.astype(jnp.float32))
        every_grad = tuple(edge_grads) + tuple(node_grads)
        param_sums = tuple((total + grad.astype(jnp.float32) for total, grad in zip(param_sums, every_grad)))
        return ((param_sums, spread), (new_nodes, new_edges, edge_grad, local_totals))
    every_param = edge_params + node_params
    start_sums = tuple((jnp.zeros(param.shape, jnp.float32) for param in every_param))
    start_spread = jnp.zeros((NODES + 1, feature_width), jnp.float32)
    device_items = (node_latents.reshape(device_count, NODE_DEV, feature_width), edge_latents.reshape(device_count, EDGE_DEV, feature_width), edge_count.astype(jnp.int32), receiver.reshape(device_count, EDGE_DEV), sender_index, cot_nodes.reshape(device_count, NODE_DEV, feature_width), cot_edges.reshape(device_count, EDGE_DEV, feature_width))
    (param_sums, spread), (new_nodes, new_edges, edge_grads, local_totals) = lax.scan(one_device, (start_sums, start_spread), device_items)
    grad_nodes = (local_totals.reshape(NODES, feature_width) + spread[:NODES]).astype(jnp.bfloat16)
    return (new_nodes.reshape(NODES, feature_width), new_edges.reshape(EDGES, feature_width), grad_nodes, edge_grads.reshape(EDGES, feature_width), param_sums[0], param_sums[1], param_sums[2], param_sums[3], param_sums[4], param_sums[5], param_sums[6], param_sums[7])
```

```python
import functools

import jax
import jax.numpy as jnp
from jax import lax
from jax.experimental import pallas as pl
from jax.experimental.pallas import tpu as pltpu
from jax.sharding import PartitionSpec as P

EPS = 1e-05
F32 = jnp.float32
BF16 = jnp.bfloat16
MESH = pl.DeviceIdType.MESH
D = 512
N = 256
EDGES = 2048
HALO = 128
FAR = 256
TABLE = HALO + FAR
SLOTS = N + TABLE
CHUNK = 512
CHUNKS = EDGES // CHUNK
GROWS = 3584
FLAT = 4 * GROWS
HALF = FLAT // 2
SECTIONS = (48, 32, 32)
OFFSETS = (0, 64 * 48, 64 * 80)
VMEM_LIMIT = 60 * 1024 * 1024


def nn(a, b):
    return jnp.dot(a, b, preferred_element_type=F32)


def nt(a, b):
    return lax.dot_general(a, b, (((1,), (1,)), ((), ())), preferred_element_type=F32)


def tn(a, b):
    return lax.dot_general(a, b, (((0,), (0,)), ((), ())), preferred_element_type=F32)


def iota(shape, dim):
    return lax.broadcasted_iota(jnp.int32, shape, dim)


def one_hot(mask):
    return jnp.where(mask, 1.0, 0.0).astype(BF16)


def index_columns(row):
    count = row.shape[1] // 128
    parts = [jnp.broadcast_to(row[:, q * 128 : (q + 1) * 128], (128, 128)).T for q in range(count)]
    return parts[0] if count == 1 else jnp.concatenate(parts, axis=0)


def one_hot_rows(columns, first, blocks):
    lane = iota(columns.shape, 1)
    parts = [one_hot(columns == lane + (first + 128 * k)) for k in range(blocks)]
    return jnp.concatenate(parts, axis=1)


def position():
    return lax.axis_index("lat"), lax.axis_index("lon")


def entry_barrier(b, t):
    barrier = pltpu.get_barrier_semaphore()
    for step in range(1, 8):
        pl.semaphore_signal(barrier, inc=1, device_id=(lax.rem(b + step, 8), t), device_id_type=MESH)
    for step in range(1, 16):
        pl.semaphore_signal(barrier, inc=1, device_id=(b, lax.rem(t + step, 16)), device_id_type=MESH)
    pl.semaphore_wait(barrier, 22)


def send(src, dst, send_sem, recv_sem, device):
    pltpu.make_async_remote_copy(
        src_ref=src, dst_ref=dst, send_sem=send_sem, recv_sem=recv_sem, device_id=device, device_id_type=MESH
    ).start()


def wait_bytes(ref, sem):
    pltpu.make_async_copy(ref, ref, sem).wait()


def halo_swap(src, land, b, t, send_sem, recv_sem):
    down, up = (lax.rem(b + 7, 8), t), (lax.rem(b + 1, 8), t)
    left, right = (b, lax.rem(t + 15, 16)), (b, lax.rem(t + 1, 16))

    def part(ref, k):
        return ref.at[pl.ds(32 * k, 32)]

    @pl.when(b > 0)
    def _():
        send(part(src, 0), part(land, 1), send_sem.at[0], recv_sem.at[1], down)

    @pl.when(b < 7)
    def _():
        send(part(src, 1), part(land, 0), send_sem.at[1], recv_sem.at[0], up)

    send(part(src, 2), part(land, 3), send_sem.at[2], recv_sem.at[3], left)
    send(part(src, 3), part(land, 2), send_sem.at[3], recv_sem.at[2], right)


def halo_wait(src, land, b, send_sem, recv_sem):
    def part(ref, k):
        return ref.at[pl.ds(32 * k, 32)]

    @pl.when(b > 0)
    def _():
        wait_bytes(part(src, 0), send_sem.at[0])
        wait_bytes(part(land, 0), recv_sem.at[0])

    @pl.when(b < 7)
    def _():
        wait_bytes(part(src, 1), send_sem.at[1])
        wait_bytes(part(land, 1), recv_sem.at[1])

    for k in (2, 3):
        wait_bytes(part(src, k), send_sem.at[k])
        wait_bytes(part(land, k), recv_sem.at[k])


def swap_order(rows_major, cols_major):
    count = rows_major * cols_major * 2
    row, col = iota((count, count), 0), iota((count, count), 1)
    p, q, c = row // (2 * cols_major), lax.rem(row // 2, cols_major), lax.rem(row, 2)
    return one_hot(col == q * (2 * rows_major) + p * 2 + c)


def fetch_kernel(nodes, index, table, out_s, land_h, land_1, far_2, land_2, hs, hr, s1, r1, s2, r2):
    b, t = position()
    columns = index_columns(index[...])
    rows = nn(one_hot_rows(columns, 0, 2), nodes[...])
    out_s[...] = rows.astype(BF16)

    @pl.when(b == 0)
    def _():
        land_h[0:32, :] = jnp.zeros((32, D), BF16)

    @pl.when(b == 7)
    def _():
        land_h[32:64, :] = jnp.zeros((32, D), BF16)

    entry_barrier(b, t)
    for step in range(1, 16):
        peer = lax.rem(t + step, 16)
        send(
            out_s.at[pl.ds(pl.multiple_of(HALO + peer * 16, 16), 16)],
            land_1.at[pl.ds(pl.multiple_of(t * 16, 16), 16)],
            s1,
            r1,
            (b, peer),
        )
    halo_swap(out_s, land_h, b, t, hs, hr)
    land_1[pl.ds(pl.multiple_of(t * 16, 16), 16), :] = out_s[
        pl.ds(pl.multiple_of(HALO + t * 16, 16), 16), :
    ]
    wait_bytes(land_1.at[pl.ds(0, 240)], r1)
    far_2[...] = nn(swap_order(8, 16), land_1[...]).astype(BF16)
    for step in range(1, 8):
        peer = lax.rem(b + step, 8)
        send(
            far_2.at[pl.ds(pl.multiple_of(peer * 32, 16), 32)],
            land_2.at[pl.ds(pl.multiple_of(b * 32, 16), 32)],
            s2,
            r2,
            (peer, t),
        )
    land_2[pl.ds(pl.multiple_of(b * 32, 16), 32), :] = far_2[pl.ds(pl.multiple_of(b * 32, 16), 32), :]
    halo_wait(out_s, land_h, b, hs, hr)
    wait_bytes(out_s.at[pl.ds(0, 240)], s1)
    wait_bytes(land_2.at[pl.ds(0, 224)], r2)
    wait_bytes(far_2.at[pl.ds(0, 224)], s2)
    table[0:HALO, :] = land_h[...]
    table[HALO:TABLE, :] = land_2[...]


def norm_parts(values):
    mean = jnp.mean(values, axis=-1, keepdims=True)
    centered = values - mean
    variance = jnp.mean(centered * centered, axis=-1, keepdims=True)
    scale = lax.rsqrt(variance + EPS)
    return centered * scale, scale


def norm_back(grad, hat, scale):
    first = jnp.mean(grad, axis=-1, keepdims=True)
    second = jnp.mean(grad * hat, axis=-1, keepdims=True)
    return scale * (grad - first - hat * second)


def silu_parts(values):
    gate = 0.5 * jnp.tanh(0.5 * values) + 0.5
    active = values * gate
    return active, gate + active * (1.0 - gate)


def put_flat(ref, first, values):
    rows = values.shape[0]
    for k in range(4):
        ref[k * GROWS + first : k * GROWS + first + rows, :] = values[:, 128 * k : 128 * (k + 1)]


def put_small(ref, first, values):
    for k in range(4):
        ref[first + k : first + k + 1, :] = values[:, 128 * k : 128 * (k + 1)]


def step_kernel(
    count, sidx, ridx, nodes, table, cot_nodes, eb, eg, nb, ng,
    edges_h, cot_edges_h, ewi_h, ewo_h, nwi_h, nwo_h,
    node_out, totals, slots, flat, small, edge_out_h, grad_edges_h,
    edges, cots, ewi, ewo, nwi, nwo, rhs, ewoT, ewiT, active_s, slope_s, hat_s, scale_s, ohr_s,
    gathered, g_in, g_out, g_slots, g_bias, g_gain, eout, gout,
    in_sems, cot_sems, w_sems, out_sems,
):
    def block(ref, i):
        return ref.at[pl.ds(pl.multiple_of(i * CHUNK, CHUNK), CHUNK)]

    weights = [(ewi_h, ewi), (ewo_h, ewo), (nwi_h, nwi), (nwo_h, nwo)]

    def weight_copy(k):
        return pltpu.make_async_copy(weights[k][0], weights[k][1], w_sems.at[k])

    weight_copy(0).start()
    weight_copy(1).start()
    for i in range(CHUNKS):
        pltpu.make_async_copy(block(edges_h, i), block(edges, i), in_sems.at[i]).start()
    weight_copy(2).start()
    weight_copy(3).start()
    for i in range(CHUNKS):
        pltpu.make_async_copy(block(cot_edges_h, i), block(cots, i), cot_sems.at[i]).start()

    gathered[...] = jnp.zeros_like(gathered)
    g_in[...] = jnp.zeros_like(g_in)
    g_out[...] = jnp.zeros_like(g_out)
    g_slots[...] = jnp.zeros_like(g_slots)
    g_bias[...] = jnp.zeros_like(g_bias)
    g_gain[...] = jnp.zeros_like(g_gain)

    weight_copy(0).wait()
    rhs[0:D, :] = ewi[0:D, :]
    rhs[D : D + N, :] = nn(nodes[...], ewi[D : 2 * D, :]).astype(BF16)
    rhs[D + N : D + SLOTS, :] = nn(table[...], ewi[D : 2 * D, :]).astype(BF16)
    rhs[D + SLOTS :, :] = nn(nodes[...], ewi[2 * D :, :]).astype(BF16)
    ewiT[...] = ewi[0:D, :].T
    weight_copy(1).wait()
    ewoT[...] = ewo[...].T
    live = count[0]

    def rows_of(i):
        return pl.ds(pl.multiple_of(i * CHUNK, CHUNK), CHUNK)

    def live_mask(i):
        return jnp.where(iota((CHUNK, 1), 0) + i * CHUNK < live, 1.0, 0.0)

    def forward(i, carry):
        rows = rows_of(i)
        pltpu.make_async_copy(block(edges_h, i), block(edges, i), in_sems.at[i]).wait()
        r_row = ridx[:, rows]
        ohs = one_hot_rows(index_columns(sidx[:, rows]), 0, 5)
        ohr = one_hot_rows(index_columns(r_row), 0, 2)
        ohr_s[rows, :] = ohr
        e = edges[rows, :]
        first = nn(jnp.concatenate([e, ohs, ohr], axis=1), rhs[...]) + eb[...]
        active, slope = silu_parts(first)
        active = active.astype(BF16)
        active_s[rows, :] = active
        slope_s[rows, :] = slope.astype(BF16)
        hat, scale = norm_parts(nn(active, ewo[...]))
        hat_s[rows, :] = hat.astype(BF16)
        scale_s[rows, :] = scale
        message = hat * eg[...] * live_mask(i)
        eout[rows, :] = (e.astype(F32) + message).astype(BF16)
        pltpu.make_async_copy(block(eout, i), block(edge_out_h, i), out_sems.at[0, i]).start()
        ohr_t = one_hot(iota((N, CHUNK), 0) == r_row)
        gathered[...] += nn(ohr_t, message.astype(BF16))
        return carry

    lax.fori_loop(0, CHUNKS, forward, 0)

    weight_copy(2).wait()
    weight_copy(3).wait()
    x = nodes[...]
    got = gathered[...].astype(BF16)
    first = nn(x, nwi[0:D, :]) + nn(got, nwi[D:, :]) + nb[...]
    active, slope = silu_parts(first)
    active = active.astype(BF16)
    hat, scale = norm_parts(nn(active, nwo[...]))
    node_out[...] = (x.astype(F32) + hat * ng[...]).astype(BF16)
    cot = cot_nodes[...].astype(F32)
    put_small(small, 12, jnp.sum(cot * hat, axis=0, keepdims=True))
    d_second = norm_back(cot * ng[...], hat, scale).astype(BF16)
    put_flat(flat, 3072, tn(active, d_second).astype(BF16))
    d_first = nt(d_second, nwo[...]) * slope
    put_small(small, 8, jnp.sum(d_first, axis=0, keepdims=True))
    d_first = d_first.astype(BF16)
    put_flat(flat, 2048, tn(x, d_first).astype(BF16))
    put_flat(flat, 2560, tn(got, d_first).astype(BF16))
    totals[...] = nt(d_first, nwi[0:D, :]) + cot
    from_gathered = nt(d_first, nwi[D:, :]).astype(BF16)

    def backward(i, carry):
        rows = rows_of(i)
        pltpu.make_async_copy(block(cot_edges_h, i), block(cots, i), cot_sems.at[i]).wait()
        ce = cots[rows, :].astype(F32)
        hat = hat_s[rows, :].astype(F32)
        d_message = (ce + nn(ohr_s[rows, :], from_gathered)) * live_mask(i)
        g_gain[...] += jnp.sum(d_message * hat, axis=0, keepdims=True)
        d_second = norm_back(d_message * eg[...], hat, scale_s[rows, :]).astype(BF16)
        g_out[...] += tn(active_s[rows, :], d_second)
        d_first = nn(d_second, ewoT[...]) * slope_s[rows, :].astype(F32)
        g_bias[...] += jnp.sum(d_first, axis=0, keepdims=True)
        d_first = d_first.astype(BF16)
        gout[rows, :] = (nn(d_first, ewiT[...]) + ce).astype(BF16)
        pltpu.make_async_copy(block(gout, i), block(grad_edges_h, i), out_sems.at[1, i]).start()
        g_in[...] += tn(edges[rows, :], d_first)
        oh_t = jnp.concatenate(
            [one_hot(iota((SLOTS, CHUNK), 0) == sidx[:, rows]), one_hot(iota((N, CHUNK), 0) == ridx[:, rows])],
            axis=0,
        )
        g_slots[...] += nn(oh_t, d_first)
        return carry

    lax.fori_loop(0, CHUNKS, backward, 0)

    put_small(small, 0, g_bias[...])
    put_small(small, 4, g_gain[...])
    put_flat(flat, 0, g_in[...].astype(BF16))
    put_flat(flat, 1536, g_out[...].astype(BF16))
    gs = g_slots[...].astype(BF16)
    put_flat(
        flat,
        512,
        (tn(nodes[...], gs[0:N, :]) + tn(table[...], gs[N:SLOTS, :])).astype(BF16),
    )
    put_flat(flat, 1024, tn(nodes[...], gs[SLOTS:, :]).astype(BF16))
    totals[...] += nt(gs[0:N, :], ewi[D : 2 * D, :]) + nt(gs[SLOTS:, :], ewi[2 * D :, :])
    slots[...] = nt(gs[N:SLOTS, :], ewi[D : 2 * D, :]).astype(BF16)
    for i in range(CHUNKS):
        pltpu.make_async_copy(block(eout, i), block(edge_out_h, i), out_sems.at[0, i]).wait()
        pltpu.make_async_copy(block(gout, i), block(grad_edges_h, i), out_sems.at[1, i]).wait()


def reduce_kernel(
    flat, small, slots, index, totals, grad_nodes, result, small_out,
    half, land_c, land_x, land_y, land_z, mid_x, mid_y, sm, sm_land,
    land_h, land_1, far_2, land_2,
    hs, hr, s1, r1, s2, r2, ss, sr, gs, gr,
):
    b, t = position()
    core, x = lax.rem(b, 2), b // 2
    y, z = lax.rem(t, 4), t // 4
    entry_barrier(b, t)

    for step in range(1, 8):
        peer = lax.rem(b + step, 8)
        send(
            slots.at[pl.ds(pl.multiple_of(HALO + peer * 32, 16), 32)],
            land_1.at[pl.ds(pl.multiple_of(b * 32, 16), 32)],
            s1,
            r1,
            (peer, t),
        )
    halo_swap(slots, land_h, b, t, hs, hr)
    land_1[pl.ds(pl.multiple_of(b * 32, 16), 32), :] = slots[
        pl.ds(pl.multiple_of(HALO + b * 32, 16), 32), :
    ]

    @pl.when(b == 0)
    def _():
        land_h[0:32, :] = jnp.zeros((32, D), BF16)

    @pl.when(b == 7)
    def _():
        land_h[32:64, :] = jnp.zeros((32, D), BF16)

    def pick(axis, values):
        return jnp.where(axis == 0, values[0], jnp.where(axis == 1, values[1], values[2]))

    def axis_of(k, stage):
        return lax.rem(core + (k + stage), 3)

    def place(k, stage):
        return pick(axis_of(k, stage), (x, y, z))

    def mate(k, stage, step):
        axis = axis_of(k, stage)
        other = lax.rem(pick(axis, (x, y, z)) + step, 4)
        ox, oy, oz = (jnp.where(axis == a, other, v) for a, v in enumerate((x, y, z)))
        return other, (ox * 2 + core, oz * 4 + oy)

    core_mate = (x * 2 + (1 - core), t)

    def rows(start, size):
        return pl.ds(pl.multiple_of(start, 16), size)

    lands = (land_x, land_y, land_z)
    for k, s in enumerate(SECTIONS):
        send(
            flat.at[rows((1 - core) * HALF + OFFSETS[k], 64 * s)],
            land_c.at[rows(OFFSETS[k], 64 * s)],
            gs.at[0, k],
            gr.at[0, k],
            core_mate,
        )
    send(small, sm_land.at[0], ss.at[0], sr.at[0], core_mate)
    for k, s in enumerate(SECTIONS):
        mine = rows(OFFSETS[k], 64 * s)
        wait_bytes(land_c.at[mine], gr.at[0, k])
        total = flat[rows(core * HALF + OFFSETS[k], 64 * s), :].astype(F32) + land_c[mine, :].astype(F32)
        half[mine, :] = total.astype(BF16)
        for step in range(1, 4):
            other, device = mate(k, 0, step)
            send(
                half.at[rows(OFFSETS[k] + other * (16 * s), 16 * s)],
                land_x.at[rows((OFFSETS[k] // 64 * 16) * 3 + (step - 1) * 16 * s, 16 * s)],
                gs.at[1, k],
                gr.at[1, k],
                device,
            )
    wait_bytes(small, ss.at[0])
    wait_bytes(sm_land.at[0], sr.at[0])
    sm[0] = small[...] + sm_land[0]

    def small_stage(stage):
        own = (x, y, z)[stage]
        for step in range(1, 4):
            other = lax.rem(own + step, 4)
            ox, oy, oz = (other if a == stage else v for a, v in enumerate((x, y, z)))
            send(
                sm.at[stage],
                sm_land.at[1 + 4 * stage + own],
                ss.at[1 + stage],
                sr.at[1 + stage],
                (ox * 2 + core, oz * 4 + oy),
            )

    def small_finish(stage):
        own = (x, y, z)[stage]
        sm_land[1 + 4 * stage + own] = sm[stage]
        wait_bytes(sm_land.at[pl.ds(0, 3)], sr.at[1 + stage])
        wait_bytes(sm_land.at[pl.ds(0, 3)], ss.at[1 + stage])
        first = 1 + 4 * stage
        total = sm_land[first] + sm_land[first + 1] + sm_land[first + 2] + sm_land[first + 3]
        if stage < 2:
            sm[stage + 1] = total
        else:
            small_out[...] = total

    small_stage(0)
    wait_bytes(land_1.at[pl.ds(0, 224)], r1)
    far_2[...] = nn(swap_order(16, 8), land_1[...]).astype(BF16)
    for step in range(1, 16):
        peer = lax.rem(t + step, 16)
        send(
            far_2.at[rows(peer * 16, 16)],
            land_2.at[rows(t * 16, 16)],
            s2,
            r2,
            (b, peer),
        )
    land_2[rows(t * 16, 16), :] = far_2[rows(t * 16, 16), :]

    sources = (half, mid_x, mid_y)
    starts = (OFFSETS, tuple(o // 4 for o in OFFSETS), tuple(o // 16 for o in OFFSETS))
    for stage in range(3):
        part = (16, 4, 1)[stage]
        source, land = sources[stage], lands[stage]
        for k, s in enumerate(SECTIONS):
            size = part * s
            first = (OFFSETS[k] // 64 * part) * 3
            wait_bytes(land.at[rows(first, 3 * size)], gr.at[1 + stage, k])
            own = place(k, stage)
            total = source[rows(starts[stage][k] + own * size, size), :].astype(F32)
            for j in range(3):
                total = total + land[rows(first + j * size, size), :].astype(F32)
            total = total.astype(BF16)
            if stage < 2:
                target = sources[stage + 1]
                begin = starts[stage + 1][k]
                target[rows(begin, size), :] = total
                for step in range(1, 4):
                    other, device = mate(k, stage + 1, step)
                    piece = size // 4
                    next_first = (OFFSETS[k] // 64 * (part // 4)) * 3
                    send(
                        target.at[rows(begin + other * piece, piece)],
                        lands[stage + 1].at[rows(next_first + (step - 1) * piece, piece)],
                        gs.at[2 + stage, k],
                        gr.at[2 + stage, k],
                        device,
                    )
            else:
                result[final_rows(core, k, s, place, rows, 3), :] = total
                spread(result, core, k, s, place, mate, rows, 2, gs, gr)
        small_finish(stage)
        if stage < 2:
            small_stage(stage + 1)

    for stage in (2, 1, 0):
        for k, s in enumerate(SECTIONS):
            size = (16, 4, 1)[stage] * s
            wait_bytes(result.at[pl.ds(0, 3 * size)], gr.at[4 + stage, k])
            if stage > 0:
                spread(result, core, k, s, place, mate, rows, stage - 1, gs, gr)
            else:
                whole = result.at[rows(core * HALF + OFFSETS[k], 64 * s)]
                send(whole, whole, gs.at[7, k], gr.at[7, k], core_mate)

    halo_wait(slots, land_h, b, hs, hr)
    wait_bytes(slots.at[pl.ds(0, 224)], s1)
    wait_bytes(land_2.at[pl.ds(0, 240)], r2)
    wait_bytes(far_2.at[pl.ds(0, 240)], s2)
    back = jnp.concatenate([land_h[...], land_2[...]], axis=0)
    spread_rows = one_hot(iota((N, TABLE), 0) == index[...])
    grad_nodes[...] = (totals[...] + nn(spread_rows, back)).astype(BF16)

    for k, s in enumerate(SECTIONS):
        wait_bytes(result.at[pl.ds(0, 64 * s)], gr.at[7, k])
        wait_bytes(result.at[pl.ds(0, 64 * s)], gs.at[7, k])
        wait_bytes(flat.at[pl.ds(0, 64 * s)], gs.at[0, k])
        for stage in range(3):
            size = (16, 4, 1)[stage] * s
            wait_bytes(result.at[pl.ds(0, 3 * size)], gs.at[1 + stage, k])
            wait_bytes(result.at[pl.ds(0, 3 * size)], gs.at[4 + stage, k])


def final_rows(core, k, s, place, rows, depth):
    start = core * HALF + OFFSETS[k]
    size = 64 * s
    for stage in range(depth):
        size //= 4
        start = start + place(k, stage) * size
    return rows(start, size)


def spread(result, core, k, s, place, mate, rows, stage, gs, gr):
    block = result.at[final_rows(core, k, s, place, rows, stage + 1)]
    for step in range(1, 4):
        _, device = mate(k, stage, step)
        send(block, block, gs.at[4 + stage, k], gr.at[4 + stage, k], device)


def widen_kernel(flat, ewi, ewo, nwi, nwo):
    i = pl.program_id(0)

    def write(ref):
        for k in range(4):
            ref[:, 128 * k : 128 * (k + 1)] = flat[k].astype(F32)

    pl.when(i < 3)(lambda: write(ewi))
    pl.when(i == 3)(lambda: write(ewo))
    pl.when((i == 4) | (i == 5))(lambda: write(nwi))
    pl.when(i == 6)(lambda: write(nwo))


def vmem(count):
    return [pl.BlockSpec(memory_space=pltpu.VMEM)] * count


def shape(rows, dtype=BF16, width=D):
    return jax.ShapeDtypeStruct((rows, width), dtype)


def fetch(nodes, index):
    dma = pltpu.SemaphoreType.DMA
    return pl.pallas_call(
        fetch_kernel,
        out_shape=shape(TABLE),
        in_specs=vmem(2),
        out_specs=vmem(1)[0],
        scratch_shapes=[
            pltpu.VMEM((TABLE, D), BF16),
            pltpu.VMEM((HALO, D), BF16),
            pltpu.VMEM((FAR, D), BF16),
            pltpu.VMEM((FAR, D), BF16),
            pltpu.VMEM((FAR, D), BF16),
            dma((4,)),
            dma((4,)),
            dma(()),
            dma(()),
            dma(()),
            dma(()),
        ],
        compiler_params=pltpu.CompilerParams(
            collective_id=0, has_side_effects=True, vmem_limit_bytes=16 * 1024 * 1024
        ),
    )(nodes, index)


def compute(count, sidx, ridx, nodes, table, cot_nodes, eb, eg, nb, ng, edges, cots, ewi, ewo, nwi, nwo):
    dma = pltpu.SemaphoreType.DMA
    hbm = pl.BlockSpec(memory_space=pl.ANY)
    v = pltpu.VMEM
    return pl.pallas_call(
        step_kernel,
        out_shape=(
            shape(N),
            shape(N, F32),
            shape(TABLE),
            shape(FLAT, BF16, 128),
            shape(16, F32, 128),
            shape(EDGES),
            shape(EDGES),
        ),
        in_specs=[pl.BlockSpec(memory_space=pltpu.SMEM)] + vmem(9) + [hbm] * 6,
        out_specs=tuple(vmem(5) + [hbm] * 2),
        scratch_shapes=[
            v((EDGES, D), BF16),
            v((EDGES, D), BF16),
            v((3 * D, D), BF16),
            v((D, D), BF16),
            v((2 * D, D), BF16),
            v((D, D), BF16),
            v((D + SLOTS + N, D), BF16),
            v((D, D), BF16),
            v((D, D), BF16),
            v((EDGES, D), BF16),
            v((EDGES, D), BF16),
            v((EDGES, D), BF16),
            v((EDGES, 1), F32),
            v((EDGES, N), BF16),
            v((N, D), F32),
            v((D, D), F32),
            v((D, D), F32),
            v((SLOTS + N, D), F32),
            v((1, D), F32),
            v((1, D), F32),
            v((EDGES, D), BF16),
            v((EDGES, D), BF16),
            dma((CHUNKS,)),
            dma((CHUNKS,)),
            dma((4,)),
            dma((2, CHUNKS)),
        ],
        compiler_params=pltpu.CompilerParams(vmem_limit_bytes=VMEM_LIMIT),
    )(count, sidx, ridx, nodes, table, cot_nodes, eb, eg, nb, ng, edges, cots, ewi, ewo, nwi, nwo)


def reduce(flat, small, slots, index, totals):
    dma = pltpu.SemaphoreType.DMA
    v = pltpu.VMEM
    return pl.pallas_call(
        reduce_kernel,
        out_shape=(shape(N), shape(FLAT, BF16, 128), shape(16, F32, 128)),
        in_specs=vmem(5),
        out_specs=tuple(vmem(3)),
        scratch_shapes=[
            v((HALF, 128), BF16),
            v((HALF, 128), BF16),
            v((HALF // 4 * 3, 128), BF16),
            v((HALF // 16 * 3, 128), BF16),
            v((HALF // 64 * 3, 128), BF16),
            v((HALF // 4, 128), BF16),
            v((HALF // 16, 128), BF16),
            v((3, 16, 128), F32),
            v((13, 16, 128), F32),
            v((HALO, D), BF16),
            v((FAR, D), BF16),
            v((FAR, D), BF16),
            v((FAR, D), BF16),
            dma((4,)),
            dma((4,)),
            dma(()),
            dma(()),
            dma(()),
            dma(()),
            dma((4,)),
            dma((4,)),
            dma((8, 3)),
            dma((8, 3)),
        ],
        compiler_params=pltpu.CompilerParams(
            collective_id=1, has_side_effects=True, vmem_limit_bytes=48 * 1024 * 1024
        ),
    )(flat, small, slots, index, totals)


def widen(flat):
    def spec(least, most):
        return pl.BlockSpec((512, 512), lambda i: (jnp.clip(i - least, 0, most), 0))

    return pl.pallas_call(
        widen_kernel,
        grid=(7,),
        out_shape=(shape(1536, F32), shape(512, F32), shape(1024, F32), shape(512, F32)),
        in_specs=[pl.BlockSpec((4, 512, 128), lambda i: (0, i, 0))],
        out_specs=(spec(0, 2), spec(3, 0), spec(4, 1), spec(6, 0)),
    )(flat.reshape(4, GROWS, 128))


def shards(
    node_latents, edge_latents, edge_count, receiver, sender, halo_send, far_send,
    edge_weight_in, edge_bias, edge_weight_out, edge_gain,
    node_weight_in, node_bias, node_weight_out, node_gain, cot_nodes, cot_edges,
):
    halo = halo_send[0]
    far = far_send[0].reshape(8, 16, 2).transpose(1, 0, 2).reshape(1, FAR)
    index = jnp.concatenate([halo.reshape(1, HALO), far], axis=1)
    table = fetch(node_latents, index)
    node_out, totals, slots, flat, small, edge_out, grad_edges = compute(
        edge_count, sender.reshape(1, EDGES), receiver.reshape(1, EDGES),
        node_latents, table, cot_nodes,
        edge_bias.reshape(1, D), edge_gain.reshape(1, D), node_bias.reshape(1, D), node_gain.reshape(1, D),
        edge_latents, cot_edges, edge_weight_in, edge_weight_out, node_weight_in, node_weight_out,
    )
    grad_nodes, flat, small = reduce(flat, small, slots, index, totals)
    g_ewi, g_ewo, g_nwi, g_nwo = widen(flat)
    small = small.reshape(4, D)
    return (
        node_out, edge_out, grad_nodes, grad_edges,
        g_ewi, small[0], g_ewo, small[1], g_nwi, small[2], g_nwo, small[3],
    )


def solution(mesh):
    split = ("lat", "lon")
    rows, flat = P(split, None), P(split)
    cube, whole = P(split, None, None), P()
    return jax.shard_map(
        shards,
        mesh=mesh,
        in_specs=(rows, rows, flat, flat, flat, cube, cube) + (whole,) * 8 + (rows, rows),
        out_specs=(rows, rows, rows, rows) + (whole,) * 8,
        check_vma=False,
    )
```

```python
import functools

import jax
import jax.numpy as jnp
from jax import lax
from jax.experimental import pallas as pl
from jax.experimental.pallas import tpu as pltpu
from jax.sharding import PartitionSpec as P

EPS = 1e-05
F32 = jnp.float32
BF16 = jnp.bfloat16
MESH = pl.DeviceIdType.MESH
D = 512
N = 256
EDGES = 2048
HALO = 128
FAR = 256
TABLE = HALO + FAR
SLOTS = N + TABLE
CHUNK = 512
CHUNKS = EDGES // CHUNK
EDGE_ROWS = 2048
NODE_ROWS = 1536
EDGE_PARTS = (32, 16, 16)
NODE_PARTS = (16, 16, 16)
VMEM_LIMIT = 63 * 1024 * 1024


def nn(a, b):
    return jnp.dot(a, b, preferred_element_type=F32)


def nt(a, b):
    return lax.dot_general(a, b, (((1,), (1,)), ((), ())), preferred_element_type=F32)


def tn(a, b):
    return lax.dot_general(a, b, (((0,), (0,)), ((), ())), preferred_element_type=F32)


def iota(shape, dim):
    return lax.broadcasted_iota(jnp.int32, shape, dim)


def one_hot(mask):
    return jnp.where(mask, 1.0, 0.0).astype(BF16)


def index_columns(row):
    count = row.shape[1] // 128
    parts = [jnp.broadcast_to(row[:, q * 128 : (q + 1) * 128], (128, 128)).T for q in range(count)]
    return parts[0] if count == 1 else jnp.concatenate(parts, axis=0)


def one_hot_rows(columns, first, blocks):
    lane = iota(columns.shape, 1)
    parts = [one_hot(columns == lane + (first + 128 * k)) for k in range(blocks)]
    return jnp.concatenate(parts, axis=1)


def position():
    return lax.axis_index("lat"), lax.axis_index("lon")


def greet(b, t):
    barrier = pltpu.get_barrier_semaphore()
    for step in range(1, 8):
        pl.semaphore_signal(barrier, inc=1, device_id=(lax.rem(b + step, 8), t), device_id_type=MESH)
    for step in range(1, 16):
        pl.semaphore_signal(barrier, inc=1, device_id=(b, lax.rem(t + step, 16)), device_id_type=MESH)


def send(src, dst, send_sem, recv_sem, device):
    pltpu.make_async_remote_copy(
        src_ref=src, dst_ref=dst, send_sem=send_sem, recv_sem=recv_sem, device_id=device, device_id_type=MESH
    ).start()


def wait_bytes(ref, sem):
    pltpu.make_async_copy(ref, ref, sem).wait()


def halo_swap(src, land, b, t, send_sem, recv_sem):
    down, up = (lax.rem(b + 7, 8), t), (lax.rem(b + 1, 8), t)
    left, right = (b, lax.rem(t + 15, 16)), (b, lax.rem(t + 1, 16))

    def part(ref, k):
        return ref.at[pl.ds(32 * k, 32)]

    @pl.when(b > 0)
    def _():
        send(part(src, 0), part(land, 1), send_sem.at[0], recv_sem.at[1], down)

    @pl.when(b < 7)
    def _():
        send(part(src, 1), part(land, 0), send_sem.at[1], recv_sem.at[0], up)

    send(part(src, 2), part(land, 3), send_sem.at[2], recv_sem.at[3], left)
    send(part(src, 3), part(land, 2), send_sem.at[3], recv_sem.at[2], right)


def halo_wait(src, land, b, send_sem, recv_sem):
    def part(ref, k):
        return ref.at[pl.ds(32 * k, 32)]

    @pl.when(b > 0)
    def _():
        wait_bytes(part(src, 0), send_sem.at[0])
        wait_bytes(part(land, 0), recv_sem.at[0])

    @pl.when(b < 7)
    def _():
        wait_bytes(part(src, 1), send_sem.at[1])
        wait_bytes(part(land, 1), recv_sem.at[1])

    for k in (2, 3):
        wait_bytes(part(src, k), send_sem.at[k])
        wait_bytes(part(land, k), recv_sem.at[k])


def swap_order(rows_major, cols_major):
    count = rows_major * cols_major * 2
    row, col = iota((count, count), 0), iota((count, count), 1)
    p, q, c = row // (2 * cols_major), lax.rem(row // 2, cols_major), lax.rem(row, 2)
    return one_hot(col == q * (2 * rows_major) + p * 2 + c)


def norm_parts(values):
    mean = jnp.mean(values, axis=-1, keepdims=True)
    centered = values - mean
    variance = jnp.mean(centered * centered, axis=-1, keepdims=True)
    scale = lax.rsqrt(variance + EPS)
    return centered * scale, scale


def norm_back(grad, hat, scale):
    first = jnp.mean(grad, axis=-1, keepdims=True)
    second = jnp.mean(grad * hat, axis=-1, keepdims=True)
    return scale * (grad - first - hat * second)


def silu_parts(values):
    gate = 0.5 * jnp.tanh(0.5 * values) + 0.5
    active = values * gate
    return active, gate + active * (1.0 - gate)


def put_flat(ref, first, values):
    rows, total = values.shape[0], ref.shape[0] // 4
    for k in range(4):
        ref[k * total + first : k * total + first + rows, :] = values[:, 128 * k : 128 * (k + 1)]


def put_small(ref, first, values):
    for k in range(4):
        ref[first + k : first + k + 1, :] = values[:, 128 * k : 128 * (k + 1)]


def rows16(start, size):
    return pl.ds(pl.multiple_of(start, 16), size)


def pick(axis, values):
    return jnp.where(axis == 0, values[0], jnp.where(axis == 1, values[1], values[2]))


class Place:
    def __init__(self):
        self.b, self.t = position()
        self.core = lax.rem(self.b, 2)
        self.xyz = (self.b // 2, lax.rem(self.t, 4), self.t // 4)
        self.core_mate = (self.xyz[0] * 2 + (1 - self.core), self.t)

    def axis(self, k, stage):
        return lax.rem(self.core + (k + stage), 3)

    def own(self, k, stage):
        return pick(self.axis(k, stage), self.xyz)

    def mate(self, k, stage, step):
        axis = self.axis(k, stage)
        other = lax.rem(pick(axis, self.xyz) + step, 4)
        ox, oy, oz = (jnp.where(axis == a, other, v) for a, v in enumerate(self.xyz))
        return other, (ox * 2 + self.core, oz * 4 + oy)


class AllReduce:
    def __init__(self, place, parts, flat, result, half, land_c, lands, mids, gs, gr):
        self.at, self.parts, self.flat, self.result = place, parts, flat, result
        self.half, self.land_c, self.lands = half, land_c, lands
        self.sources = (half,) + mids
        self.gs, self.gr = gs, gr
        self.units = [sum(parts[:k]) for k in range(len(parts))]
        self.base = place.core * (flat.shape[0] // 2)
        self.other_base = (1 - place.core) * (flat.shape[0] // 2)

    def core_send(self):
        for k, s in enumerate(self.parts):
            first = 64 * self.units[k]
            send(
                self.flat.at[rows16(self.other_base + first, 64 * s)],
                self.land_c.at[rows16(first, 64 * s)],
                self.gs.at[0, k],
                self.gr.at[0, k],
                self.at.core_mate,
            )

    def send_parts(self, k, stage):
        size = (16, 4, 1)[stage] * self.parts[k]
        first = (64, 16, 4)[stage] * self.units[k]
        land_first = (16, 4, 1)[stage] * self.units[k] * 3
        for step in range(1, 4):
            other, device = self.at.mate(k, stage, step)
            send(
                self.sources[stage].at[rows16(first + other * size, size)],
                self.lands[stage].at[rows16(land_first + (step - 1) * size, size)],
                self.gs.at[1 + stage, k],
                self.gr.at[1 + stage, k],
                device,
            )

    def core_sum(self):
        for k, s in enumerate(self.parts):
            mine = rows16(64 * self.units[k], 64 * s)
            wait_bytes(self.land_c.at[mine], self.gr.at[0, k])
            own = self.flat[rows16(self.base + 64 * self.units[k], 64 * s), :]
            self.half[mine, :] = (own.astype(F32) + self.land_c[mine, :].astype(F32)).astype(BF16)
            self.send_parts(k, 0)

    def axis_sum(self, stage):
        for k, s in enumerate(self.parts):
            size = (16, 4, 1)[stage] * s
            first = (64, 16, 4)[stage] * self.units[k]
            land_first = (16, 4, 1)[stage] * self.units[k] * 3
            land = self.lands[stage]
            wait_bytes(land.at[rows16(land_first, 3 * size)], self.gr.at[1 + stage, k])
            total = self.sources[stage][rows16(first + self.at.own(k, stage) * size, size), :].astype(F32)
            for j in range(3):
                total = total + land[rows16(land_first + j * size, size), :].astype(F32)
            total = total.astype(BF16)
            if stage < 2:
                self.sources[stage + 1][rows16((16, 4)[stage] * self.units[k], size), :] = total
                self.send_parts(k, stage + 1)
            else:
                self.result[self.final(k, 3), :] = total
                self.spread(k, 2)

    def final(self, k, depth):
        start, size = self.base + 64 * self.units[k], 64 * self.parts[k]
        for stage in range(depth):
            size //= 4
            start = start + self.at.own(k, stage) * size
        return rows16(start, size)

    def spread(self, k, stage):
        block = self.result.at[self.final(k, stage + 1)]
        for step in range(1, 4):
            _, device = self.at.mate(k, stage, step)
            send(block, block, self.gs.at[4 + stage, k], self.gr.at[4 + stage, k], device)

    def back(self, stage):
        for k, s in enumerate(self.parts):
            size = (16, 4, 1)[stage] * s
            wait_bytes(self.result.at[pl.ds(0, 3 * size)], self.gr.at[4 + stage, k])
            if stage > 0:
                self.spread(k, stage - 1)
            else:
                whole = self.result.at[self.final(k, 0)]
                send(whole, whole, self.gs.at[7, k], self.gr.at[7, k], self.at.core_mate)

    def finish(self):
        for k, s in enumerate(self.parts):
            wait_bytes(self.result.at[pl.ds(0, 64 * s)], self.gr.at[7, k])
            wait_bytes(self.result.at[pl.ds(0, 64 * s)], self.gs.at[7, k])
            wait_bytes(self.flat.at[pl.ds(0, 64 * s)], self.gs.at[0, k])
            for stage in range(3):
                size = (16, 4, 1)[stage] * s
                wait_bytes(self.result.at[pl.ds(0, 3 * size)], self.gs.at[1 + stage, k])
                wait_bytes(self.result.at[pl.ds(0, 3 * size)], self.gs.at[4 + stage, k])


class SmallSum:
    def __init__(self, place, small, out, sums, land, ss, sr):
        self.at, self.small, self.out, self.sums, self.land = place, small, out, sums, land
        self.ss, self.sr = ss, sr

    def core_send(self):
        send(self.small, self.land.at[0], self.ss.at[0], self.sr.at[0], self.at.core_mate)

    def core_sum(self):
        wait_bytes(self.small, self.ss.at[0])
        wait_bytes(self.land.at[0], self.sr.at[0])
        self.sums[0] = self.small[...] + self.land[0]
        self.axis_send(0)

    def axis_send(self, stage):
        own = self.at.xyz[stage]
        for step in range(1, 4):
            other = lax.rem(own + step, 4)
            ox, oy, oz = (other if a == stage else v for a, v in enumerate(self.at.xyz))
            send(
                self.sums.at[stage],
                self.land.at[1 + 4 * stage + own],
                self.ss.at[1 + stage],
                self.sr.at[1 + stage],
                (ox * 2 + self.at.core, oz * 4 + oy),
            )

    def axis_sum(self, stage):
        first = 1 + 4 * stage
        self.land[first + self.at.xyz[stage]] = self.sums[stage]
        wait_bytes(self.land.at[pl.ds(0, 3)], self.sr.at[1 + stage])
        wait_bytes(self.land.at[pl.ds(0, 3)], self.ss.at[1 + stage])
        total = self.land[first] + self.land[first + 1] + self.land[first + 2] + self.land[first + 3]
        if stage < 2:
            self.sums[stage + 1] = total
            self.axis_send(stage + 1)
        else:
            self.out[...] = total


def step_kernel(
    count, halo_send_h, far_send_h, sidx_h, ridx_h, nodes_h, cot_nodes_h, eb_h, eg_h, nb_h, ng_h,
    edges_h, cot_edges_h, ewi_h, ewo_h, nwi_h, nwo_h,
    node_out, grad_nodes, edge_sum, node_sum, small_out, edge_out_h, grad_edges_h,
    halo_send, far_send, sidx, ridx, nodes, cot_nodes, eb, eg, nb, ng,
    edges, cots, ewi, ewo, nwi, nwo, rhs, rhs_far, ewoT, ewiT,
    first_s, active_s, slope_s, scale_s, ohr_s,
    picks, order, gathered, g_in, g_out, g_slots, g_bias, g_gain, totals, slots, small,
    out_s, table, land_1, far_2, edge_flat, node_flat,
    e_half, e_land_c, e_land_x, e_land_y, e_land_z, e_mid_x, e_mid_y,
    n_half, n_land_c, n_land_x, n_land_y, n_land_z, n_mid_x, n_mid_y,
    sm, sm_land, halo_back, land_1b, far_2b, land_2b,
    early_sems, in_sems, cot_sems, w_sems, out_sems,
    hs, hr, s1, r1, s2, r2, bhs, bhr, bs1, br1, bs2, br2, ss, sr, egs, egr, ngs, ngr,
):
    at = Place()
    b, t = at.b, at.t
    early = [
        pltpu.make_async_copy(source, target, early_sems.at[k])
        for k, (source, target) in enumerate(
            (
                (nodes_h, nodes), (halo_send_h, halo_send), (far_send_h, far_send), (sidx_h, sidx), (ridx_h, ridx),
                (eb_h, eb), (eg_h, eg), (nb_h, nb), (ng_h, ng), (cot_nodes_h, cot_nodes),
            )
        )
    ]
    for copy in early:
        copy.start()
    greet(b, t)

    def block(ref, i):
        return ref.at[pl.ds(pl.multiple_of(i * CHUNK, CHUNK), CHUNK)]

    weights = [(ewi_h, ewi), (ewo_h, ewo), (nwi_h, nwi), (nwo_h, nwo)]

    def weight_copy(k):
        return pltpu.make_async_copy(weights[k][0], weights[k][1], w_sems.at[k])

    weight_copy(0).start()
    for i in range(CHUNKS):
        pltpu.make_async_copy(block(edges_h, i), block(edges, i), in_sems.at[i]).start()
    for k in range(1, 4):
        weight_copy(k).start()
    for i in range(CHUNKS):
        pltpu.make_async_copy(block(cot_edges_h, i), block(cots, i), cot_sems.at[i]).start()

    for copy in early:
        copy.wait()
    x = nodes[...]
    halo_list = jnp.concatenate([halo_send[0, k : k + 1, :] for k in range(4)], axis=1)
    picks[0:HALO, :] = one_hot_rows(index_columns(halo_list), 0, 2)
    for c in range(2):
        wanted = index_columns(far_send[0, c : c + 1, :])
        picks[HALO + 128 * c : HALO + 128 * (c + 1), :] = one_hot_rows(wanted, 0, 2)
    out_s[0:HALO, :] = nn(picks[0:HALO, :], x).astype(BF16)
    far_rows = nn(picks[HALO:TABLE, :], x).astype(BF16)
    row, col = iota((FAR, FAR), 0), iota((FAR, FAR), 1)
    peer = lax.rem(col, 128)
    order[...] = one_hot(
        (lax.rem(row, 2) == col // 128) & (lax.rem(row // 2, 8) == peer // 16) & (row // 16 == lax.rem(peer, 16))
    )
    out_s[HALO:TABLE, :] = nn(order[...], far_rows).astype(BF16)

    @pl.when(b == 0)
    def _():
        table[0:32, :] = jnp.zeros((32, D), BF16)

    @pl.when(b == 7)
    def _():
        table[32:64, :] = jnp.zeros((32, D), BF16)

    pl.semaphore_wait(pltpu.get_barrier_semaphore(), 22)
    for step in range(1, 16):
        peer = lax.rem(t + step, 16)
        send(
            out_s.at[rows16(HALO + peer * 16, 16)], land_1.at[rows16(t * 16, 16)], s1, r1, (b, peer)
        )
    halo_swap(out_s, table, b, t, hs, hr)
    land_1[rows16(t * 16, 16), :] = out_s[rows16(HALO + t * 16, 16), :]

    gathered[...] = jnp.zeros_like(gathered)
    g_in[...] = jnp.zeros_like(g_in)
    g_out[...] = jnp.zeros_like(g_out)
    g_slots[...] = jnp.zeros_like(g_slots)
    g_bias[...] = jnp.zeros_like(g_bias)
    g_gain[...] = jnp.zeros_like(g_gain)

    weight_copy(0).wait()
    rhs[0:D, :] = ewi[0:D, :]
    rhs[D : D + N, :] = nn(x, ewi[D : 2 * D, :]).astype(BF16)
    rhs[D + N :, :] = nn(x, ewi[2 * D :, :]).astype(BF16)
    ewiT[...] = ewi[0:D, :].T
    live = count[0]

    def rows_of(i):
        return pl.ds(pl.multiple_of(i * CHUNK, CHUNK), CHUNK)

    def live_mask(i):
        return jnp.where(iota((CHUNK, 1), 0) + i * CHUNK < live, 1.0, 0.0)

    def local_part(i, carry):
        rows = rows_of(i)
        pltpu.make_async_copy(block(edges_h, i), block(edges, i), in_sems.at[i]).wait()
        own = one_hot_rows(index_columns(sidx[:, rows]), 0, 2)
        ohr = one_hot_rows(index_columns(ridx[:, rows]), 0, 2)
        ohr_s[rows, :] = ohr
        first_s[rows, :] = nn(jnp.concatenate([edges[rows, :], own, ohr], axis=1), rhs[...]) + eb[...]
        return carry

    lax.fori_loop(0, CHUNKS // 2, local_part, 0)
    wait_bytes(land_1.at[pl.ds(0, 240)], r1)
    far_2[...] = nn(swap_order(8, 16), land_1[...]).astype(BF16)
    for step in range(1, 8):
        peer = lax.rem(b + step, 8)
        send(
            far_2.at[rows16(peer * 32, 32)],
            table.at[rows16(HALO + b * 32, 32)],
            s2,
            r2,
            (peer, t),
        )
    table[rows16(HALO + b * 32, 32), :] = far_2[rows16(b * 32, 32), :]
    lax.fori_loop(CHUNKS // 2, CHUNKS, local_part, 0)
    weight_copy(1).wait()
    ewoT[...] = ewo[...].T
    halo_wait(out_s, table, b, hs, hr)
    wait_bytes(out_s.at[pl.ds(0, 240)], s1)
    wait_bytes(table.at[pl.ds(0, 224)], r2)
    wait_bytes(far_2.at[pl.ds(0, 224)], s2)
    rhs_far[...] = nn(table[...], ewi[D : 2 * D, :]).astype(BF16)

    def forward(i, carry):
        rows = rows_of(i)
        far = one_hot_rows(index_columns(sidx[:, rows]), N, 3)
        active, slope = silu_parts(first_s[rows, :] + nn(far, rhs_far[...]))
        active = active.astype(BF16)
        active_s[rows, :] = active
        slope_s[rows, :] = slope.astype(BF16)
        hat, scale = norm_parts(nn(active, ewo[...]))
        first_s[rows, :] = hat
        scale_s[rows, :] = scale
        message = hat * eg[...] * live_mask(i)
        ohr_t = one_hot(iota((N, CHUNK), 0) == ridx[:, rows])
        gathered[...] += nn(ohr_t, message.astype(BF16))
        return carry

    lax.fori_loop(0, CHUNKS, forward, 0)

    weight_copy(2).wait()
    weight_copy(3).wait()
    got = gathered[...].astype(BF16)
    first = nn(x, nwi[0:D, :]) + nn(got, nwi[D:, :]) + nb[...]
    active, slope = silu_parts(first)
    active = active.astype(BF16)
    hat, scale = norm_parts(nn(active, nwo[...]))
    node_out[...] = (x.astype(F32) + hat * ng[...]).astype(BF16)
    cot = cot_nodes[...].astype(F32)
    put_small(small, 12, jnp.sum(cot * hat, axis=0, keepdims=True))
    d_second = norm_back(cot * ng[...], hat, scale).astype(BF16)
    put_flat(node_flat, 1024, tn(active, d_second).astype(BF16))
    d_first = nt(d_second, nwo[...]) * slope
    put_small(small, 8, jnp.sum(d_first, axis=0, keepdims=True))
    d_first = d_first.astype(BF16)
    put_flat(node_flat, 0, tn(x, d_first).astype(BF16))
    put_flat(node_flat, 512, tn(got, d_first).astype(BF16))
    totals[...] = nt(d_first, nwi[0:D, :]) + cot
    from_gathered = nt(d_first, nwi[D:, :]).astype(BF16)

    node_ar = AllReduce(
        at, NODE_PARTS, node_flat, node_sum, n_half, n_land_c, (n_land_x, n_land_y, n_land_z),
        (n_mid_x, n_mid_y), ngs, ngr,
    )
    edge_ar = AllReduce(
        at, EDGE_PARTS, edge_flat, edge_sum, e_half, e_land_c, (e_land_x, e_land_y, e_land_z),
        (e_mid_x, e_mid_y), egs, egr,
    )
    small_ar = SmallSum(at, small, small_out, sm, sm_land, ss, sr)
    node_ar.core_send()

    def backward(i, carry):
        rows = rows_of(i)
        pltpu.make_async_copy(block(cot_edges_h, i), block(cots, i), cot_sems.at[i]).wait()
        ce = cots[rows, :].astype(F32)
        hat = first_s[rows, :]
        d_message = (ce + nn(ohr_s[rows, :], from_gathered)) * live_mask(i)
        g_gain[...] += jnp.sum(d_message * hat, axis=0, keepdims=True)
        d_second = norm_back(d_message * eg[...], hat, scale_s[rows, :]).astype(BF16)
        g_out[...] += tn(active_s[rows, :], d_second)
        d_first = nn(d_second, ewoT[...]) * slope_s[rows, :].astype(F32)
        g_bias[...] += jnp.sum(d_first, axis=0, keepdims=True)
        d_first = d_first.astype(BF16)
        slope_s[rows, :] = d_first
        g_in[...] += tn(edges[rows, :], d_first)
        oh_t = jnp.concatenate(
            [one_hot(iota((SLOTS, CHUNK), 0) == sidx[:, rows]), one_hot(iota((N, CHUNK), 0) == ridx[:, rows])],
            axis=0,
        )
        g_slots[...] += nn(oh_t, d_first)
        pl.when(i == 0)(node_ar.core_sum)
        pl.when(i == 2)(functools.partial(node_ar.axis_sum, 0))
        return carry

    lax.fori_loop(0, CHUNKS, backward, 0)

    put_small(small, 0, g_bias[...])
    put_small(small, 4, g_gain[...])
    put_flat(edge_flat, 0, g_in[...].astype(BF16))
    put_flat(edge_flat, 1536, g_out[...].astype(BF16))
    gs = g_slots[...].astype(BF16)
    put_flat(edge_flat, 512, (tn(x, gs[0:N, :]) + tn(table[...], gs[N:SLOTS, :])).astype(BF16))
    put_flat(edge_flat, 1024, tn(x, gs[SLOTS:, :]).astype(BF16))
    edge_ar.core_send()
    small_ar.core_send()

    slots[...] = nt(gs[N:SLOTS, :], ewi[D : 2 * D, :]).astype(BF16)
    for step in range(1, 8):
        peer = lax.rem(b + step, 8)
        send(
            slots.at[rows16(HALO + peer * 32, 32)], land_1b.at[rows16(b * 32, 32)], bs1, br1, (peer, t)
        )
    halo_swap(slots, halo_back, b, t, bhs, bhr)
    land_1b[rows16(b * 32, 32), :] = slots[rows16(HALO + b * 32, 32), :]

    @pl.when(b == 0)
    def _():
        halo_back[0:32, :] = jnp.zeros((32, D), BF16)

    @pl.when(b == 7)
    def _():
        halo_back[32:64, :] = jnp.zeros((32, D), BF16)

    def edge_grad(i):
        rows = slice(i * CHUNK, (i + 1) * CHUNK)
        cots[rows, :] = (nn(slope_s[rows, :], ewiT[...]) + cots[rows, :].astype(F32)).astype(BF16)
        pltpu.make_async_copy(block(cots, i), block(grad_edges_h, i), out_sems.at[1, i]).start()

    def edge_result(i):
        rows = slice(i * CHUNK, (i + 1) * CHUNK)
        message = first_s[rows, :] * (eg[...] * live_mask(i))
        edges[rows, :] = (edges[rows, :].astype(F32) + message).astype(BF16)
        pltpu.make_async_copy(block(edges, i), block(edge_out_h, i), out_sems.at[0, i]).start()

    node_ar.axis_sum(1)
    edge_ar.core_sum()
    small_ar.core_sum()
    node_ar.axis_sum(2)
    for i in range(CHUNKS):
        edge_grad(i)
    totals[...] += nt(gs[0:N, :], ewi[D : 2 * D, :]) + nt(gs[SLOTS:, :], ewi[2 * D :, :])
    wait_bytes(land_1b.at[pl.ds(0, 224)], br1)
    far_2b[...] = nn(swap_order(16, 8), land_1b[...]).astype(BF16)
    for step in range(1, 16):
        peer = lax.rem(t + step, 16)
        send(
            far_2b.at[rows16(peer * 16, 16)], land_2b.at[rows16(t * 16, 16)], bs2, br2, (b, peer)
        )
    land_2b[rows16(t * 16, 16), :] = far_2b[rows16(t * 16, 16), :]
    node_ar.back(2)
    edge_ar.axis_sum(0)
    small_ar.axis_sum(0)
    edge_result(0)
    edge_result(1)
    node_ar.back(1)
    edge_ar.axis_sum(1)
    small_ar.axis_sum(1)
    edge_result(2)
    edge_result(3)
    edge_ar.axis_sum(2)
    small_ar.axis_sum(2)
    halo_wait(slots, halo_back, b, bhs, bhr)
    wait_bytes(slots.at[pl.ds(0, 224)], bs1)
    wait_bytes(land_2b.at[pl.ds(0, 240)], br2)
    wait_bytes(far_2b.at[pl.ds(0, 240)], bs2)
    far_back = tn(order[...], land_2b[...]).astype(BF16)
    returned = tn(picks[...], jnp.concatenate([halo_back[...], far_back], axis=0))
    grad_nodes[...] = (totals[...] + returned).astype(BF16)
    node_ar.back(0)
    for stage in (2, 1, 0):
        edge_ar.back(stage)
    for i in range(CHUNKS):
        pltpu.make_async_copy(block(edges, i), block(edge_out_h, i), out_sems.at[0, i]).wait()
        pltpu.make_async_copy(block(cots, i), block(grad_edges_h, i), out_sems.at[1, i]).wait()
    node_ar.finish()
    edge_ar.finish()


def final_kernel(
    edge_sum, node_sum, small, node_out, edge_out, grad_nodes, grad_edges,
    node_out_h, edge_out_h, grad_nodes_h, grad_edges_h, ewi_h, eb, ewo_h, eg, nwi_h, nb, nwo_h, ng,
    wide, parts, small_s, rows_s, through, in_sems, move_sems, sems,
):
    targets = [(nwi_h, 0, node_sum, 0), (nwi_h, 512, node_sum, 512), (nwo_h, 0, node_sum, 1024)]
    targets += [(ewi_h, 0, edge_sum, 0), (ewi_h, 512, edge_sum, 512), (ewi_h, 1024, edge_sum, 1024)]
    targets += [(ewo_h, 0, edge_sum, 1536)]

    def fetch(j):
        _, _, source, first = targets[j]
        return pltpu.make_async_copy(source.at[:, pl.ds(first, 512), :], parts.at[j], in_sems.at[j])

    small_copy = pltpu.make_async_copy(small, small_s, in_sems.at[7])
    for j in range(len(targets)):
        fetch(j).start()
    small_copy.start()
    copies = []
    moves = [(node_out, node_out_h, 0, N), (grad_nodes, grad_nodes_h, 0, N)]
    for i in range(CHUNKS):
        moves += [(edge_out, edge_out_h, i * CHUNK, CHUNK), (grad_edges, grad_edges_h, i * CHUNK, CHUNK)]
    places = [sum(size for _, _, _, size in moves[:j]) for j in range(len(moves))]

    def move(j, inward):
        source, target, first, size = moves[j]
        near = through.at[pl.ds(places[j], size)]
        if inward:
            return pltpu.make_async_copy(source.at[pl.ds(first, size)], near, move_sems.at[0, j])
        return pltpu.make_async_copy(near, target.at[pl.ds(first, size)], move_sems.at[1, j])

    for j in range(len(moves)):
        move(j, True).start()
    for j in range(len(moves)):
        move(j, True).wait()
        move(j, False).start()
        copies.append(move(j, False))
    for j, (ref, out_first, _, _) in enumerate(targets):
        fetch(j).wait()
        for k in range(4):
            wide[512 * j : 512 * (j + 1), 128 * k : 128 * (k + 1)] = parts[j, k].astype(F32)
        copy = pltpu.make_async_copy(
            wide.at[pl.ds(512 * j, 512)], ref.at[pl.ds(out_first, 512)], sems.at[4 + j]
        )
        copy.start()
        copies.append(copy)
    small_copy.wait()
    for j, ref in enumerate((eb, eg, nb, ng)):
        for k in range(4):
            rows_s[j, :, 128 * k : 128 * (k + 1)] = small_s[4 * j + k : 4 * j + k + 1, :]
        copy = pltpu.make_async_copy(rows_s.at[j], ref, sems.at[11 + j])
        copy.start()
        copies.append(copy)
    for copy in copies:
        copy.wait()


def vmem(count):
    return [pl.BlockSpec(memory_space=pltpu.VMEM)] * count


def shape(rows, dtype=BF16, width=D):
    return jax.ShapeDtypeStruct((rows, width), dtype)


def reduce_scratch(total):
    v, half = pltpu.VMEM, total // 2
    return [
        v((half, 128), BF16),
        v((half, 128), BF16),
        v((half // 4 * 3, 128), BF16),
        v((half // 16 * 3, 128), BF16),
        v((half // 64 * 3, 128), BF16),
        v((half // 4, 128), BF16),
        v((half // 16, 128), BF16),
    ]


def step(*operands):
    dma = pltpu.SemaphoreType.DMA
    hbm = pl.BlockSpec(memory_space=pltpu.HBM)
    v = pltpu.VMEM
    wide = v((EDGES, D), BF16)
    square = v((D, D), BF16)
    total = v((D, D), F32)
    return pl.pallas_call(
        step_kernel,
        out_shape=(
            shape(N),
            shape(N),
            shape(4 * EDGE_ROWS, BF16, 128),
            shape(4 * NODE_ROWS, BF16, 128),
            shape(16, F32, 128),
            shape(EDGES),
            shape(EDGES),
        ),
        in_specs=[pl.BlockSpec(memory_space=pltpu.SMEM)] + [hbm] * 16,
        out_specs=tuple(vmem(5) + [hbm] * 2),
        scratch_shapes=[
            v((1, 4, 32), jnp.int32),
            v((1, 2, 128), jnp.int32),
            v((1, EDGES), jnp.int32),
            v((1, EDGES), jnp.int32),
            v((N, D), BF16),
            v((N, D), BF16),
            v((1, D), F32),
            v((1, D), F32),
            v((1, D), F32),
            v((1, D), F32),
            wide,
            wide,
            v((3 * D, D), BF16),
            square,
            v((2 * D, D), BF16),
            square,
            v((D + 2 * N, D), BF16),
            v((TABLE, D), BF16),
            square,
            square,
            v((EDGES, D), F32),
            wide,
            wide,
            v((EDGES, 1), F32),
            v((EDGES, N), BF16),
            v((TABLE, N), BF16),
            v((FAR, FAR), BF16),
            v((N, D), F32),
            total,
            total,
            v((SLOTS + N, D), F32),
            v((1, D), F32),
            v((1, D), F32),
            v((N, D), F32),
            v((TABLE, D), BF16),
            v((16, 128), F32),
            v((TABLE, D), BF16),
            v((TABLE, D), BF16),
            v((FAR, D), BF16),
            v((FAR, D), BF16),
            v((4 * EDGE_ROWS, 128), BF16),
            v((4 * NODE_ROWS, 128), BF16),
        ]
        + reduce_scratch(4 * EDGE_ROWS)
        + reduce_scratch(4 * NODE_ROWS)
        + [
            v((3, 16, 128), F32),
            v((13, 16, 128), F32),
            v((HALO, D), BF16),
            v((FAR, D), BF16),
            v((FAR, D), BF16),
            v((FAR, D), BF16),
            dma((10,)),
            dma((CHUNKS,)),
            dma((CHUNKS,)),
            dma((4,)),
            dma((2, CHUNKS)),
        ]
        + [dma((4,)), dma((4,)), dma(()), dma(()), dma(()), dma(())] * 2
        + [dma((4,)), dma((4,)), dma((8, 3)), dma((8, 3)), dma((8, 3)), dma((8, 3))],
        compiler_params=pltpu.CompilerParams(
            collective_id=0, has_side_effects=True, vmem_limit_bytes=VMEM_LIMIT
        ),
    )(*operands)


def final(edge_sum, node_sum, small, node_out, edge_out, grad_nodes, grad_edges):
    hbm = pl.BlockSpec(memory_space=pl.ANY)
    v, dma = pltpu.VMEM, pltpu.SemaphoreType.DMA
    return pl.pallas_call(
        final_kernel,
        out_shape=(
            shape(N), shape(EDGES), shape(N), shape(EDGES),
            shape(1536, F32), shape(1, F32), shape(512, F32), shape(1, F32),
            shape(1024, F32), shape(1, F32), shape(512, F32), shape(1, F32),
        ),
        in_specs=[hbm] * 7,
        out_specs=(hbm,) * 12,
        scratch_shapes=[
            v((3584, D), F32),
            v((7, 4, 512, 128), BF16),
            v((16, 128), F32),
            v((4, 1, D), F32),
            v((2 * N + 2 * EDGES, D), BF16),
            dma((8,)),
            dma((2, 2 + 2 * CHUNKS)),
            dma((15,)),
        ],
        compiler_params=pltpu.CompilerParams(vmem_limit_bytes=VMEM_LIMIT),
    )(edge_sum.reshape(4, EDGE_ROWS, 128), node_sum.reshape(4, NODE_ROWS, 128), small, node_out, edge_out, grad_nodes, grad_edges)


def shards(
    node_latents, edge_latents, edge_count, receiver, sender, halo_send, far_send,
    edge_weight_in, edge_bias, edge_weight_out, edge_gain,
    node_weight_in, node_bias, node_weight_out, node_gain, cot_nodes, cot_edges,
):
    node_out, grad_nodes, edge_sum, node_sum, small, edge_out, grad_edges = step(
        edge_count, halo_send, far_send.transpose(0, 2, 1), sender.reshape(1, EDGES), receiver.reshape(1, EDGES),
        node_latents, cot_nodes,
        edge_bias.reshape(1, D), edge_gain.reshape(1, D), node_bias.reshape(1, D), node_gain.reshape(1, D),
        edge_latents, cot_edges, edge_weight_in, edge_weight_out, node_weight_in, node_weight_out,
    )
    outs = final(edge_sum, node_sum, small, node_out, edge_out, grad_nodes, grad_edges)
    return tuple(out.reshape(D) if out.shape[0] == 1 else out for out in outs)


def solution(mesh):
    split = ("lat", "lon")
    rows, flat = P(split, None), P(split)
    cube, whole = P(split, None, None), P()
    return jax.shard_map(
        shards,
        mesh=mesh,
        in_specs=(rows, rows, flat, flat, flat, cube, cube) + (whole,) * 8 + (rows, rows),
        out_specs=(rows, rows, rows, rows) + (whole,) * 8,
        check_vma=False,
    )
```

```python
import functools

import jax
import jax.numpy as jnp
from jax import lax
from jax.experimental import pallas as pl
from jax.experimental.pallas import tpu as pltpu
from jax.sharding import PartitionSpec as P

EPS = 1e-05
F32 = jnp.float32
BF16 = jnp.bfloat16
MESH = pl.DeviceIdType.MESH
D = 512
N = 256
EDGES = 2048
HALO = 128
FAR = 256
TABLE = HALO + FAR
SLOTS = N + TABLE
CHUNK = 512
CHUNKS = EDGES // CHUNK
EDGE_ROWS = 2048
NODE_ROWS = 1536
EDGE_PARTS = (32, 16, 16)
NODE_PARTS = (16, 16, 16)
VMEM_LIMIT = 63 * 1024 * 1024


def nn(a, b):
    return jnp.dot(a, b, preferred_element_type=F32)


def nt(a, b):
    return lax.dot_general(a, b, (((1,), (1,)), ((), ())), preferred_element_type=F32)


def tn(a, b):
    return lax.dot_general(a, b, (((0,), (0,)), ((), ())), preferred_element_type=F32)


def iota(shape, dim):
    return lax.broadcasted_iota(jnp.int32, shape, dim)


def one_hot(mask):
    return jnp.where(mask, 1.0, 0.0).astype(BF16)


def index_columns(row):
    count = row.shape[1] // 128
    parts = [jnp.broadcast_to(row[:, q * 128 : (q + 1) * 128], (128, 128)).T for q in range(count)]
    return parts[0] if count == 1 else jnp.concatenate(parts, axis=0)


def one_hot_rows(columns, first, blocks):
    lane = iota(columns.shape, 1)
    parts = [one_hot(columns == lane + (first + 128 * k)) for k in range(blocks)]
    return jnp.concatenate(parts, axis=1)


def position():
    return lax.axis_index("lat"), lax.axis_index("lon")


def greet(b, t):
    barrier = pltpu.get_barrier_semaphore()
    for step in range(1, 8):
        pl.semaphore_signal(barrier, inc=1, device_id=(lax.rem(b + step, 8), t), device_id_type=MESH)
    for step in range(1, 16):
        pl.semaphore_signal(barrier, inc=1, device_id=(b, lax.rem(t + step, 16)), device_id_type=MESH)


def send(src, dst, send_sem, recv_sem, device):
    pltpu.make_async_remote_copy(
        src_ref=src, dst_ref=dst, send_sem=send_sem, recv_sem=recv_sem, device_id=device, device_id_type=MESH
    ).start()


def wait_bytes(ref, sem):
    pltpu.make_async_copy(ref, ref, sem).wait()


def halo_swap(src, land, b, t, send_sem, recv_sem):
    down, up = (lax.rem(b + 7, 8), t), (lax.rem(b + 1, 8), t)
    left, right = (b, lax.rem(t + 15, 16)), (b, lax.rem(t + 1, 16))

    def part(ref, k):
        return ref.at[pl.ds(32 * k, 32)]

    @pl.when(b > 0)
    def _():
        send(part(src, 0), part(land, 1), send_sem.at[0], recv_sem.at[1], down)

    @pl.when(b < 7)
    def _():
        send(part(src, 1), part(land, 0), send_sem.at[1], recv_sem.at[0], up)

    send(part(src, 2), part(land, 3), send_sem.at[2], recv_sem.at[3], left)
    send(part(src, 3), part(land, 2), send_sem.at[3], recv_sem.at[2], right)


def halo_wait(src, land, b, send_sem, recv_sem):
    def part(ref, k):
        return ref.at[pl.ds(32 * k, 32)]

    @pl.when(b > 0)
    def _():
        wait_bytes(part(src, 0), send_sem.at[0])
        wait_bytes(part(land, 0), recv_sem.at[0])

    @pl.when(b < 7)
    def _():
        wait_bytes(part(src, 1), send_sem.at[1])
        wait_bytes(part(land, 1), recv_sem.at[1])

    for k in (2, 3):
        wait_bytes(part(src, k), send_sem.at[k])
        wait_bytes(part(land, k), recv_sem.at[k])


def swap_order(rows_major, cols_major):
    count = rows_major * cols_major * 2
    row, col = iota((count, count), 0), iota((count, count), 1)
    p, q, c = row // (2 * cols_major), lax.rem(row // 2, cols_major), lax.rem(row, 2)
    return one_hot(col == q * (2 * rows_major) + p * 2 + c)


def norm_parts(values):
    mean = jnp.mean(values, axis=-1, keepdims=True)
    centered = values - mean
    variance = jnp.mean(centered * centered, axis=-1, keepdims=True)
    scale = lax.rsqrt(variance + EPS)
    return centered * scale, scale


def norm_back(grad, hat, scale):
    first = jnp.mean(grad, axis=-1, keepdims=True)
    second = jnp.mean(grad * hat, axis=-1, keepdims=True)
    return scale * (grad - first - hat * second)


def silu_parts(values):
    gate = 0.5 * jnp.tanh(0.5 * values) + 0.5
    active = values * gate
    return active, gate + active * (1.0 - gate)


def put_flat(ref, piece, values):
    half = ref.shape[0] // 2
    for k in range(4):
        first = (k // 2) * half + piece * 1024 + (k % 2) * 512
        ref[first : first + 512, :] = values[:, 128 * k : 128 * (k + 1)]


def put_small(ref, first, values):
    for k in range(4):
        ref[first + k : first + k + 1, :] = values[:, 128 * k : 128 * (k + 1)]


def rows16(start, size):
    return pl.ds(pl.multiple_of(start, 16), size)


def pick(axis, values):
    return jnp.where(axis == 0, values[0], jnp.where(axis == 1, values[1], values[2]))


class Place:
    def __init__(self):
        self.b, self.t = position()
        self.core = lax.rem(self.b, 2)
        self.xyz = (self.b // 2, lax.rem(self.t, 4), self.t // 4)
        self.core_mate = (self.xyz[0] * 2 + (1 - self.core), self.t)

    def axis(self, k, stage):
        return lax.rem(self.core + (k + stage), 3)

    def own(self, k, stage):
        return pick(self.axis(k, stage), self.xyz)

    def mate(self, k, step):
        axis = self.axis(k, 0)
        other = lax.rem(pick(axis, self.xyz) + step, 4)
        ox, oy, oz = (jnp.where(axis == a, other, v) for a, v in enumerate(self.xyz))
        return ox * 2 + self.core, oz * 4 + oy

    def plane_mate(self, k, step):
        second, third = self.axis(k, 1), self.axis(k, 2)
        c2 = lax.rem(pick(second, self.xyz) + step // 4, 4)
        c3 = lax.rem(pick(third, self.xyz) + lax.rem(step, 4), 4)
        ox, oy, oz = (
            jnp.where(second == a, c2, jnp.where(third == a, c3, v)) for a, v in enumerate(self.xyz)
        )
        return c2 * 4 + c3, (ox * 2 + self.core, oz * 4 + oy)


class AllReduce:
    def __init__(self, place, parts, flat, result, half, land_c, land_a, land_p, mid, sems):
        self.at, self.parts, self.flat, self.result = place, parts, flat, result
        self.half, self.land_c, self.land_a, self.land_p, self.mid = half, land_c, land_a, land_p, mid
        self.gs, self.gr, self.cr, self.ar = sems
        self.units = [sum(parts[:k]) for k in range(len(parts))]
        self.base = place.core * (flat.shape[0] // 2)
        self.other_base = (1 - place.core) * (flat.shape[0] // 2)

    def core_send(self, k):
        size, first = 16 * self.parts[k], 64 * self.units[k]
        own = pick(lax.rem((1 - self.at.core) + k, 3), self.at.xyz)
        for step in (1, 2, 3, 0):
            start = first + lax.rem(own + step, 4) * size
            send(
                self.flat.at[rows16(self.other_base + start, size)],
                self.land_c.at[rows16(start, size)],
                self.gs.at[0, k],
                self.cr.at[k, step],
                self.at.core_mate,
            )

    def core_sum(self):
        for step in (1, 2, 3, 0):
            for k, s in enumerate(self.parts):
                size = 16 * s
                start = 64 * self.units[k] + lax.rem(self.at.own(k, 0) + step, 4) * size
                block = rows16(start, size)
                wait_bytes(self.land_c.at[block], self.cr.at[k, step])
                own = self.flat[rows16(self.base + start, size), :]
                self.half[block, :] = (own.astype(F32) + self.land_c[block, :].astype(F32)).astype(BF16)
                if step:
                    send(
                        self.half.at[block],
                        self.land_a.at[rows16(48 * self.units[k] + (step - 1) * size, size)],
                        self.gs.at[1, k],
                        self.gr.at[1, k],
                        self.at.mate(k, step),
                    )

    def axis_sum(self):
        for k, s in enumerate(self.parts):
            size, first, landed = 16 * s, 16 * self.units[k], 48 * self.units[k]
            wait_bytes(self.land_a.at[rows16(landed, 3 * size)], self.gr.at[1, k])
            own = rows16(64 * self.units[k] + self.at.own(k, 0) * size, size)
            total = self.half[own, :].astype(F32)
            for j in range(3):
                total = total + self.land_a[rows16(landed + j * size, size), :].astype(F32)
            self.mid[rows16(first, size), :] = total.astype(BF16)

            def plane_send(step, carry, k=k, s=s, first=first):
                block, device = self.at.plane_mate(k, step)
                send(
                    self.mid.at[rows16(first + block * s, s)],
                    self.land_p.at[rows16(15 * self.units[k] + (step - 1) * s, s)],
                    self.gs.at[2, k],
                    self.gr.at[2, k],
                    device,
                )
                return carry

            lax.fori_loop(1, 16, plane_send, 0)

    def plane_sum(self):
        for k, s in enumerate(self.parts):
            landed = 15 * self.units[k]
            wait_bytes(self.land_p.at[rows16(landed, 15 * s)], self.gr.at[2, k])
            own = self.at.own(k, 1) * 4 + self.at.own(k, 2)
            total = self.mid[rows16(16 * self.units[k] + own * s, s), :].astype(F32)
            for j in range(15):
                total = total + self.land_p[rows16(landed + j * s, s), :].astype(F32)
            mine = self.final(k, 3)
            self.result[mine, :] = total.astype(BF16)

            def plane_spread(step, carry, k=k, mine=mine):
                _, device = self.at.plane_mate(k, step)
                block = self.result.at[mine]
                send(block, block, self.gs.at[3, k], self.gr.at[3, k], device)
                return carry

            lax.fori_loop(1, 16, plane_spread, 0)

    def final(self, k, depth):
        start, size = self.base + 64 * self.units[k], 64 * self.parts[k]
        for stage in range(depth):
            size //= 4
            start = start + self.at.own(k, stage) * size
        return rows16(start, size)

    def to_core(self, k, block):
        send(block, block, self.gs.at[5, k], self.gr.at[5, k], self.at.core_mate)

    def back_plane(self):
        for k, s in enumerate(self.parts):
            wait_bytes(self.result.at[pl.ds(0, 15 * s)], self.gr.at[3, k])
            block = self.result.at[self.final(k, 1)]
            for step in range(1, 4):
                send(block, block, self.gs.at[4, k], self.ar.at[k, step - 1], self.at.mate(k, step))
            self.to_core(k, block)

    def back_axis(self):
        for step in (1, 3, 2):
            for k, s in enumerate(self.parts):
                size = 16 * s
                wait_bytes(self.result.at[pl.ds(0, size)], self.ar.at[k, step - 1])
                other = lax.rem(self.at.own(k, 0) + (4 - step), 4)
                start = self.base + 64 * self.units[k] + other * size
                self.to_core(k, self.result.at[rows16(start, size)])

    def finish(self):
        for k, s in enumerate(self.parts):
            wait_bytes(self.result.at[pl.ds(0, 64 * s)], self.gr.at[5, k])
            for j, rows in enumerate((64, 48, 15, 15, 48, 64)):
                wait_bytes(self.result.at[pl.ds(0, rows * s)], self.gs.at[j, k])


class SmallSum:
    def __init__(self, place, small, out, sums, land, ss, sr):
        self.at, self.small, self.out, self.sums, self.land = place, small, out, sums, land
        self.ss, self.sr = ss, sr

    def core_send(self):
        send(self.small, self.land.at[0], self.ss.at[0], self.sr.at[0], self.at.core_mate)

    def core_sum(self):
        wait_bytes(self.small, self.ss.at[0])
        wait_bytes(self.land.at[0], self.sr.at[0])
        self.sums[0] = self.small[...] + self.land[0]
        self.axis_send(0)

    def axis_send(self, stage):
        own = self.at.xyz[stage]
        for step in range(1, 4):
            other = lax.rem(own + step, 4)
            ox, oy, oz = (other if a == stage else v for a, v in enumerate(self.at.xyz))
            send(
                self.sums.at[stage],
                self.land.at[1 + 4 * stage + own],
                self.ss.at[1 + stage],
                self.sr.at[1 + stage],
                (ox * 2 + self.at.core, oz * 4 + oy),
            )

    def axis_sum(self, stage):
        first = 1 + 4 * stage
        self.land[first + self.at.xyz[stage]] = self.sums[stage]
        wait_bytes(self.land.at[pl.ds(0, 3)], self.sr.at[1 + stage])
        wait_bytes(self.land.at[pl.ds(0, 3)], self.ss.at[1 + stage])
        total = self.land[first] + self.land[first + 1] + self.land[first + 2] + self.land[first + 3]
        if stage < 2:
            self.sums[stage + 1] = total
            self.axis_send(stage + 1)
        else:
            self.out[...] = total


def step_kernel(
    count, halo_send_h, far_send_h, sidx_h, ridx_h, nodes_h, cot_nodes_h, eb_h, eg_h, nb_h, ng_h,
    edges_h, cot_edges_h, ewi_h, ewo_h, nwi_h, nwo_h,
    node_out, grad_nodes, edge_sum, node_sum, small_out, edge_out_h, grad_edges_h,
    halo_send, far_send, sidx, ridx, nodes, cot_nodes, eb, eg, nb, ng,
    edges, cots, ewi, ewo, nwi, nwo, rhs, rhs_far, ewoT, ewiT,
    first_s, active_s, slope_s, scale_s, ohr_s,
    picks, order, gathered, g_in, g_out, g_slots, g_bias, g_gain, totals, slots, small,
    out_s, table, land_1, far_2, edge_flat, node_flat,
    e_half, e_land_c, e_land_a, e_land_p, e_mid,
    n_half, n_land_c, n_land_a, n_land_p, n_mid,
    far_s, oht_s, node_pre,
    sm, sm_land, halo_back, land_1b, far_2b, land_2b,
    early_sems, in_sems, cot_sems, w_sems, out_sems,
    hs, hr, s1, r1, s2, r2, bhs, bhr, bs1, br1, bs2, br2, ss, sr, egs, egr, ecr, ear, ngs, ngr, ncr, nar,
):
    at = Place()
    b, t = at.b, at.t
    early = [
        pltpu.make_async_copy(source, target, early_sems.at[k])
        for k, (source, target) in enumerate(
            (
                (nodes_h, nodes), (halo_send_h, halo_send), (far_send_h, far_send), (sidx_h, sidx), (ridx_h, ridx),
                (eb_h, eb), (eg_h, eg), (nb_h, nb), (ng_h, ng), (cot_nodes_h, cot_nodes),
            )
        )
    ]
    for copy in early:
        copy.start()
    greet(b, t)

    def block(ref, i):
        return ref.at[pl.ds(pl.multiple_of(i * CHUNK, CHUNK), CHUNK)]

    weights = [(ewi_h, ewi), (ewo_h, ewo), (nwi_h, nwi), (nwo_h, nwo)]

    def weight_copy(k):
        return pltpu.make_async_copy(weights[k][0], weights[k][1], w_sems.at[k])

    weight_copy(0).start()
    for i in range(CHUNKS):
        pltpu.make_async_copy(block(edges_h, i), block(edges, i), in_sems.at[i]).start()
    for k in range(1, 4):
        weight_copy(k).start()
    for i in range(CHUNKS):
        pltpu.make_async_copy(block(cot_edges_h, i), block(cots, i), cot_sems.at[i]).start()

    for copy in early:
        copy.wait()
    x = nodes[...]
    halo_list = jnp.concatenate([halo_send[0, k : k + 1, :] for k in range(4)], axis=1)
    picks[0:HALO, :] = one_hot_rows(index_columns(halo_list), 0, 2)
    for c in range(2):
        wanted = index_columns(far_send[0, c : c + 1, :])
        picks[HALO + 128 * c : HALO + 128 * (c + 1), :] = one_hot_rows(wanted, 0, 2)
    out_s[0:HALO, :] = nn(picks[0:HALO, :], x).astype(BF16)
    far_rows = nn(picks[HALO:TABLE, :], x).astype(BF16)
    row, col = iota((FAR, FAR), 0), iota((FAR, FAR), 1)
    peer = lax.rem(col, 128)
    order[...] = one_hot(
        (lax.rem(row, 2) == col // 128) & (lax.rem(row // 2, 8) == peer // 16) & (row // 16 == lax.rem(peer, 16))
    )
    out_s[HALO:TABLE, :] = nn(order[...], far_rows).astype(BF16)

    @pl.when(b == 0)
    def _():
        table[0:32, :] = jnp.zeros((32, D), BF16)

    @pl.when(b == 7)
    def _():
        table[32:64, :] = jnp.zeros((32, D), BF16)

    pl.semaphore_wait(pltpu.get_barrier_semaphore(), 22)
    for step in range(1, 16):
        peer = lax.rem(t + step, 16)
        send(
            out_s.at[rows16(HALO + peer * 16, 16)], land_1.at[rows16(t * 16, 16)], s1, r1, (b, peer)
        )
    halo_swap(out_s, table, b, t, hs, hr)
    land_1[rows16(t * 16, 16), :] = out_s[rows16(HALO + t * 16, 16), :]

    gathered[...] = jnp.zeros_like(gathered)
    g_in[...] = jnp.zeros_like(g_in)
    g_out[...] = jnp.zeros_like(g_out)
    g_slots[...] = jnp.zeros_like(g_slots)
    g_bias[...] = jnp.zeros_like(g_bias)
    g_gain[...] = jnp.zeros_like(g_gain)

    weight_copy(0).wait()
    rhs[0:D, :] = ewi[0:D, :]
    rhs[D : D + N, :] = nn(x, ewi[D : 2 * D, :]).astype(BF16)
    rhs[D + N :, :] = nn(x, ewi[2 * D :, :]).astype(BF16)
    ewiT[...] = ewi[0:D, :].T
    live = count[0]

    def rows_of(i):
        return pl.ds(pl.multiple_of(i * CHUNK, CHUNK), CHUNK)

    def live_mask(i):
        return jnp.where(iota((CHUNK, 1), 0) + i * CHUNK < live, 1.0, 0.0)

    def local_part(i, carry):
        rows = rows_of(i)
        pltpu.make_async_copy(block(edges_h, i), block(edges, i), in_sems.at[i]).wait()
        sent = index_columns(sidx[:, rows])
        own = one_hot_rows(sent, 0, 2)
        far_s[rows, :] = one_hot_rows(sent, N, 3)
        oht_s[0:SLOTS, rows] = one_hot(iota((SLOTS, CHUNK), 0) == sidx[:, rows])
        oht_s[SLOTS:, rows] = one_hot(iota((N, CHUNK), 0) == ridx[:, rows])
        ohr = one_hot_rows(index_columns(ridx[:, rows]), 0, 2)
        ohr_s[rows, :] = ohr
        first_s[rows, :] = nn(jnp.concatenate([edges[rows, :], own, ohr], axis=1), rhs[...]) + eb[...]
        return carry

    lax.fori_loop(0, CHUNKS // 2, local_part, 0)
    wait_bytes(land_1.at[pl.ds(0, 240)], r1)
    far_2[...] = nn(swap_order(8, 16), land_1[...]).astype(BF16)
    for step in range(1, 8):
        peer = lax.rem(b + step, 8)
        send(
            far_2.at[rows16(peer * 32, 32)],
            table.at[rows16(HALO + b * 32, 32)],
            s2,
            r2,
            (peer, t),
        )
    table[rows16(HALO + b * 32, 32), :] = far_2[rows16(b * 32, 32), :]
    lax.fori_loop(CHUNKS // 2, CHUNKS, local_part, 0)
    weight_copy(1).wait()
    ewoT[...] = ewo[...].T
    weight_copy(2).wait()
    weight_copy(3).wait()
    node_pre[...] = nn(x, nwi[0:D, :]) + nb[...]
    halo_wait(out_s, table, b, hs, hr)
    wait_bytes(out_s.at[pl.ds(0, 240)], s1)
    wait_bytes(table.at[pl.ds(0, 224)], r2)
    wait_bytes(far_2.at[pl.ds(0, 224)], s2)
    rhs_far[...] = nn(table[...], ewi[D : 2 * D, :]).astype(BF16)

    def forward(i, carry):
        rows = rows_of(i)
        active, slope = silu_parts(first_s[rows, :] + nn(far_s[rows, :], rhs_far[...]))
        active = active.astype(BF16)
        active_s[rows, :] = active
        slope_s[rows, :] = slope.astype(BF16)
        hat, scale = norm_parts(nn(active, ewo[...]))
        first_s[rows, :] = hat
        scale_s[rows, :] = scale
        message = hat * eg[...] * live_mask(i)
        gathered[...] += nn(oht_s[SLOTS:, rows], message.astype(BF16))
        return carry

    lax.fori_loop(0, CHUNKS, forward, 0)

    got = gathered[...].astype(BF16)
    first = node_pre[...] + nn(got, nwi[D:, :])
    active, slope = silu_parts(first)
    active = active.astype(BF16)
    hat, scale = norm_parts(nn(active, nwo[...]))
    node_out[...] = (x.astype(F32) + hat * ng[...]).astype(BF16)
    cot = cot_nodes[...].astype(F32)
    put_small(small, 12, jnp.sum(cot * hat, axis=0, keepdims=True))
    d_second = norm_back(cot * ng[...], hat, scale).astype(BF16)
    put_flat(node_flat, 2, tn(active, d_second).astype(BF16))
    d_first = nt(d_second, nwo[...]) * slope
    put_small(small, 8, jnp.sum(d_first, axis=0, keepdims=True))
    d_first = d_first.astype(BF16)
    put_flat(node_flat, 0, tn(x, d_first).astype(BF16))
    put_flat(node_flat, 1, tn(got, d_first).astype(BF16))
    totals[...] = nt(d_first, nwi[0:D, :]) + cot
    from_gathered = nt(d_first, nwi[D:, :]).astype(BF16)

    node_ar = AllReduce(
        at, NODE_PARTS, node_flat, node_sum, n_half, n_land_c, n_land_a, n_land_p, n_mid,
        (ngs, ngr, ncr, nar),
    )
    edge_ar = AllReduce(
        at, EDGE_PARTS, edge_flat, edge_sum, e_half, e_land_c, e_land_a, e_land_p, e_mid,
        (egs, egr, ecr, ear),
    )
    small_ar = SmallSum(at, small, small_out, sm, sm_land, ss, sr)
    for k in range(3):
        node_ar.core_send(k)

    def backward(i, carry):
        rows = rows_of(i)
        pltpu.make_async_copy(block(cot_edges_h, i), block(cots, i), cot_sems.at[i]).wait()
        ce = cots[rows, :].astype(F32)
        hat = first_s[rows, :]
        d_message = (ce + nn(ohr_s[rows, :], from_gathered)) * live_mask(i)
        g_gain[...] += jnp.sum(d_message * hat, axis=0, keepdims=True)
        d_second = norm_back(d_message * eg[...], hat, scale_s[rows, :]).astype(BF16)
        g_out[...] += tn(active_s[rows, :], d_second)
        d_first = nn(d_second, ewoT[...]) * slope_s[rows, :].astype(F32)
        g_bias[...] += jnp.sum(d_first, axis=0, keepdims=True)
        d_first = d_first.astype(BF16)
        slope_s[rows, :] = d_first
        g_in[...] += tn(edges[rows, :], d_first)
        g_slots[...] += nn(oht_s[:, rows], d_first)
        pl.when(i == 0)(node_ar.core_sum)
        pl.when(i == 2)(node_ar.axis_sum)
        return carry

    lax.fori_loop(0, CHUNKS, backward, 0)

    put_flat(edge_flat, 0, g_in[...].astype(BF16))
    put_flat(edge_flat, 1, g_out[...].astype(BF16))
    edge_ar.core_send(0)
    gs = g_slots[...].astype(BF16)
    put_flat(edge_flat, 2, (tn(x, gs[0:N, :]) + tn(table[...], gs[N:SLOTS, :])).astype(BF16))
    edge_ar.core_send(1)
    put_flat(edge_flat, 3, tn(x, gs[SLOTS:, :]).astype(BF16))
    edge_ar.core_send(2)
    put_small(small, 0, g_bias[...])
    put_small(small, 4, g_gain[...])
    small_ar.core_send()

    slots[...] = nt(gs[N:SLOTS, :], ewi[D : 2 * D, :]).astype(BF16)
    for step in range(1, 8):
        peer = lax.rem(b + step, 8)
        send(
            slots.at[rows16(HALO + peer * 32, 32)], land_1b.at[rows16(b * 32, 32)], bs1, br1, (peer, t)
        )
    halo_swap(slots, halo_back, b, t, bhs, bhr)
    land_1b[rows16(b * 32, 32), :] = slots[rows16(HALO + b * 32, 32), :]

    @pl.when(b == 0)
    def _():
        halo_back[0:32, :] = jnp.zeros((32, D), BF16)

    @pl.when(b == 7)
    def _():
        halo_back[32:64, :] = jnp.zeros((32, D), BF16)

    def edge_grad(i):
        rows = slice(i * CHUNK, (i + 1) * CHUNK)
        cots[rows, :] = (nn(slope_s[rows, :], ewiT[...]) + cots[rows, :].astype(F32)).astype(BF16)
        pltpu.make_async_copy(block(cots, i), block(grad_edges_h, i), out_sems.at[1, i]).start()

    def edge_result(i):
        rows = slice(i * CHUNK, (i + 1) * CHUNK)
        message = first_s[rows, :] * (eg[...] * live_mask(i))
        edges[rows, :] = (edges[rows, :].astype(F32) + message).astype(BF16)
        pltpu.make_async_copy(block(edges, i), block(edge_out_h, i), out_sems.at[0, i]).start()

    node_ar.plane_sum()
    edge_ar.core_sum()
    small_ar.core_sum()
    for i in range(CHUNKS):
        edge_grad(i)
    totals[...] += nt(gs[0:N, :], ewi[D : 2 * D, :]) + nt(gs[SLOTS:, :], ewi[2 * D :, :])
    wait_bytes(land_1b.at[pl.ds(0, 224)], br1)
    far_2b[...] = nn(swap_order(16, 8), land_1b[...]).astype(BF16)
    for step in range(1, 16):
        peer = lax.rem(t + step, 16)
        send(
            far_2b.at[rows16(peer * 16, 16)], land_2b.at[rows16(t * 16, 16)], bs2, br2, (b, peer)
        )
    land_2b[rows16(t * 16, 16), :] = far_2b[rows16(t * 16, 16), :]
    node_ar.back_plane()
    edge_ar.axis_sum()
    small_ar.axis_sum(0)
    edge_result(0)
    edge_result(1)
    edge_result(2)
    edge_result(3)
    node_ar.back_axis()
    small_ar.axis_sum(1)
    edge_ar.plane_sum()
    halo_wait(slots, halo_back, b, bhs, bhr)
    wait_bytes(slots.at[pl.ds(0, 224)], bs1)
    wait_bytes(land_2b.at[pl.ds(0, 240)], br2)
    wait_bytes(far_2b.at[pl.ds(0, 240)], bs2)
    far_back = tn(order[...], land_2b[...]).astype(BF16)
    returned = tn(picks[...], jnp.concatenate([halo_back[...], far_back], axis=0))
    grad_nodes[...] = (totals[...] + returned).astype(BF16)
    small_ar.axis_sum(2)
    edge_ar.back_plane()
    for i in range(CHUNKS):
        pltpu.make_async_copy(block(edges, i), block(edge_out_h, i), out_sems.at[0, i]).wait()
        pltpu.make_async_copy(block(cots, i), block(grad_edges_h, i), out_sems.at[1, i]).wait()
    node_ar.finish()
    edge_ar.back_axis()
    edge_ar.finish()


def final_kernel(
    edge_sum, node_sum, small, node_out, edge_out, grad_nodes, grad_edges,
    node_out_h, edge_out_h, grad_nodes_h, grad_edges_h, ewi_h, eb, ewo_h, eg, nwi_h, nb, nwo_h, ng,
    wide, parts, small_s, rows_s, through, in_sems, move_sems, sems,
):
    targets = [(nwi_h, 0, node_sum, 0), (nwi_h, 512, node_sum, 1), (nwo_h, 0, node_sum, 2)]
    targets += [(ewi_h, 0, edge_sum, 0), (ewi_h, 512, edge_sum, 2), (ewi_h, 1024, edge_sum, 3)]
    targets += [(ewo_h, 0, edge_sum, 1)]

    def fetch(j):
        _, _, source, piece = targets[j]
        return pltpu.make_async_copy(source.at[:, piece], parts.at[j], in_sems.at[j])

    small_copy = pltpu.make_async_copy(small, small_s, in_sems.at[7])
    for j in range(len(targets)):
        fetch(j).start()
    small_copy.start()
    copies = []
    moves = [(node_out, node_out_h, 0, N), (grad_nodes, grad_nodes_h, 0, N)]
    for i in range(CHUNKS):
        moves += [(edge_out, edge_out_h, i * CHUNK, CHUNK), (grad_edges, grad_edges_h, i * CHUNK, CHUNK)]
    places = [sum(size for _, _, _, size in moves[:j]) for j in range(len(moves))]

    def move(j, inward):
        source, target, first, size = moves[j]
        near = through.at[pl.ds(places[j], size)]
        if inward:
            return pltpu.make_async_copy(source.at[pl.ds(first, size)], near, move_sems.at[0, j])
        return pltpu.make_async_copy(near, target.at[pl.ds(first, size)], move_sems.at[1, j])

    for j in range(len(moves)):
        move(j, True).start()
    for j in range(len(moves)):
        move(j, True).wait()
        move(j, False).start()
        copies.append(move(j, False))
    for j, (ref, out_first, _, _) in enumerate(targets):
        fetch(j).wait()
        for k in range(4):
            wide[512 * j : 512 * (j + 1), 128 * k : 128 * (k + 1)] = parts[j, k // 2, k % 2].astype(F32)
        copy = pltpu.make_async_copy(
            wide.at[pl.ds(512 * j, 512)], ref.at[pl.ds(out_first, 512)], sems.at[4 + j]
        )
        copy.start()
        copies.append(copy)
    small_copy.wait()
    for j, ref in enumerate((eb, eg, nb, ng)):
        for k in range(4):
            rows_s[j, :, 128 * k : 128 * (k + 1)] = small_s[4 * j + k : 4 * j + k + 1, :]
        copy = pltpu.make_async_copy(rows_s.at[j], ref, sems.at[11 + j])
        copy.start()
        copies.append(copy)
    for copy in copies:
        copy.wait()


def vmem(count):
    return [pl.BlockSpec(memory_space=pltpu.VMEM)] * count


def shape(rows, dtype=BF16, width=D):
    return jax.ShapeDtypeStruct((rows, width), dtype)


def reduce_scratch(total):
    v, half = pltpu.VMEM, total // 2
    return [
        v((half, 128), BF16),
        v((half, 128), BF16),
        v((half // 4 * 3, 128), BF16),
        v((half // 64 * 15, 128), BF16),
        v((half // 4, 128), BF16),
    ]


def step(*operands):
    dma = pltpu.SemaphoreType.DMA
    hbm = pl.BlockSpec(memory_space=pltpu.HBM)
    v = pltpu.VMEM
    wide = v((EDGES, D), BF16)
    square = v((D, D), BF16)
    total = v((D, D), F32)
    return pl.pallas_call(
        step_kernel,
        out_shape=(
            shape(N),
            shape(N),
            shape(4 * EDGE_ROWS, BF16, 128),
            shape(4 * NODE_ROWS, BF16, 128),
            shape(16, F32, 128),
            shape(EDGES),
            shape(EDGES),
        ),
        in_specs=[pl.BlockSpec(memory_space=pltpu.SMEM)] + [hbm] * 16,
        out_specs=tuple(vmem(5) + [hbm] * 2),
        scratch_shapes=[
            v((1, 4, 32), jnp.int32),
            v((1, 2, 128), jnp.int32),
            v((1, EDGES), jnp.int32),
            v((1, EDGES), jnp.int32),
            v((N, D), BF16),
            v((N, D), BF16),
            v((1, D), F32),
            v((1, D), F32),
            v((1, D), F32),
            v((1, D), F32),
            wide,
            wide,
            v((3 * D, D), BF16),
            square,
            v((2 * D, D), BF16),
            square,
            v((D + 2 * N, D), BF16),
            v((TABLE, D), BF16),
            square,
            square,
            v((EDGES, D), F32),
            wide,
            wide,
            v((EDGES, 1), F32),
            v((EDGES, N), BF16),
            v((TABLE, N), BF16),
            v((FAR, FAR), BF16),
            v((N, D), F32),
            total,
            total,
            v((SLOTS + N, D), F32),
            v((1, D), F32),
            v((1, D), F32),
            v((N, D), F32),
            v((TABLE, D), BF16),
            v((16, 128), F32),
            v((TABLE, D), BF16),
            v((TABLE, D), BF16),
            v((FAR, D), BF16),
            v((FAR, D), BF16),
            v((4 * EDGE_ROWS, 128), BF16),
            v((4 * NODE_ROWS, 128), BF16),
        ]
        + reduce_scratch(4 * EDGE_ROWS)
        + reduce_scratch(4 * NODE_ROWS)
        + [
            v((EDGES, TABLE), BF16),
            v((SLOTS + N, EDGES), BF16),
            v((N, D), F32),
            v((3, 16, 128), F32),
            v((13, 16, 128), F32),
            v((HALO, D), BF16),
            v((FAR, D), BF16),
            v((FAR, D), BF16),
            v((FAR, D), BF16),
            dma((10,)),
            dma((CHUNKS,)),
            dma((CHUNKS,)),
            dma((4,)),
            dma((2, CHUNKS)),
        ]
        + [dma((4,)), dma((4,)), dma(()), dma(()), dma(()), dma(())] * 2
        + [dma((4,)), dma((4,))]
        + [dma((6, 3)), dma((6, 3)), dma((3, 4)), dma((3, 3))] * 2,
        compiler_params=pltpu.CompilerParams(
            collective_id=0, has_side_effects=True, vmem_limit_bytes=VMEM_LIMIT
        ),
    )(*operands)


def final(edge_sum, node_sum, small, node_out, edge_out, grad_nodes, grad_edges):
    hbm = pl.BlockSpec(memory_space=pl.ANY)
    v, dma = pltpu.VMEM, pltpu.SemaphoreType.DMA
    return pl.pallas_call(
        final_kernel,
        out_shape=(
            shape(N), shape(EDGES), shape(N), shape(EDGES),
            shape(1536, F32), shape(1, F32), shape(512, F32), shape(1, F32),
            shape(1024, F32), shape(1, F32), shape(512, F32), shape(1, F32),
        ),
        in_specs=[hbm] * 7,
        out_specs=(hbm,) * 12,
        scratch_shapes=[
            v((3584, D), F32),
            v((7, 2, 2, 512, 128), BF16),
            v((16, 128), F32),
            v((4, 1, D), F32),
            v((2 * N + 2 * EDGES, D), BF16),
            dma((8,)),
            dma((2, 2 + 2 * CHUNKS)),
            dma((15,)),
        ],
        compiler_params=pltpu.CompilerParams(vmem_limit_bytes=VMEM_LIMIT),
    )(edge_sum.reshape(2, 4, 2, 512, 128), node_sum.reshape(2, 3, 2, 512, 128), small, node_out, edge_out, grad_nodes, grad_edges)


def shards(
    node_latents, edge_latents, edge_count, receiver, sender, halo_send, far_send,
    edge_weight_in, edge_bias, edge_weight_out, edge_gain,
    node_weight_in, node_bias, node_weight_out, node_gain, cot_nodes, cot_edges,
):
    node_out, grad_nodes, edge_sum, node_sum, small, edge_out, grad_edges = step(
        edge_count, halo_send, far_send.transpose(0, 2, 1), sender.reshape(1, EDGES), receiver.reshape(1, EDGES),
        node_latents, cot_nodes,
        edge_bias.reshape(1, D), edge_gain.reshape(1, D), node_bias.reshape(1, D), node_gain.reshape(1, D),
        edge_latents, cot_edges, edge_weight_in, edge_weight_out, node_weight_in, node_weight_out,
    )
    outs = final(edge_sum, node_sum, small, node_out, edge_out, grad_nodes, grad_edges)
    return tuple(out.reshape(D) if out.shape[0] == 1 else out for out in outs)


def solution(mesh):
    split = ("lat", "lon")
    rows, flat = P(split, None), P(split)
    cube, whole = P(split, None, None), P()
    return jax.shard_map(
        shards,
        mesh=mesh,
        in_specs=(rows, rows, flat, flat, flat, cube, cube) + (whole,) * 8 + (rows, rows),
        out_specs=(rows, rows, rows, rows) + (whole,) * 8,
        check_vma=False,
    )
```

```python
import functools

import jax
import jax.numpy as jnp
from jax import lax
from jax.experimental import pallas as pl
from jax.experimental.pallas import tpu as pltpu
from jax.sharding import PartitionSpec as P

EPS = 1e-05
F32 = jnp.float32
BF16 = jnp.bfloat16
MESH = pl.DeviceIdType.MESH
D = 512
N = 256
EDGES = 2048
HALO = 128
FAR = 256
TABLE = HALO + FAR
SLOTS = N + TABLE
CHUNK = 1024
CHUNKS = EDGES // CHUNK
EDGE_ROWS = 1536
NODE_ROWS = 2048
EDGE_PARTS = (16, 16, 16)
NODE_PARTS = (32, 16, 16)
VMEM_LIMIT = 63 * 1024 * 1024


def nn(a, b):
    return jnp.dot(a, b, preferred_element_type=F32)


def tn(a, b):
    return lax.dot_general(a, b, (((0,), (0,)), ((), ())), preferred_element_type=F32)


def iota(shape, dim):
    return lax.broadcasted_iota(jnp.int32, shape, dim)


def one_hot(mask):
    return jnp.where(mask, 1.0, 0.0).astype(BF16)


def index_columns(row):
    count = row.shape[1] // 128
    parts = [jnp.broadcast_to(row[:, q * 128 : (q + 1) * 128], (128, 128)).T for q in range(count)]
    return parts[0] if count == 1 else jnp.concatenate(parts, axis=0)


def one_hot_rows(columns, first, blocks):
    lane = iota(columns.shape, 1)
    parts = [one_hot(columns == lane + (first + 128 * k)) for k in range(blocks)]
    return jnp.concatenate(parts, axis=1)


def position():
    return lax.axis_index("lat"), lax.axis_index("lon")


def greet(b, t):
    barrier = pltpu.get_barrier_semaphore()
    for step in range(1, 8):
        pl.semaphore_signal(barrier, inc=1, device_id=(lax.rem(b + step, 8), t), device_id_type=MESH)
    for step in range(1, 16):
        pl.semaphore_signal(barrier, inc=1, device_id=(b, lax.rem(t + step, 16)), device_id_type=MESH)


def send(src, dst, send_sem, recv_sem, device):
    pltpu.make_async_remote_copy(
        src_ref=src, dst_ref=dst, send_sem=send_sem, recv_sem=recv_sem, device_id=device, device_id_type=MESH
    ).start()


def wait_bytes(ref, sem):
    pltpu.make_async_copy(ref, ref, sem).wait()


def halo_swap(src, land, b, t, send_sem, recv_sem):
    down, up = (lax.rem(b + 7, 8), t), (lax.rem(b + 1, 8), t)
    left, right = (b, lax.rem(t + 15, 16)), (b, lax.rem(t + 1, 16))

    def part(ref, k):
        return ref.at[pl.ds(32 * k, 32)]

    @pl.when(b > 0)
    def _():
        send(part(src, 0), part(land, 1), send_sem.at[0], recv_sem.at[1], down)

    @pl.when(b < 7)
    def _():
        send(part(src, 1), part(land, 0), send_sem.at[1], recv_sem.at[0], up)

    send(part(src, 2), part(land, 3), send_sem.at[2], recv_sem.at[3], left)
    send(part(src, 3), part(land, 2), send_sem.at[3], recv_sem.at[2], right)


def halo_wait(src, land, b, send_sem, recv_sem):
    def part(ref, k):
        return ref.at[pl.ds(32 * k, 32)]

    @pl.when(b > 0)
    def _():
        wait_bytes(part(src, 0), send_sem.at[0])
        wait_bytes(part(land, 0), recv_sem.at[0])

    @pl.when(b < 7)
    def _():
        wait_bytes(part(src, 1), send_sem.at[1])
        wait_bytes(part(land, 1), recv_sem.at[1])

    for k in (2, 3):
        wait_bytes(part(src, k), send_sem.at[k])
        wait_bytes(part(land, k), recv_sem.at[k])


def swap_order(rows_major, cols_major):
    count = rows_major * cols_major * 2
    row, col = iota((count, count), 0), iota((count, count), 1)
    p, q, c = row // (2 * cols_major), lax.rem(row // 2, cols_major), lax.rem(row, 2)
    return one_hot(col == q * (2 * rows_major) + p * 2 + c)


def norm_parts(values, live=None):
    mean = jnp.mean(values, axis=-1, keepdims=True)
    centered = values - mean
    variance = jnp.mean(centered * centered, axis=-1, keepdims=True)
    scale = lax.rsqrt(variance + EPS)
    if live is not None:
        scale = scale * live
    return centered * scale, scale


def norm_back(grad, hat, scale):
    first = jnp.mean(grad, axis=-1, keepdims=True)
    second = jnp.mean(grad * hat, axis=-1, keepdims=True)
    return scale * (grad - first - hat * second)


def silu_parts(values):
    gate = 0.5 * jnp.tanh(0.5 * values) + 0.5
    active = values * gate
    return active, gate + active * (1.0 - gate)


def put_flat(ref, piece, values):
    half = ref.shape[0] // 2
    for k in range(4):
        first = (k // 2) * half + piece * 1024 + (k % 2) * 512
        ref[first : first + 512, :] = values[:, 128 * k : 128 * (k + 1)]


def put_small(ref, first, values):
    for k in range(4):
        ref[first + k : first + k + 1, :] = values[:, 128 * k : 128 * (k + 1)]


def rows16(start, size):
    return pl.ds(pl.multiple_of(start, 16), size)


def pick(axis, values):
    return jnp.where(axis == 0, values[0], jnp.where(axis == 1, values[1], values[2]))


class Place:
    def __init__(self):
        self.b, self.t = position()
        self.core = lax.rem(self.b, 2)
        self.xyz = (self.b // 2, lax.rem(self.t, 4), self.t // 4)
        self.core_mate = (self.xyz[0] * 2 + (1 - self.core), self.t)

    def axis(self, k, stage):
        return lax.rem(self.core + (k + stage), 3)

    def own(self, k, stage):
        return pick(self.axis(k, stage), self.xyz)

    def mate(self, k, step):
        axis = self.axis(k, 0)
        other = lax.rem(pick(axis, self.xyz) + step, 4)
        ox, oy, oz = (jnp.where(axis == a, other, v) for a, v in enumerate(self.xyz))
        return ox * 2 + self.core, oz * 4 + oy

    def plane_mate(self, k, step):
        second, third = self.axis(k, 1), self.axis(k, 2)
        c2 = lax.rem(pick(second, self.xyz) + step // 4, 4)
        c3 = lax.rem(pick(third, self.xyz) + lax.rem(step, 4), 4)
        ox, oy, oz = (
            jnp.where(second == a, c2, jnp.where(third == a, c3, v)) for a, v in enumerate(self.xyz)
        )
        return c2 * 4 + c3, (ox * 2 + self.core, oz * 4 + oy)


class AllReduce:
    def __init__(self, place, parts, flat, result, half, land_c, land_a, land_p, mid, sems):
        self.at, self.parts, self.flat, self.result = place, parts, flat, result
        self.half, self.land_c, self.land_a, self.land_p, self.mid = half, land_c, land_a, land_p, mid
        self.gs, self.gr, self.cr, self.ar = sems
        self.units = [sum(parts[:k]) for k in range(len(parts))]
        self.base = place.core * (flat.shape[0] // 2)
        self.other_base = (1 - place.core) * (flat.shape[0] // 2)

    def core_send(self, k):
        size, first = 16 * self.parts[k], 64 * self.units[k]
        own = pick(lax.rem((1 - self.at.core) + k, 3), self.at.xyz)
        for step in (1, 2, 3, 0):
            start = first + lax.rem(own + step, 4) * size
            send(
                self.flat.at[rows16(self.other_base + start, size)],
                self.land_c.at[rows16(start, size)],
                self.gs.at[0, k],
                self.cr.at[k, step],
                self.at.core_mate,
            )

    def core_sum(self):
        for step in (1, 2, 3, 0):
            for k, s in enumerate(self.parts):
                size = 16 * s
                start = 64 * self.units[k] + lax.rem(self.at.own(k, 0) + step, 4) * size
                block = rows16(start, size)
                wait_bytes(self.land_c.at[block], self.cr.at[k, step])
                own = self.flat[rows16(self.base + start, size), :]
                self.half[block, :] = (own.astype(F32) + self.land_c[block, :].astype(F32)).astype(BF16)
                if step:
                    send(
                        self.half.at[block],
                        self.land_a.at[rows16(48 * self.units[k] + (step - 1) * size, size)],
                        self.gs.at[1, k],
                        self.gr.at[1, k],
                        self.at.mate(k, step),
                    )

    def axis_sum(self):
        for k, s in enumerate(self.parts):
            size, first, landed = 16 * s, 16 * self.units[k], 48 * self.units[k]
            wait_bytes(self.land_a.at[rows16(landed, 3 * size)], self.gr.at[1, k])
            own = rows16(64 * self.units[k] + self.at.own(k, 0) * size, size)
            total = self.half[own, :].astype(F32)
            for j in range(3):
                total = total + self.land_a[rows16(landed + j * size, size), :].astype(F32)
            self.mid[rows16(first, size), :] = total.astype(BF16)

            def plane_send(step, carry, k=k, s=s, first=first):
                block, device = self.at.plane_mate(k, step)
                send(
                    self.mid.at[rows16(first + block * s, s)],
                    self.land_p.at[rows16(15 * self.units[k] + (step - 1) * s, s)],
                    self.gs.at[2, k],
                    self.gr.at[2, k],
                    device,
                )
                return carry

            lax.fori_loop(1, 16, plane_send, 0)

    def plane_sum(self):
        for k, s in enumerate(self.parts):
            landed = 15 * self.units[k]
            wait_bytes(self.land_p.at[rows16(landed, 15 * s)], self.gr.at[2, k])
            own = self.at.own(k, 1) * 4 + self.at.own(k, 2)
            total = self.mid[rows16(16 * self.units[k] + own * s, s), :].astype(F32)
            for j in range(15):
                total = total + self.land_p[rows16(landed + j * s, s), :].astype(F32)
            mine = self.final(k, 3)
            self.result[mine, :] = total.astype(BF16)

            def plane_spread(step, carry, k=k, mine=mine):
                _, device = self.at.plane_mate(k, step)
                block = self.result.at[mine]
                send(block, block, self.gs.at[3, k], self.gr.at[3, k], device)
                return carry

            lax.fori_loop(1, 16, plane_spread, 0)

    def final(self, k, depth):
        start, size = self.base + 64 * self.units[k], 64 * self.parts[k]
        for stage in range(depth):
            size //= 4
            start = start + self.at.own(k, stage) * size
        return rows16(start, size)

    def to_core(self, k, block):
        send(block, block, self.gs.at[5, k], self.gr.at[5, k], self.at.core_mate)

    def back_plane(self):
        for k, s in enumerate(self.parts):
            wait_bytes(self.result.at[pl.ds(0, 15 * s)], self.gr.at[3, k])
            block = self.result.at[self.final(k, 1)]
            for step in range(1, 4):
                send(block, block, self.gs.at[4, k], self.ar.at[k, step - 1], self.at.mate(k, step))
            self.to_core(k, block)

    def back_axis(self):
        for step in (1, 3, 2):
            for k, s in enumerate(self.parts):
                size = 16 * s
                wait_bytes(self.result.at[pl.ds(0, size)], self.ar.at[k, step - 1])
                other = lax.rem(self.at.own(k, 0) + (4 - step), 4)
                start = self.base + 64 * self.units[k] + other * size
                self.to_core(k, self.result.at[rows16(start, size)])

    def copy_out(self, target, sems, part):
        half = self.flat.shape[0] // 2
        rows = rows16((self.base, self.other_base)[part], half)
        return pltpu.make_async_copy(self.result.at[rows], target.at[rows], sems.at[part])

    def finish(self, target, sems):
        self.copy_out(target, sems, 0).start()
        for k, s in enumerate(self.parts):
            wait_bytes(self.result.at[pl.ds(0, 64 * s)], self.gr.at[5, k])
        self.copy_out(target, sems, 1).start()
        for k, s in enumerate(self.parts):
            for j, rows in enumerate((64, 48, 15, 15, 48, 64)):
                wait_bytes(self.result.at[pl.ds(0, rows * s)], self.gs.at[j, k])


class SmallSum:
    def __init__(self, place, small, out, sums, land, ss, sr):
        self.at, self.small, self.out, self.sums, self.land = place, small, out, sums, land
        self.ss, self.sr = ss, sr

    def core_send(self):
        send(self.small, self.land.at[0], self.ss.at[0], self.sr.at[0], self.at.core_mate)

    def core_sum(self):
        wait_bytes(self.small, self.ss.at[0])
        wait_bytes(self.land.at[0], self.sr.at[0])
        self.sums[0] = self.small[...] + self.land[0]
        self.axis_send(0)

    def axis_send(self, stage):
        own = self.at.xyz[stage]
        for step in range(1, 4):
            other = lax.rem(own + step, 4)
            ox, oy, oz = (other if a == stage else v for a, v in enumerate(self.at.xyz))
            send(
                self.sums.at[stage],
                self.land.at[1 + 4 * stage + own],
                self.ss.at[1 + stage],
                self.sr.at[1 + stage],
                (ox * 2 + self.at.core, oz * 4 + oy),
            )

    def axis_sum(self, stage):
        first = 1 + 4 * stage
        self.land[first + self.at.xyz[stage]] = self.sums[stage]
        wait_bytes(self.land.at[pl.ds(0, 3)], self.sr.at[1 + stage])
        wait_bytes(self.land.at[pl.ds(0, 3)], self.ss.at[1 + stage])
        total = self.land[first] + self.land[first + 1] + self.land[first + 2] + self.land[first + 3]
        if stage < 2:
            self.sums[stage + 1] = total
            self.axis_send(stage + 1)
        else:
            self.out[...] = total


def step_kernel(
    count, halo_send_h, far_send_h, sidx_h, ridx_h, nodes_h, cot_nodes_h, eb_h, eg_h, nb_h, ng_h,
    edges_h, cot_edges_h, ewi_h, ewo_h, nwi_h, nwo_h,
    node_out_h, grad_nodes_h, edge_sum_h, node_sum_h, small_out_h, edge_out_h, grad_edges_h,
    halo_send, far_send, sidx, ridx, nodes, cot_nodes, eb, eg, nb, ng,
    edges, cots, ewi, ewo, nwi, nwo, rhs, rhs_far, ewoT, ewiT, nwoT, nwiT,
    first_s, active_s, slope_s, hat_s, scale_s, ohr_s,
    picks, order, gathered, g_in, g_out, g_slots, g_bias, g_gain, totals, slots, small,
    out_s, table, land_1, far_2, edge_flat, node_flat,
    e_half, e_land_c, e_land_a, e_land_p, e_mid,
    n_half, n_land_c, n_land_a, n_land_p, n_mid,
    far_s, oht_s, node_pre, node_out, grad_nodes, edge_sum, node_sum, small_out,
    sm, sm_land, halo_back, land_1b, far_2b, land_2b,
    late_sems, early_sems, in_sems, cot_sems, w_sems, out_sems,
    hs, hr, s1, r1, s2, r2, bhs, bhr, bs1, br1, bs2, br2, ss, sr, egs, egr, ecr, ear, ngs, ngr, ncr, nar,
):
    at = Place()
    b, t = at.b, at.t
    early = [
        pltpu.make_async_copy(source, target, early_sems.at[k])
        for k, (source, target) in enumerate(
            (
                (nodes_h, nodes), (halo_send_h, halo_send), (far_send_h, far_send), (sidx_h, sidx), (ridx_h, ridx),
                (eb_h, eb), (eg_h, eg), (nb_h, nb), (ng_h, ng), (cot_nodes_h, cot_nodes),
            )
        )
    ]
    for copy in early:
        copy.start()
    greet(b, t)

    def block(ref, i):
        return ref.at[pl.ds(pl.multiple_of(i * CHUNK, CHUNK), CHUNK)]

    weights = [(ewi_h, ewi), (ewo_h, ewo), (nwi_h, nwi), (nwo_h, nwo)]

    def weight_copy(k):
        return pltpu.make_async_copy(weights[k][0], weights[k][1], w_sems.at[k])

    weight_copy(0).start()
    for i in range(CHUNKS):
        pltpu.make_async_copy(block(edges_h, i), block(edges, i), in_sems.at[i]).start()
    for k in range(1, 4):
        weight_copy(k).start()
    for i in range(CHUNKS):
        pltpu.make_async_copy(block(cot_edges_h, i), block(cots, i), cot_sems.at[i]).start()

    for copy in early:
        copy.wait()
    x = nodes[...]
    halo_list = jnp.concatenate([halo_send[0, k : k + 1, :] for k in range(4)], axis=1)
    picks[0:HALO, :] = one_hot_rows(index_columns(halo_list), 0, 2)
    for c in range(2):
        wanted = index_columns(far_send[0, c : c + 1, :])
        picks[HALO + 128 * c : HALO + 128 * (c + 1), :] = one_hot_rows(wanted, 0, 2)
    out_s[0:HALO, :] = nn(picks[0:HALO, :], x).astype(BF16)
    far_rows = nn(picks[HALO:TABLE, :], x).astype(BF16)
    row, col = iota((FAR, FAR), 0), iota((FAR, FAR), 1)
    peer = lax.rem(col, 128)
    order[...] = one_hot(
        (lax.rem(row, 2) == col // 128) & (lax.rem(row // 2, 8) == peer // 16) & (row // 16 == lax.rem(peer, 16))
    )
    out_s[HALO:TABLE, :] = nn(order[...], far_rows).astype(BF16)

    @pl.when(b == 0)
    def _():
        table[0:32, :] = jnp.zeros((32, D), BF16)

    @pl.when(b == 7)
    def _():
        table[32:64, :] = jnp.zeros((32, D), BF16)

    pl.semaphore_wait(pltpu.get_barrier_semaphore(), 22)
    for step in range(1, 16):
        peer = lax.rem(t + step, 16)
        send(
            out_s.at[rows16(HALO + peer * 16, 16)], land_1.at[rows16(t * 16, 16)], s1, r1, (b, peer)
        )
    halo_swap(out_s, table, b, t, hs, hr)
    land_1[rows16(t * 16, 16), :] = out_s[rows16(HALO + t * 16, 16), :]

    gathered[...] = jnp.zeros_like(gathered)
    g_in[...] = jnp.zeros_like(g_in)
    g_out[...] = jnp.zeros_like(g_out)
    g_slots[...] = jnp.zeros_like(g_slots)
    g_bias[...] = jnp.zeros_like(g_bias)
    g_gain[...] = jnp.zeros_like(g_gain)

    weight_copy(0).wait()
    rhs[0:D, :] = ewi[0:D, :]
    rhs[D : D + N, :] = nn(x, ewi[D : 2 * D, :]).astype(BF16)
    rhs[D + N :, :] = nn(x, ewi[2 * D :, :]).astype(BF16)
    live = count[0]

    def rows_of(i):
        return pl.ds(pl.multiple_of(i * CHUNK, CHUNK), CHUNK)

    def live_mask(i):
        return jnp.where(iota((CHUNK, 1), 0) + i * CHUNK < live, 1.0, 0.0)

    def local_part(i, carry):
        rows = rows_of(i)
        pltpu.make_async_copy(block(edges_h, i), block(edges, i), in_sems.at[i]).wait()
        sent = index_columns(sidx[:, rows])
        own = one_hot_rows(sent, 0, 2)
        far_s[rows, :] = one_hot_rows(sent, N, 3)
        oht_s[0:SLOTS, rows] = one_hot(iota((SLOTS, CHUNK), 0) == sidx[:, rows])
        oht_s[SLOTS:, rows] = one_hot(iota((N, CHUNK), 0) == ridx[:, rows])
        ohr = one_hot_rows(index_columns(ridx[:, rows]), 0, 2)
        ohr_s[rows, :] = ohr
        first_s[rows, :] = nn(jnp.concatenate([edges[rows, :], own, ohr], axis=1), rhs[...]) + eb[...]
        return carry

    lax.fori_loop(0, CHUNKS // 2, local_part, 0)
    wait_bytes(land_1.at[pl.ds(0, 240)], r1)
    far_2[...] = nn(swap_order(8, 16), land_1[...]).astype(BF16)
    for step in range(1, 8):
        peer = lax.rem(b + step, 8)
        send(
            far_2.at[rows16(peer * 32, 32)],
            table.at[rows16(HALO + b * 32, 32)],
            s2,
            r2,
            (peer, t),
        )
    table[rows16(HALO + b * 32, 32), :] = far_2[rows16(b * 32, 32), :]
    lax.fori_loop(CHUNKS // 2, CHUNKS, local_part, 0)
    weight_copy(1).wait()
    ewoT[...] = ewo[...].T
    weight_copy(2).wait()
    weight_copy(3).wait()
    for k in range(2):
        nwiT[:, D * k : D * (k + 1)] = nwi[D * k : D * (k + 1), :].T
    nwoT[...] = nwo[...].T
    for k in range(3):
        ewiT[:, D * k : D * (k + 1)] = ewi[D * k : D * (k + 1), :].T
    node_pre[...] = nn(x, nwi[0:D, :]) + nb[...]
    halo_wait(out_s, table, b, hs, hr)
    wait_bytes(out_s.at[pl.ds(0, 240)], s1)
    wait_bytes(table.at[pl.ds(0, 224)], r2)
    wait_bytes(far_2.at[pl.ds(0, 224)], s2)
    rhs_far[...] = nn(table[...], ewi[D : 2 * D, :]).astype(BF16)

    def forward(i, carry):
        rows = rows_of(i)
        active, slope = silu_parts(first_s[rows, :] + nn(far_s[rows, :], rhs_far[...]))
        active = active.astype(BF16)
        active_s[rows, :] = active
        slope_s[rows, :] = slope.astype(BF16)
        hat, scale = norm_parts(nn(active, ewo[...]), live_mask(i))
        hat = hat.astype(BF16)
        hat_s[rows, :] = hat
        scale_s[rows, :] = scale
        gathered[...] += nn(oht_s[SLOTS:, rows], hat)
        return carry

    lax.fori_loop(0, CHUNKS, forward, 0)

    got = (gathered[...] * eg[...]).astype(BF16)
    first = node_pre[...] + nn(got, nwi[D:, :])
    active, slope = silu_parts(first)
    active = active.astype(BF16)
    hat, scale = norm_parts(nn(active, nwo[...]))
    node_out[...] = (x.astype(F32) + hat * ng[...]).astype(BF16)
    node_out_copy = pltpu.make_async_copy(node_out, node_out_h, late_sems.at[4])
    node_out_copy.start()
    cot = cot_nodes[...].astype(F32)
    put_small(small, 12, jnp.sum(cot * hat, axis=0, keepdims=True))
    d_second = norm_back(cot * ng[...], hat, scale).astype(BF16)
    d_first = nn(d_second, nwoT[...]) * slope
    put_small(small, 8, jnp.sum(d_first, axis=0, keepdims=True))
    d_first = d_first.astype(BF16)
    totals[...] = nn(d_first, nwiT[:, 0:D]) + cot
    from_gathered = nn(d_first, nwiT[:, D:]).astype(BF16)

    put_flat(node_flat, 2, tn(active, d_second).astype(BF16))
    put_flat(node_flat, 0, tn(x, d_first).astype(BF16))
    put_flat(node_flat, 1, tn(got, d_first).astype(BF16))
    node_ar = AllReduce(
        at, NODE_PARTS, node_flat, node_sum, n_half, n_land_c, n_land_a, n_land_p, n_mid,
        (ngs, ngr, ncr, nar),
    )
    edge_ar = AllReduce(
        at, EDGE_PARTS, edge_flat, edge_sum, e_half, e_land_c, e_land_a, e_land_p, e_mid,
        (egs, egr, ecr, ear),
    )
    small_ar = SmallSum(at, small, small_out, sm, sm_land, ss, sr)
    node_ar.core_send(0)
    node_ar.core_send(1)

    def backward_out(i, carry):
        rows = rows_of(i)
        pltpu.make_async_copy(block(cot_edges_h, i), block(cots, i), cot_sems.at[i]).wait()
        ce = cots[rows, :].astype(F32)
        hat = hat_s[rows, :].astype(F32)
        d_message = ce + nn(ohr_s[rows, :], from_gathered)
        g_gain[...] += jnp.sum(d_message * hat, axis=0, keepdims=True)
        d_second = norm_back(d_message * eg[...], hat, scale_s[rows, :]).astype(BF16)
        g_out[...] += tn(active_s[rows, :], d_second)
        active_s[rows, :] = d_second
        return carry

    lax.fori_loop(0, CHUNKS, backward_out, 0)
    put_flat(node_flat, 3, g_out[...].astype(BF16))
    node_ar.core_send(2)

    def backward_in(i, carry):
        rows = rows_of(i)
        d_first = nn(active_s[rows, :], ewoT[...]) * slope_s[rows, :].astype(F32)
        g_bias[...] += jnp.sum(d_first, axis=0, keepdims=True)
        d_first = d_first.astype(BF16)
        slope_s[rows, :] = d_first
        g_in[...] += tn(edges[rows, :], d_first)
        g_slots[...] += nn(oht_s[:, rows], d_first)
        pl.when(i == 0)(node_ar.core_sum)
        return carry

    lax.fori_loop(0, CHUNKS, backward_in, 0)

    put_flat(edge_flat, 0, g_in[...].astype(BF16))
    edge_ar.core_send(0)
    gs = g_slots[...].astype(BF16)
    put_flat(edge_flat, 1, (tn(x, gs[0:N, :]) + tn(table[...], gs[N:SLOTS, :])).astype(BF16))
    edge_ar.core_send(1)
    put_flat(edge_flat, 2, tn(x, gs[SLOTS:, :]).astype(BF16))
    edge_ar.core_send(2)
    put_small(small, 0, g_bias[...])
    put_small(small, 4, g_gain[...])
    small_ar.core_send()

    slots[...] = nn(gs[N:SLOTS, :], ewiT[:, D : 2 * D]).astype(BF16)
    for step in range(1, 8):
        peer = lax.rem(b + step, 8)
        send(
            slots.at[rows16(HALO + peer * 32, 32)], land_1b.at[rows16(b * 32, 32)], bs1, br1, (peer, t)
        )
    halo_swap(slots, halo_back, b, t, bhs, bhr)
    land_1b[rows16(b * 32, 32), :] = slots[rows16(HALO + b * 32, 32), :]

    @pl.when(b == 0)
    def _():
        halo_back[0:32, :] = jnp.zeros((32, D), BF16)

    @pl.when(b == 7)
    def _():
        halo_back[32:64, :] = jnp.zeros((32, D), BF16)

    def edge_grad(i):
        rows = slice(i * CHUNK, (i + 1) * CHUNK)
        cots[rows, :] = (nn(slope_s[rows, :], ewiT[:, 0:D]) + cots[rows, :].astype(F32)).astype(BF16)
        pltpu.make_async_copy(block(cots, i), block(grad_edges_h, i), out_sems.at[1, i]).start()

    def edge_result(i):
        rows = slice(i * CHUNK, (i + 1) * CHUNK)
        message = hat_s[rows, :].astype(F32) * eg[...]
        edges[rows, :] = (edges[rows, :].astype(F32) + message).astype(BF16)
        pltpu.make_async_copy(block(edges, i), block(edge_out_h, i), out_sems.at[0, i]).start()

    edge_ar.core_sum()
    small_ar.core_sum()
    node_ar.axis_sum()
    for i in range(CHUNKS):
        edge_grad(i)
    totals[...] += nn(gs[0:N, :], ewiT[:, D : 2 * D]) + nn(gs[SLOTS:, :], ewiT[:, 2 * D :])
    wait_bytes(land_1b.at[pl.ds(0, 224)], br1)
    far_2b[...] = nn(swap_order(16, 8), land_1b[...]).astype(BF16)
    for step in range(1, 16):
        peer = lax.rem(t + step, 16)
        send(
            far_2b.at[rows16(peer * 16, 16)], land_2b.at[rows16(t * 16, 16)], bs2, br2, (b, peer)
        )
    land_2b[rows16(t * 16, 16), :] = far_2b[rows16(t * 16, 16), :]
    edge_ar.axis_sum()
    small_ar.axis_sum(0)
    node_ar.plane_sum()
    for i in range(CHUNKS):
        edge_result(i)
    small_ar.axis_sum(1)
    edge_ar.plane_sum()
    node_ar.back_plane()
    halo_wait(slots, halo_back, b, bhs, bhr)
    wait_bytes(slots.at[pl.ds(0, 224)], bs1)
    wait_bytes(land_2b.at[pl.ds(0, 240)], br2)
    wait_bytes(far_2b.at[pl.ds(0, 240)], bs2)
    far_back = tn(order[...], land_2b[...]).astype(BF16)
    returned = tn(picks[...], jnp.concatenate([halo_back[...], far_back], axis=0))
    grad_nodes[...] = (totals[...] + returned).astype(BF16)
    grad_nodes_copy = pltpu.make_async_copy(grad_nodes, grad_nodes_h, late_sems.at[5])
    grad_nodes_copy.start()
    small_ar.axis_sum(2)
    small_copy = pltpu.make_async_copy(small_out, small_out_h, late_sems.at[6])
    small_copy.start()
    edge_ar.back_plane()
    for i in range(CHUNKS):
        pltpu.make_async_copy(block(edges, i), block(edge_out_h, i), out_sems.at[0, i]).wait()
        pltpu.make_async_copy(block(cots, i), block(grad_edges_h, i), out_sems.at[1, i]).wait()
    node_out_copy.wait()
    node_ar.back_axis()
    node_late, edge_late = late_sems.at[pl.ds(0, 2)], late_sems.at[pl.ds(2, 2)]
    node_ar.finish(node_sum_h, node_late)
    edge_ar.back_axis()
    edge_ar.finish(edge_sum_h, edge_late)
    grad_nodes_copy.wait()
    small_copy.wait()
    for part in range(2):
        node_ar.copy_out(node_sum_h, node_late, part).wait()
        edge_ar.copy_out(edge_sum_h, edge_late, part).wait()


def final_kernel(
    edge_sum, node_sum, small, node_out, edge_out, grad_nodes, grad_edges,
    node_out_h, edge_out_h, grad_nodes_h, grad_edges_h, ewi_h, eb, ewo_h, eg, nwi_h, nb, nwo_h, ng,
    wide, parts, small_s, rows_s, through, in_sems, move_sems, sems,
):
    targets = [(nwi_h, 0, node_sum, 0), (nwi_h, 512, node_sum, 1), (nwo_h, 0, node_sum, 2)]
    targets += [(ewo_h, 0, node_sum, 3)]
    targets += [(ewi_h, 0, edge_sum, 0), (ewi_h, 512, edge_sum, 1), (ewi_h, 1024, edge_sum, 2)]

    def fetch(j):
        _, _, source, piece = targets[j]
        return pltpu.make_async_copy(source.at[:, piece], parts.at[j], in_sems.at[j])

    small_copy = pltpu.make_async_copy(small, small_s, in_sems.at[7])
    for j in range(len(targets)):
        fetch(j).start()
    small_copy.start()
    copies = []
    moves = [(node_out, node_out_h, 0, N), (grad_nodes, grad_nodes_h, 0, N)]
    for i in range(CHUNKS):
        moves += [(edge_out, edge_out_h, i * CHUNK, CHUNK), (grad_edges, grad_edges_h, i * CHUNK, CHUNK)]
    places = [sum(size for _, _, _, size in moves[:j]) for j in range(len(moves))]

    def move(j, inward):
        source, target, first, size = moves[j]
        near = through.at[pl.ds(places[j], size)]
        if inward:
            return pltpu.make_async_copy(source.at[pl.ds(first, size)], near, move_sems.at[0, j])
        return pltpu.make_async_copy(near, target.at[pl.ds(first, size)], move_sems.at[1, j])

    for j in range(len(moves)):
        move(j, True).start()
    for j in range(len(moves)):
        move(j, True).wait()
        move(j, False).start()
        copies.append(move(j, False))
    for j, (ref, out_first, _, _) in enumerate(targets):
        fetch(j).wait()
        for k in range(4):
            wide[512 * j : 512 * (j + 1), 128 * k : 128 * (k + 1)] = parts[j, k // 2, k % 2].astype(F32)
        copy = pltpu.make_async_copy(
            wide.at[pl.ds(512 * j, 512)], ref.at[pl.ds(out_first, 512)], sems.at[4 + j]
        )
        copy.start()
        copies.append(copy)
    small_copy.wait()
    for j, ref in enumerate((eb, eg, nb, ng)):
        for k in range(4):
            rows_s[j, :, 128 * k : 128 * (k + 1)] = small_s[4 * j + k : 4 * j + k + 1, :]
        copy = pltpu.make_async_copy(rows_s.at[j], ref, sems.at[11 + j])
        copy.start()
        copies.append(copy)
    for copy in copies:
        copy.wait()


def vmem(count):
    return [pl.BlockSpec(memory_space=pltpu.VMEM)] * count


def shape(rows, dtype=BF16, width=D):
    return jax.ShapeDtypeStruct((rows, width), dtype)


def reduce_scratch(total):
    v, half = pltpu.VMEM, total // 2
    return [
        v((half, 128), BF16),
        v((half, 128), BF16),
        v((half // 4 * 3, 128), BF16),
        v((half // 64 * 15, 128), BF16),
        v((half // 4, 128), BF16),
    ]


def step(*operands):
    dma = pltpu.SemaphoreType.DMA
    hbm = pl.BlockSpec(memory_space=pltpu.HBM)
    v = pltpu.VMEM
    wide = v((EDGES, D), BF16)
    square = v((D, D), BF16)
    total = v((D, D), F32)
    return pl.pallas_call(
        step_kernel,
        out_shape=(
            shape(N),
            shape(N),
            shape(4 * EDGE_ROWS, BF16, 128),
            shape(4 * NODE_ROWS, BF16, 128),
            shape(16, F32, 128),
            shape(EDGES),
            shape(EDGES),
        ),
        in_specs=[pl.BlockSpec(memory_space=pltpu.SMEM)] + [hbm] * 16,
        out_specs=(hbm,) * 7,
        scratch_shapes=[
            v((1, 4, 32), jnp.int32),
            v((1, 2, 128), jnp.int32),
            v((1, EDGES), jnp.int32),
            v((1, EDGES), jnp.int32),
            v((N, D), BF16),
            v((N, D), BF16),
            v((1, D), F32),
            v((1, D), F32),
            v((1, D), F32),
            v((1, D), F32),
            wide,
            wide,
            v((3 * D, D), BF16),
            square,
            v((2 * D, D), BF16),
            square,
            v((D + 2 * N, D), BF16),
            v((TABLE, D), BF16),
            square,
            v((D, 3 * D), BF16),
            square,
            v((D, 2 * D), BF16),
            v((EDGES, D), F32),
            wide,
            wide,
            wide,
            v((EDGES, 1), F32),
            v((EDGES, N), BF16),
            v((TABLE, N), BF16),
            v((FAR, FAR), BF16),
            v((N, D), F32),
            total,
            total,
            v((SLOTS + N, D), F32),
            v((1, D), F32),
            v((1, D), F32),
            v((N, D), F32),
            v((TABLE, D), BF16),
            v((16, 128), F32),
            v((TABLE, D), BF16),
            v((TABLE, D), BF16),
            v((FAR, D), BF16),
            v((FAR, D), BF16),
            v((4 * EDGE_ROWS, 128), BF16),
            v((4 * NODE_ROWS, 128), BF16),
        ]
        + reduce_scratch(4 * EDGE_ROWS)
        + reduce_scratch(4 * NODE_ROWS)
        + [
            v((EDGES, TABLE), BF16),
            v((SLOTS + N, EDGES), BF16),
            v((N, D), F32),
            v((N, D), BF16),
            v((N, D), BF16),
            v((4 * EDGE_ROWS, 128), BF16),
            v((4 * NODE_ROWS, 128), BF16),
            v((16, 128), F32),
            v((3, 16, 128), F32),
            v((13, 16, 128), F32),
            v((HALO, D), BF16),
            v((FAR, D), BF16),
            v((FAR, D), BF16),
            v((FAR, D), BF16),
            dma((7,)),
            dma((10,)),
            dma((CHUNKS,)),
            dma((CHUNKS,)),
            dma((4,)),
            dma((2, CHUNKS)),
        ]
        + [dma((4,)), dma((4,)), dma(()), dma(()), dma(()), dma(())] * 2
        + [dma((4,)), dma((4,))]
        + [dma((6, 3)), dma((6, 3)), dma((3, 4)), dma((3, 3))] * 2,
        compiler_params=pltpu.CompilerParams(
            collective_id=0, has_side_effects=True, vmem_limit_bytes=VMEM_LIMIT
        ),
    )(*operands)


def final(edge_sum, node_sum, small, node_out, edge_out, grad_nodes, grad_edges):
    hbm = pl.BlockSpec(memory_space=pl.ANY)
    v, dma = pltpu.VMEM, pltpu.SemaphoreType.DMA
    return pl.pallas_call(
        final_kernel,
        out_shape=(
            shape(N), shape(EDGES), shape(N), shape(EDGES),
            shape(1536, F32), shape(1, F32), shape(512, F32), shape(1, F32),
            shape(1024, F32), shape(1, F32), shape(512, F32), shape(1, F32),
        ),
        in_specs=[hbm] * 7,
        out_specs=(hbm,) * 12,
        scratch_shapes=[
            v((3584, D), F32),
            v((7, 2, 2, 512, 128), BF16),
            v((16, 128), F32),
            v((4, 1, D), F32),
            v((2 * N + 2 * EDGES, D), BF16),
            dma((8,)),
            dma((2, 2 + 2 * CHUNKS)),
            dma((15,)),
        ],
        compiler_params=pltpu.CompilerParams(vmem_limit_bytes=VMEM_LIMIT),
    )(edge_sum.reshape(2, 3, 2, 512, 128), node_sum.reshape(2, 4, 2, 512, 128), small, node_out, edge_out, grad_nodes, grad_edges)


def shards(
    node_latents, edge_latents, edge_count, receiver, sender, halo_send, far_send,
    edge_weight_in, edge_bias, edge_weight_out, edge_gain,
    node_weight_in, node_bias, node_weight_out, node_gain, cot_nodes, cot_edges,
):
    node_out, grad_nodes, edge_sum, node_sum, small, edge_out, grad_edges = step(
        edge_count, halo_send, far_send.transpose(0, 2, 1), sender.reshape(1, EDGES), receiver.reshape(1, EDGES),
        node_latents, cot_nodes,
        edge_bias.reshape(1, D), edge_gain.reshape(1, D), node_bias.reshape(1, D), node_gain.reshape(1, D),
        edge_latents, cot_edges, edge_weight_in, edge_weight_out, node_weight_in, node_weight_out,
    )
    outs = final(edge_sum, node_sum, small, node_out, edge_out, grad_nodes, grad_edges)
    return tuple(out.reshape(D) if out.shape[0] == 1 else out for out in outs)


def solution(mesh):
    split = ("lat", "lon")
    rows, flat = P(split, None), P(split)
    cube, whole = P(split, None, None), P()
    return jax.shard_map(
        shards,
        mesh=mesh,
        in_specs=(rows, rows, flat, flat, flat, cube, cube) + (whole,) * 8 + (rows, rows),
        out_specs=(rows, rows, rows, rows) + (whole,) * 8,
        check_vma=False,
    )
```

```python
import functools

import jax
import jax.numpy as jnp
from jax import lax
from jax.experimental import pallas as pl
from jax.experimental.pallas import tpu as pltpu
from jax.sharding import PartitionSpec as P

EPS = 1e-05
F32 = jnp.float32
BF16 = jnp.bfloat16
MESH = pl.DeviceIdType.MESH
D = 512
N = 256
EDGES = 2048
HALO = 128
FAR = 256
TABLE = HALO + FAR
SLOTS = N + TABLE
CHUNK = 1024
CHUNKS = EDGES // CHUNK
EDGE_ROWS = 1536
NODE_ROWS = 2048
EDGE_PARTS = (16, 16, 16)
NODE_PARTS = (32, 16, 16)
VMEM_LIMIT = 63 * 1024 * 1024


def nn(a, b):
    return jnp.dot(a, b, preferred_element_type=F32)


def tn(a, b):
    return lax.dot_general(a, b, (((0,), (0,)), ((), ())), preferred_element_type=F32)


def iota(shape, dim):
    return lax.broadcasted_iota(jnp.int32, shape, dim)


def one_hot(mask):
    return jnp.where(mask, 1.0, 0.0).astype(BF16)


def index_columns(row):
    count = row.shape[1] // 128
    parts = [jnp.broadcast_to(row[:, q * 128 : (q + 1) * 128], (128, 128)).T for q in range(count)]
    return parts[0] if count == 1 else jnp.concatenate(parts, axis=0)


def one_hot_rows(columns, first, blocks):
    lane = iota(columns.shape, 1)
    parts = [one_hot(columns == lane + (first + 128 * k)) for k in range(blocks)]
    return jnp.concatenate(parts, axis=1)


def position():
    return lax.axis_index("lat"), lax.axis_index("lon")


def greet(b, t):
    barrier = pltpu.get_barrier_semaphore()
    for step in range(1, 8):
        pl.semaphore_signal(barrier, inc=1, device_id=(lax.rem(b + step, 8), t), device_id_type=MESH)
    for step in range(1, 16):
        pl.semaphore_signal(barrier, inc=1, device_id=(b, lax.rem(t + step, 16)), device_id_type=MESH)


def send(src, dst, send_sem, recv_sem, device):
    pltpu.make_async_remote_copy(
        src_ref=src, dst_ref=dst, send_sem=send_sem, recv_sem=recv_sem, device_id=device, device_id_type=MESH
    ).start()


def wait_bytes(ref, sem):
    pltpu.make_async_copy(ref, ref, sem).wait()


def halo_swap(src, land, b, t, send_sem, recv_sem):
    down, up = (lax.rem(b + 7, 8), t), (lax.rem(b + 1, 8), t)
    left, right = (b, lax.rem(t + 15, 16)), (b, lax.rem(t + 1, 16))

    def part(ref, k):
        return ref.at[pl.ds(32 * k, 32)]

    @pl.when(b > 0)
    def _():
        send(part(src, 0), part(land, 1), send_sem.at[0], recv_sem.at[1], down)

    @pl.when(b < 7)
    def _():
        send(part(src, 1), part(land, 0), send_sem.at[1], recv_sem.at[0], up)

    send(part(src, 2), part(land, 3), send_sem.at[2], recv_sem.at[3], left)
    send(part(src, 3), part(land, 2), send_sem.at[3], recv_sem.at[2], right)


def halo_wait(src, land, b, send_sem, recv_sem):
    def part(ref, k):
        return ref.at[pl.ds(32 * k, 32)]

    @pl.when(b > 0)
    def _():
        wait_bytes(part(src, 0), send_sem.at[0])
        wait_bytes(part(land, 0), recv_sem.at[0])

    @pl.when(b < 7)
    def _():
        wait_bytes(part(src, 1), send_sem.at[1])
        wait_bytes(part(land, 1), recv_sem.at[1])

    for k in (2, 3):
        wait_bytes(part(src, k), send_sem.at[k])
        wait_bytes(part(land, k), recv_sem.at[k])


def swap_order(rows_major, cols_major):
    count = rows_major * cols_major * 2
    row, col = iota((count, count), 0), iota((count, count), 1)
    p, q, c = row // (2 * cols_major), lax.rem(row // 2, cols_major), lax.rem(row, 2)
    return one_hot(col == q * (2 * rows_major) + p * 2 + c)


def norm_parts(values, live=None):
    mean = jnp.mean(values, axis=-1, keepdims=True)
    centered = values - mean
    variance = jnp.mean(centered * centered, axis=-1, keepdims=True)
    scale = lax.rsqrt(variance + EPS)
    if live is not None:
        scale = scale * live
    return centered * scale, scale


def norm_back(grad, hat, scale):
    first = jnp.mean(grad, axis=-1, keepdims=True)
    second = jnp.mean(grad * hat, axis=-1, keepdims=True)
    return scale * (grad - first - hat * second)


def silu_parts(values):
    gate = 0.5 * jnp.tanh(0.5 * values) + 0.5
    active = values * gate
    return active, gate + active * (1.0 - gate)


def put_flat(ref, piece, values):
    half = ref.shape[0] // 2
    for k in range(4):
        first = (k // 2) * half + piece * 1024 + (k % 2) * 512
        ref[first : first + 512, :] = values[:, 128 * k : 128 * (k + 1)]


def put_small(ref, first, values):
    for k in range(4):
        ref[first + k : first + k + 1, :] = values[:, 128 * k : 128 * (k + 1)]


def rows16(start, size):
    return pl.ds(pl.multiple_of(start, 16), size)


def pick(axis, values):
    return jnp.where(axis == 0, values[0], jnp.where(axis == 1, values[1], values[2]))


class Place:
    def __init__(self):
        self.b, self.t = position()
        self.core = lax.rem(self.b, 2)
        self.xyz = (self.b // 2, lax.rem(self.t, 4), self.t // 4)
        self.core_mate = (self.xyz[0] * 2 + (1 - self.core), self.t)

    def axis(self, k, stage):
        return lax.rem(self.core + (k + stage), 3)

    def own(self, k, stage):
        return pick(self.axis(k, stage), self.xyz)

    def mate(self, k, step):
        axis = self.axis(k, 0)
        other = lax.rem(pick(axis, self.xyz) + step, 4)
        ox, oy, oz = (jnp.where(axis == a, other, v) for a, v in enumerate(self.xyz))
        return ox * 2 + self.core, oz * 4 + oy

    def plane_mate(self, k, step):
        second, third = self.axis(k, 1), self.axis(k, 2)
        c2 = lax.rem(pick(second, self.xyz) + step // 4, 4)
        c3 = lax.rem(pick(third, self.xyz) + lax.rem(step, 4), 4)
        ox, oy, oz = (
            jnp.where(second == a, c2, jnp.where(third == a, c3, v)) for a, v in enumerate(self.xyz)
        )
        return c2 * 4 + c3, (ox * 2 + self.core, oz * 4 + oy)


class AllReduce:
    def __init__(self, place, parts, flat, result, half, land_c, land_a, land_p, mid, sems):
        self.at, self.parts, self.flat, self.result = place, parts, flat, result
        self.half, self.land_c, self.land_a, self.land_p, self.mid = half, land_c, land_a, land_p, mid
        self.gs, self.gr, self.cr, self.ar = sems
        self.units = [sum(parts[:k]) for k in range(len(parts))]
        self.base = place.core * (flat.shape[0] // 2)
        self.other_base = (1 - place.core) * (flat.shape[0] // 2)

    def core_send(self, k):
        size, first = 16 * self.parts[k], 64 * self.units[k]
        own = pick(lax.rem((1 - self.at.core) + k, 3), self.at.xyz)
        for step in (1, 2, 3, 0):
            start = first + lax.rem(own + step, 4) * size
            send(
                self.flat.at[rows16(self.other_base + start, size)],
                self.land_c.at[rows16(start, size)],
                self.gs.at[0, k],
                self.cr.at[k, step],
                self.at.core_mate,
            )

    def core_sum(self):
        for step in (1, 2, 3, 0):
            for k, s in enumerate(self.parts):
                size = 16 * s
                start = 64 * self.units[k] + lax.rem(self.at.own(k, 0) + step, 4) * size
                block = rows16(start, size)
                wait_bytes(self.land_c.at[block], self.cr.at[k, step])
                own = self.flat[rows16(self.base + start, size), :]
                self.half[block, :] = (own.astype(F32) + self.land_c[block, :].astype(F32)).astype(BF16)
                if step:
                    send(
                        self.half.at[block],
                        self.land_a.at[rows16(48 * self.units[k] + (step - 1) * size, size)],
                        self.gs.at[1, k],
                        self.gr.at[1, k],
                        self.at.mate(k, step),
                    )

    def axis_sum(self):
        for k, s in enumerate(self.parts):
            size, first, landed = 16 * s, 16 * self.units[k], 48 * self.units[k]
            wait_bytes(self.land_a.at[rows16(landed, 3 * size)], self.gr.at[1, k])
            own = rows16(64 * self.units[k] + self.at.own(k, 0) * size, size)
            total = self.half[own, :].astype(F32)
            for j in range(3):
                total = total + self.land_a[rows16(landed + j * size, size), :].astype(F32)
            self.mid[rows16(first, size), :] = total.astype(BF16)

            def plane_send(step, carry, k=k, s=s, first=first):
                block, device = self.at.plane_mate(k, step)
                send(
                    self.mid.at[rows16(first + block * s, s)],
                    self.land_p.at[rows16(15 * self.units[k] + (step - 1) * s, s)],
                    self.gs.at[2, k],
                    self.gr.at[2, k],
                    device,
                )
                return carry

            lax.fori_loop(1, 16, plane_send, 0)

    def plane_sum(self):
        for k, s in enumerate(self.parts):
            landed = 15 * self.units[k]
            wait_bytes(self.land_p.at[rows16(landed, 15 * s)], self.gr.at[2, k])
            own = self.at.own(k, 1) * 4 + self.at.own(k, 2)
            total = self.mid[rows16(16 * self.units[k] + own * s, s), :].astype(F32)
            for j in range(15):
                total = total + self.land_p[rows16(landed + j * s, s), :].astype(F32)
            mine = self.final(k, 3)
            self.result[mine, :] = total.astype(BF16)

            def plane_spread(step, carry, k=k, mine=mine):
                _, device = self.at.plane_mate(k, step)
                block = self.result.at[mine]
                send(block, block, self.gs.at[3, k], self.gr.at[3, k], device)
                return carry

            lax.fori_loop(1, 16, plane_spread, 0)

    def final(self, k, depth):
        start, size = self.base + 64 * self.units[k], 64 * self.parts[k]
        for stage in range(depth):
            size //= 4
            start = start + self.at.own(k, stage) * size
        return rows16(start, size)

    def to_core(self, k, block):
        send(block, block, self.gs.at[5, k], self.gr.at[5, k], self.at.core_mate)

    def back_plane(self):
        for k, s in enumerate(self.parts):
            wait_bytes(self.result.at[pl.ds(0, 15 * s)], self.gr.at[3, k])
            block = self.result.at[self.final(k, 1)]
            for step in range(1, 4):
                send(block, block, self.gs.at[4, k], self.ar.at[k, step - 1], self.at.mate(k, step))
            self.to_core(k, block)

    def back_axis(self):
        for step in (1, 3, 2):
            for k, s in enumerate(self.parts):
                size = 16 * s
                wait_bytes(self.result.at[pl.ds(0, size)], self.ar.at[k, step - 1])
                other = lax.rem(self.at.own(k, 0) + (4 - step), 4)
                start = self.base + 64 * self.units[k] + other * size
                self.to_core(k, self.result.at[rows16(start, size)])

    def copy_out(self, target, sems, part):
        half = self.flat.shape[0] // 2
        rows = rows16((self.base, self.other_base)[part], half)
        return pltpu.make_async_copy(self.result.at[rows], target.at[rows], sems.at[part])

    def finish(self, target, sems):
        self.copy_out(target, sems, 0).start()
        for k, s in enumerate(self.parts):
            wait_bytes(self.result.at[pl.ds(0, 64 * s)], self.gr.at[5, k])
        self.copy_out(target, sems, 1).start()
        for k, s in enumerate(self.parts):
            for j, rows in enumerate((64, 48, 15, 15, 48, 64)):
                wait_bytes(self.result.at[pl.ds(0, rows * s)], self.gs.at[j, k])


class SmallSum:
    def __init__(self, place, small, out, sums, land, ss, sr):
        self.at, self.small, self.out, self.sums, self.land = place, small, out, sums, land
        self.ss, self.sr = ss, sr

    def core_send(self):
        send(self.small, self.land.at[0], self.ss.at[0], self.sr.at[0], self.at.core_mate)

    def core_sum(self):
        wait_bytes(self.small, self.ss.at[0])
        wait_bytes(self.land.at[0], self.sr.at[0])
        self.sums[0] = self.small[...] + self.land[0]
        self.axis_send(0)

    def axis_send(self, stage):
        own = self.at.xyz[stage]
        for step in range(1, 4):
            other = lax.rem(own + step, 4)
            ox, oy, oz = (other if a == stage else v for a, v in enumerate(self.at.xyz))
            send(
                self.sums.at[stage],
                self.land.at[1 + 4 * stage + own],
                self.ss.at[1 + stage],
                self.sr.at[1 + stage],
                (ox * 2 + self.at.core, oz * 4 + oy),
            )

    def axis_sum(self, stage):
        first = 1 + 4 * stage
        self.land[first + self.at.xyz[stage]] = self.sums[stage]
        wait_bytes(self.land.at[pl.ds(0, 3)], self.sr.at[1 + stage])
        wait_bytes(self.land.at[pl.ds(0, 3)], self.ss.at[1 + stage])
        total = self.land[first] + self.land[first + 1] + self.land[first + 2] + self.land[first + 3]
        if stage < 2:
            self.sums[stage + 1] = total
            self.axis_send(stage + 1)
        else:
            self.out[...] = total


def step_kernel(
    count, halo_send_h, far_send_h, sidx_h, ridx_h, nodes_h, cot_nodes_h, eb_h, eg_h, nb_h, ng_h,
    edges_h, cot_edges_h, ewi_h, ewo_h, nwi_h, nwo_h,
    node_out_h, grad_nodes_h, edge_sum_h, node_sum_h, small_out_h, edge_out_h, grad_edges_h,
    halo_send, far_send, sidx, ridx, nodes, cot_nodes, eb, eg, nb, ng,
    edges, cots, ewi, ewo, nwi, nwo, rhs, rhs_far, ewoT, ewiT, nwoT, nwiT,
    first_s, active_s, slope_s, hat_s, scale_s, ohr_s,
    picks, order, gathered, g_in, g_out, g_bias, g_gain, totals, slots, small,
    out_s, table, land_1, far_2, edge_flat, node_flat,
    e_half, e_land_c, e_land_a, e_land_p, e_mid,
    n_half, n_land_c, n_land_a, n_land_p, n_mid,
    far_s, oht_s, node_pre, node_out, grad_nodes, edge_sum, node_sum, small_out,
    sm, sm_land, halo_back, land_1b, far_2b, land_2b,
    late_sems, early_sems, in_sems, cot_sems, w_sems, out_sems,
    hs, hr, s1, r1, s2, r2, bhs, bhr, bs1, br1, bs2, br2, ss, sr, egs, egr, ecr, ear, ngs, ngr, ncr, nar,
):
    at = Place()
    b, t = at.b, at.t
    early = [
        pltpu.make_async_copy(source, target, early_sems.at[k])
        for k, (source, target) in enumerate(
            (
                (nodes_h, nodes), (halo_send_h, halo_send), (far_send_h, far_send), (sidx_h, sidx), (ridx_h, ridx),
                (eb_h, eb), (eg_h, eg), (nb_h, nb), (ng_h, ng), (cot_nodes_h, cot_nodes),
            )
        )
    ]
    for copy in early:
        copy.start()
    greet(b, t)

    def block(ref, i):
        return ref.at[pl.ds(pl.multiple_of(i * CHUNK, CHUNK), CHUNK)]

    weights = [(ewi_h, ewi), (ewo_h, ewo), (nwi_h, nwi), (nwo_h, nwo)]

    def weight_copy(k):
        return pltpu.make_async_copy(weights[k][0], weights[k][1], w_sems.at[k])

    weight_copy(0).start()
    for i in range(CHUNKS):
        pltpu.make_async_copy(block(edges_h, i), block(edges, i), in_sems.at[i]).start()
    for k in range(1, 4):
        weight_copy(k).start()
    for i in range(CHUNKS):
        pltpu.make_async_copy(block(cot_edges_h, i), block(cots, i), cot_sems.at[i]).start()

    for copy in early:
        copy.wait()
    x = nodes[...]
    halo_list = jnp.concatenate([halo_send[0, k : k + 1, :] for k in range(4)], axis=1)
    picks[0:HALO, :] = one_hot_rows(index_columns(halo_list), 0, 2)
    for c in range(2):
        wanted = index_columns(far_send[0, c : c + 1, :])
        picks[HALO + 128 * c : HALO + 128 * (c + 1), :] = one_hot_rows(wanted, 0, 2)
    out_s[0:HALO, :] = nn(picks[0:HALO, :], x).astype(BF16)
    far_rows = nn(picks[HALO:TABLE, :], x).astype(BF16)
    row, col = iota((FAR, FAR), 0), iota((FAR, FAR), 1)
    peer = lax.rem(col, 128)
    order[...] = one_hot(
        (lax.rem(row, 2) == col // 128) & (lax.rem(row // 2, 8) == peer // 16) & (row // 16 == lax.rem(peer, 16))
    )
    out_s[HALO:TABLE, :] = nn(order[...], far_rows).astype(BF16)

    @pl.when(b == 0)
    def _():
        table[0:32, :] = jnp.zeros((32, D), BF16)

    @pl.when(b == 7)
    def _():
        table[32:64, :] = jnp.zeros((32, D), BF16)

    pl.semaphore_wait(pltpu.get_barrier_semaphore(), 22)
    for step in range(1, 16):
        peer = lax.rem(t + step, 16)
        send(
            out_s.at[rows16(HALO + peer * 16, 16)], land_1.at[rows16(t * 16, 16)], s1, r1, (b, peer)
        )
    halo_swap(out_s, table, b, t, hs, hr)
    land_1[rows16(t * 16, 16), :] = out_s[rows16(HALO + t * 16, 16), :]

    gathered[...] = jnp.zeros_like(gathered)
    g_in[...] = jnp.zeros_like(g_in)
    g_out[...] = jnp.zeros_like(g_out)
    g_bias[...] = jnp.zeros_like(g_bias)
    g_gain[...] = jnp.zeros_like(g_gain)

    weight_copy(0).wait()
    rhs[0:D, :] = ewi[0:D, :]
    rhs[D : D + N, :] = nn(x, ewi[D : 2 * D, :]).astype(BF16)
    rhs[D + N :, :] = nn(x, ewi[2 * D :, :]).astype(BF16)
    live = count[0]

    def rows_of(i):
        return pl.ds(pl.multiple_of(i * CHUNK, CHUNK), CHUNK)

    def live_mask(i):
        return jnp.where(iota((CHUNK, 1), 0) + i * CHUNK < live, 1.0, 0.0)

    def local_part(i, carry):
        rows = rows_of(i)
        pltpu.make_async_copy(block(edges_h, i), block(edges, i), in_sems.at[i]).wait()
        sent = index_columns(sidx[:, rows])
        own = one_hot_rows(sent, 0, 2)
        far_s[rows, :] = one_hot_rows(sent, N, 3)
        oht_s[0:SLOTS, rows] = one_hot(iota((SLOTS, CHUNK), 0) == sidx[:, rows])
        oht_s[SLOTS:, rows] = one_hot(iota((N, CHUNK), 0) == ridx[:, rows])
        ohr = one_hot_rows(index_columns(ridx[:, rows]), 0, 2)
        ohr_s[rows, :] = ohr
        first_s[rows, :] = nn(jnp.concatenate([edges[rows, :], own, ohr], axis=1), rhs[...]) + eb[...]
        return carry

    lax.fori_loop(0, CHUNKS // 2, local_part, 0)
    wait_bytes(land_1.at[pl.ds(0, 240)], r1)
    far_2[...] = nn(swap_order(8, 16), land_1[...]).astype(BF16)
    for step in range(1, 8):
        peer = lax.rem(b + step, 8)
        send(
            far_2.at[rows16(peer * 32, 32)],
            table.at[rows16(HALO + b * 32, 32)],
            s2,
            r2,
            (peer, t),
        )
    table[rows16(HALO + b * 32, 32), :] = far_2[rows16(b * 32, 32), :]
    lax.fori_loop(CHUNKS // 2, CHUNKS, local_part, 0)
    weight_copy(1).wait()
    ewoT[...] = ewo[...].T
    weight_copy(2).wait()
    weight_copy(3).wait()
    for k in range(2):
        nwiT[:, D * k : D * (k + 1)] = nwi[D * k : D * (k + 1), :].T
    nwoT[...] = nwo[...].T
    for k in range(3):
        ewiT[:, D * k : D * (k + 1)] = ewi[D * k : D * (k + 1), :].T
    node_pre[...] = nn(x, nwi[0:D, :]) + nb[...]
    halo_wait(out_s, table, b, hs, hr)
    wait_bytes(out_s.at[pl.ds(0, 240)], s1)
    wait_bytes(table.at[pl.ds(0, 224)], r2)
    wait_bytes(far_2.at[pl.ds(0, 224)], s2)
    rhs_far[...] = nn(table[...], ewi[D : 2 * D, :]).astype(BF16)

    def forward(i, carry):
        rows = rows_of(i)
        active, slope = silu_parts(first_s[rows, :] + nn(far_s[rows, :], rhs_far[...]))
        active = active.astype(BF16)
        active_s[rows, :] = active
        slope_s[rows, :] = slope.astype(BF16)
        hat, scale = norm_parts(nn(active, ewo[...]), live_mask(i))
        hat = hat.astype(BF16)
        hat_s[rows, :] = hat
        scale_s[rows, :] = scale
        gathered[...] += nn(oht_s[SLOTS:, rows], hat)
        return carry

    lax.fori_loop(0, CHUNKS, forward, 0)

    got = (gathered[...] * eg[...]).astype(BF16)
    first = node_pre[...] + nn(got, nwi[D:, :])
    active, slope = silu_parts(first)
    active = active.astype(BF16)
    hat, scale = norm_parts(nn(active, nwo[...]))
    node_out[...] = (x.astype(F32) + hat * ng[...]).astype(BF16)
    node_out_copy = pltpu.make_async_copy(node_out, node_out_h, late_sems.at[4])
    node_out_copy.start()
    cot = cot_nodes[...].astype(F32)
    put_small(small, 12, jnp.sum(cot * hat, axis=0, keepdims=True))
    d_second = norm_back(cot * ng[...], hat, scale).astype(BF16)
    d_first = nn(d_second, nwoT[...]) * slope
    put_small(small, 8, jnp.sum(d_first, axis=0, keepdims=True))
    d_first = d_first.astype(BF16)
    totals[...] = nn(d_first, nwiT[:, 0:D]) + cot
    from_gathered = nn(d_first, nwiT[:, D:]).astype(BF16)

    put_flat(node_flat, 2, tn(active, d_second).astype(BF16))
    put_flat(node_flat, 0, tn(x, d_first).astype(BF16))
    put_flat(node_flat, 1, tn(got, d_first).astype(BF16))
    node_ar = AllReduce(
        at, NODE_PARTS, node_flat, node_sum, n_half, n_land_c, n_land_a, n_land_p, n_mid,
        (ngs, ngr, ncr, nar),
    )
    edge_ar = AllReduce(
        at, EDGE_PARTS, edge_flat, edge_sum, e_half, e_land_c, e_land_a, e_land_p, e_mid,
        (egs, egr, ecr, ear),
    )
    small_ar = SmallSum(at, small, small_out, sm, sm_land, ss, sr)
    node_ar.core_send(0)
    node_ar.core_send(1)

    def backward_out(i, carry):
        rows = rows_of(i)
        pltpu.make_async_copy(block(cot_edges_h, i), block(cots, i), cot_sems.at[i]).wait()
        ce = cots[rows, :].astype(F32)
        hat = hat_s[rows, :].astype(F32)
        d_message = ce + nn(ohr_s[rows, :], from_gathered)
        g_gain[...] += jnp.sum(d_message * hat, axis=0, keepdims=True)
        d_second = norm_back(d_message * eg[...], hat, scale_s[rows, :]).astype(BF16)
        g_out[...] += tn(active_s[rows, :], d_second)
        active_s[rows, :] = d_second
        return carry

    lax.fori_loop(0, CHUNKS, backward_out, 0)
    put_flat(node_flat, 3, g_out[...].astype(BF16))
    node_ar.core_send(2)

    def backward_in(i, carry):
        rows = rows_of(i)
        d_first = nn(active_s[rows, :], ewoT[...]) * slope_s[rows, :].astype(F32)
        g_bias[...] += jnp.sum(d_first, axis=0, keepdims=True)
        d_first = d_first.astype(BF16)
        slope_s[rows, :] = d_first
        g_in[...] += tn(edges[rows, :], d_first)
        pl.when(i == 0)(node_ar.core_sum)
        return carry

    lax.fori_loop(0, CHUNKS, backward_in, 0)

    put_flat(edge_flat, 0, g_in[...].astype(BF16))
    edge_ar.core_send(0)
    gs = nn(oht_s[...], slope_s[...]).astype(BF16)
    put_flat(edge_flat, 1, (tn(x, gs[0:N, :]) + tn(table[...], gs[N:SLOTS, :])).astype(BF16))
    edge_ar.core_send(1)
    put_flat(edge_flat, 2, tn(x, gs[SLOTS:, :]).astype(BF16))
    edge_ar.core_send(2)
    put_small(small, 0, g_bias[...])
    put_small(small, 4, g_gain[...])
    small_ar.core_send()

    slots[...] = nn(gs[N:SLOTS, :], ewiT[:, D : 2 * D]).astype(BF16)
    for step in range(1, 8):
        peer = lax.rem(b + step, 8)
        send(
            slots.at[rows16(HALO + peer * 32, 32)], land_1b.at[rows16(b * 32, 32)], bs1, br1, (peer, t)
        )
    halo_swap(slots, halo_back, b, t, bhs, bhr)
    land_1b[rows16(b * 32, 32), :] = slots[rows16(HALO + b * 32, 32), :]

    @pl.when(b == 0)
    def _():
        halo_back[0:32, :] = jnp.zeros((32, D), BF16)

    @pl.when(b == 7)
    def _():
        halo_back[32:64, :] = jnp.zeros((32, D), BF16)

    def edge_grad(i):
        rows = slice(i * CHUNK, (i + 1) * CHUNK)
        cots[rows, :] = (nn(slope_s[rows, :], ewiT[:, 0:D]) + cots[rows, :].astype(F32)).astype(BF16)
        pltpu.make_async_copy(block(cots, i), block(grad_edges_h, i), out_sems.at[1, i]).start()

    def edge_result(i):
        rows = slice(i * CHUNK, (i + 1) * CHUNK)
        message = hat_s[rows, :].astype(F32) * eg[...]
        edges[rows, :] = (edges[rows, :].astype(F32) + message).astype(BF16)
        pltpu.make_async_copy(block(edges, i), block(edge_out_h, i), out_sems.at[0, i]).start()

    edge_ar.core_sum()
    small_ar.core_sum()
    node_ar.axis_sum()
    for i in range(CHUNKS):
        edge_grad(i)
    totals[...] += nn(gs[0:N, :], ewiT[:, D : 2 * D]) + nn(gs[SLOTS:, :], ewiT[:, 2 * D :])
    wait_bytes(land_1b.at[pl.ds(0, 224)], br1)
    far_2b[...] = nn(swap_order(16, 8), land_1b[...]).astype(BF16)
    for step in range(1, 16):
        peer = lax.rem(t + step, 16)
        send(
            far_2b.at[rows16(peer * 16, 16)], land_2b.at[rows16(t * 16, 16)], bs2, br2, (b, peer)
        )
    land_2b[rows16(t * 16, 16), :] = far_2b[rows16(t * 16, 16), :]
    edge_ar.axis_sum()
    small_ar.axis_sum(0)
    node_ar.plane_sum()
    for i in range(CHUNKS):
        edge_result(i)
    small_ar.axis_sum(1)
    edge_ar.plane_sum()
    node_ar.back_plane()
    halo_wait(slots, halo_back, b, bhs, bhr)
    wait_bytes(slots.at[pl.ds(0, 224)], bs1)
    wait_bytes(land_2b.at[pl.ds(0, 240)], br2)
    wait_bytes(far_2b.at[pl.ds(0, 240)], bs2)
    far_back = tn(order[...], land_2b[...]).astype(BF16)
    returned = tn(picks[...], jnp.concatenate([halo_back[...], far_back], axis=0))
    grad_nodes[...] = (totals[...] + returned).astype(BF16)
    grad_nodes_copy = pltpu.make_async_copy(grad_nodes, grad_nodes_h, late_sems.at[5])
    grad_nodes_copy.start()
    small_ar.axis_sum(2)
    small_copy = pltpu.make_async_copy(small_out, small_out_h, late_sems.at[6])
    small_copy.start()
    edge_ar.back_plane()
    for i in range(CHUNKS):
        pltpu.make_async_copy(block(edges, i), block(edge_out_h, i), out_sems.at[0, i]).wait()
        pltpu.make_async_copy(block(cots, i), block(grad_edges_h, i), out_sems.at[1, i]).wait()
    node_out_copy.wait()
    node_ar.back_axis()
    node_late, edge_late = late_sems.at[pl.ds(0, 2)], late_sems.at[pl.ds(2, 2)]
    node_ar.finish(node_sum_h, node_late)
    edge_ar.back_axis()
    edge_ar.finish(edge_sum_h, edge_late)
    grad_nodes_copy.wait()
    small_copy.wait()
    for part in range(2):
        node_ar.copy_out(node_sum_h, node_late, part).wait()
        edge_ar.copy_out(edge_sum_h, edge_late, part).wait()


def final_kernel(
    edge_sum, node_sum, small, node_out, edge_out, grad_nodes, grad_edges,
    node_out_h, edge_out_h, grad_nodes_h, grad_edges_h, ewi_h, eb, ewo_h, eg, nwi_h, nb, nwo_h, ng,
    wide, parts, small_s, rows_s, through, in_sems, move_sems, sems,
):
    targets = [(nwi_h, 0, node_sum, 0), (nwi_h, 512, node_sum, 1), (nwo_h, 0, node_sum, 2)]
    targets += [(ewo_h, 0, node_sum, 3)]
    targets += [(ewi_h, 0, edge_sum, 0), (ewi_h, 512, edge_sum, 1), (ewi_h, 1024, edge_sum, 2)]

    def fetch(j):
        _, _, source, piece = targets[j]
        return pltpu.make_async_copy(source.at[:, piece], parts.at[j], in_sems.at[j])

    small_copy = pltpu.make_async_copy(small, small_s, in_sems.at[7])
    for j in range(len(targets)):
        fetch(j).start()
    small_copy.start()
    copies = []
    moves = [(node_out, node_out_h, 0, N), (grad_nodes, grad_nodes_h, 0, N)]
    moves += [(edge_out, edge_out_h, 0, EDGES), (grad_edges, grad_edges_h, 0, EDGES)]
    places = [sum(size for _, _, _, size in moves[:j]) for j in range(len(moves))]

    def move(j, inward):
        source, target, first, size = moves[j]
        near = through.at[pl.ds(places[j], size)]
        if inward:
            return pltpu.make_async_copy(source.at[pl.ds(first, size)], near, move_sems.at[0, j])
        return pltpu.make_async_copy(near, target.at[pl.ds(first, size)], move_sems.at[1, j])

    for j in range(len(moves)):
        move(j, True).start()
    for j in range(len(moves)):
        move(j, True).wait()
        move(j, False).start()
        copies.append(move(j, False))
    for j, (ref, out_first, _, _) in enumerate(targets):
        fetch(j).wait()
        for k in range(4):
            wide[512 * j : 512 * (j + 1), 128 * k : 128 * (k + 1)] = parts[j, k // 2, k % 2].astype(F32)
        copy = pltpu.make_async_copy(
            wide.at[pl.ds(512 * j, 512)], ref.at[pl.ds(out_first, 512)], sems.at[4 + j]
        )
        copy.start()
        copies.append(copy)
    small_copy.wait()
    for j, ref in enumerate((eb, eg, nb, ng)):
        for k in range(4):
            rows_s[j, :, 128 * k : 128 * (k + 1)] = small_s[4 * j + k : 4 * j + k + 1, :]
        copy = pltpu.make_async_copy(rows_s.at[j], ref, sems.at[11 + j])
        copy.start()
        copies.append(copy)
    for copy in copies:
        copy.wait()


def vmem(count):
    return [pl.BlockSpec(memory_space=pltpu.VMEM)] * count


def shape(rows, dtype=BF16, width=D):
    return jax.ShapeDtypeStruct((rows, width), dtype)


def reduce_scratch(total):
    v, half = pltpu.VMEM, total // 2
    return [
        v((half, 128), BF16),
        v((half, 128), BF16),
        v((half // 4 * 3, 128), BF16),
        v((half // 64 * 15, 128), BF16),
        v((half // 4, 128), BF16),
    ]


def step(*operands):
    dma = pltpu.SemaphoreType.DMA
    hbm = pl.BlockSpec(memory_space=pltpu.HBM)
    v = pltpu.VMEM
    wide = v((EDGES, D), BF16)
    square = v((D, D), BF16)
    total = v((D, D), F32)
    return pl.pallas_call(
        step_kernel,
        out_shape=(
            shape(N),
            shape(N),
            shape(4 * EDGE_ROWS, BF16, 128),
            shape(4 * NODE_ROWS, BF16, 128),
            shape(16, F32, 128),
            shape(EDGES),
            shape(EDGES),
        ),
        in_specs=[pl.BlockSpec(memory_space=pltpu.SMEM)] + [hbm] * 16,
        out_specs=(hbm,) * 7,
        scratch_shapes=[
            v((1, 4, 32), jnp.int32),
            v((1, 2, 128), jnp.int32),
            v((1, EDGES), jnp.int32),
            v((1, EDGES), jnp.int32),
            v((N, D), BF16),
            v((N, D), BF16),
            v((1, D), F32),
            v((1, D), F32),
            v((1, D), F32),
            v((1, D), F32),
            wide,
            wide,
            v((3 * D, D), BF16),
            square,
            v((2 * D, D), BF16),
            square,
            v((D + 2 * N, D), BF16),
            v((TABLE, D), BF16),
            square,
            v((D, 3 * D), BF16),
            square,
            v((D, 2 * D), BF16),
            v((EDGES, D), F32),
            wide,
            wide,
            wide,
            v((EDGES, 1), F32),
            v((EDGES, N), BF16),
            v((TABLE, N), BF16),
            v((FAR, FAR), BF16),
            v((N, D), F32),
            total,
            total,
            v((1, D), F32),
            v((1, D), F32),
            v((N, D), F32),
            v((TABLE, D), BF16),
            v((16, 128), F32),
            v((TABLE, D), BF16),
            v((TABLE, D), BF16),
            v((FAR, D), BF16),
            v((FAR, D), BF16),
            v((4 * EDGE_ROWS, 128), BF16),
            v((4 * NODE_ROWS, 128), BF16),
        ]
        + reduce_scratch(4 * EDGE_ROWS)
        + reduce_scratch(4 * NODE_ROWS)
        + [
            v((EDGES, TABLE), BF16),
            v((SLOTS + N, EDGES), BF16),
            v((N, D), F32),
            v((N, D), BF16),
            v((N, D), BF16),
            v((4 * EDGE_ROWS, 128), BF16),
            v((4 * NODE_ROWS, 128), BF16),
            v((16, 128), F32),
            v((3, 16, 128), F32),
            v((13, 16, 128), F32),
            v((HALO, D), BF16),
            v((FAR, D), BF16),
            v((FAR, D), BF16),
            v((FAR, D), BF16),
            dma((7,)),
            dma((10,)),
            dma((CHUNKS,)),
            dma((CHUNKS,)),
            dma((4,)),
            dma((2, CHUNKS)),
        ]
        + [dma((4,)), dma((4,)), dma(()), dma(()), dma(()), dma(())] * 2
        + [dma((4,)), dma((4,))]
        + [dma((6, 3)), dma((6, 3)), dma((3, 4)), dma((3, 3))] * 2,
        compiler_params=pltpu.CompilerParams(
            collective_id=0, has_side_effects=True, vmem_limit_bytes=VMEM_LIMIT
        ),
    )(*operands)


def final(edge_sum, node_sum, small, node_out, edge_out, grad_nodes, grad_edges):
    hbm = pl.BlockSpec(memory_space=pl.ANY)
    v, dma = pltpu.VMEM, pltpu.SemaphoreType.DMA
    return pl.pallas_call(
        final_kernel,
        out_shape=(
            shape(N), shape(EDGES), shape(N), shape(EDGES),
            shape(1536, F32), shape(1, F32), shape(512, F32), shape(1, F32),
            shape(1024, F32), shape(1, F32), shape(512, F32), shape(1, F32),
        ),
        in_specs=[hbm] * 7,
        out_specs=(hbm,) * 12,
        scratch_shapes=[
            v((3584, D), F32),
            v((7, 2, 2, 512, 128), BF16),
            v((16, 128), F32),
            v((4, 1, D), F32),
            v((2 * N + 2 * EDGES, D), BF16),
            dma((8,)),
            dma((2, 4)),
            dma((15,)),
        ],
        compiler_params=pltpu.CompilerParams(vmem_limit_bytes=VMEM_LIMIT),
    )(edge_sum.reshape(2, 3, 2, 512, 128), node_sum.reshape(2, 4, 2, 512, 128), small, node_out, edge_out, grad_nodes, grad_edges)


def shards(
    node_latents, edge_latents, edge_count, receiver, sender, halo_send, far_send,
    edge_weight_in, edge_bias, edge_weight_out, edge_gain,
    node_weight_in, node_bias, node_weight_out, node_gain, cot_nodes, cot_edges,
):
    node_out, grad_nodes, edge_sum, node_sum, small, edge_out, grad_edges = step(
        edge_count, halo_send, far_send.transpose(0, 2, 1), sender.reshape(1, EDGES), receiver.reshape(1, EDGES),
        node_latents, cot_nodes,
        edge_bias.reshape(1, D), edge_gain.reshape(1, D), node_bias.reshape(1, D), node_gain.reshape(1, D),
        edge_latents, cot_edges, edge_weight_in, edge_weight_out, node_weight_in, node_weight_out,
    )
    outs = final(edge_sum, node_sum, small, node_out, edge_out, grad_nodes, grad_edges)
    return tuple(out.reshape(D) if out.shape[0] == 1 else out for out in outs)


def solution(mesh):
    split = ("lat", "lon")
    rows, flat = P(split, None), P(split)
    cube, whole = P(split, None, None), P()
    return jax.shard_map(
        shards,
        mesh=mesh,
        in_specs=(rows, rows, flat, flat, flat, cube, cube) + (whole,) * 8 + (rows, rows),
        out_specs=(rows, rows, rows, rows) + (whole,) * 8,
        check_vma=False,
    )
```

```python
import functools

import jax
import jax.numpy as jnp
from jax import lax
from jax.experimental import pallas as pl
from jax.experimental.pallas import tpu as pltpu
from jax.sharding import PartitionSpec as P

EPS = 1e-05
F32 = jnp.float32
BF16 = jnp.bfloat16
MESH = pl.DeviceIdType.MESH
D = 512
N = 256
EDGES = 2048
HALO = 128
FAR = 256
TABLE = HALO + FAR
SLOTS = N + TABLE
CHUNK = 1024
CHUNKS = EDGES // CHUNK
EDGE_ROWS = 1536
NODE_ROWS = 2048
EDGE_PARTS = (16, 16, 16)
NODE_PARTS = (32, 16, 16)
VMEM_LIMIT = 63 * 1024 * 1024


def nn(a, b):
    return jnp.dot(a, b, preferred_element_type=F32)


def tn(a, b):
    return lax.dot_general(a, b, (((0,), (0,)), ((), ())), preferred_element_type=F32)


def iota(shape, dim):
    return lax.broadcasted_iota(jnp.int32, shape, dim)


def one_hot(mask):
    return jnp.where(mask, 1.0, 0.0).astype(BF16)


def index_columns(row):
    count = row.shape[1] // 128
    parts = [jnp.broadcast_to(row[:, q * 128 : (q + 1) * 128], (128, 128)).T for q in range(count)]
    return parts[0] if count == 1 else jnp.concatenate(parts, axis=0)


def one_hot_rows(columns, first, blocks):
    lane = iota(columns.shape, 1)
    parts = [one_hot(columns == lane + (first + 128 * k)) for k in range(blocks)]
    return jnp.concatenate(parts, axis=1)


def position():
    return lax.axis_index("lat"), lax.axis_index("lon")


def greet(b, t):
    barrier = pltpu.get_barrier_semaphore()
    for step in range(1, 8):
        pl.semaphore_signal(barrier, inc=1, device_id=(lax.rem(b + step, 8), t), device_id_type=MESH)
    for step in range(1, 16):
        pl.semaphore_signal(barrier, inc=1, device_id=(b, lax.rem(t + step, 16)), device_id_type=MESH)


def send(src, dst, send_sem, recv_sem, device):
    pltpu.make_async_remote_copy(
        src_ref=src, dst_ref=dst, send_sem=send_sem, recv_sem=recv_sem, device_id=device, device_id_type=MESH
    ).start()


def wait_bytes(ref, sem):
    pltpu.make_async_copy(ref, ref, sem).wait()


def halo_swap(src, land, b, t, send_sem, recv_sem):
    down, up = (lax.rem(b + 7, 8), t), (lax.rem(b + 1, 8), t)
    left, right = (b, lax.rem(t + 15, 16)), (b, lax.rem(t + 1, 16))

    def part(ref, k):
        return ref.at[pl.ds(32 * k, 32)]

    @pl.when(b > 0)
    def _():
        send(part(src, 0), part(land, 1), send_sem.at[0], recv_sem.at[1], down)

    @pl.when(b < 7)
    def _():
        send(part(src, 1), part(land, 0), send_sem.at[1], recv_sem.at[0], up)

    send(part(src, 2), part(land, 3), send_sem.at[2], recv_sem.at[3], left)
    send(part(src, 3), part(land, 2), send_sem.at[3], recv_sem.at[2], right)


def halo_wait(src, land, b, send_sem, recv_sem):
    def part(ref, k):
        return ref.at[pl.ds(32 * k, 32)]

    @pl.when(b > 0)
    def _():
        wait_bytes(part(src, 0), send_sem.at[0])
        wait_bytes(part(land, 0), recv_sem.at[0])

    @pl.when(b < 7)
    def _():
        wait_bytes(part(src, 1), send_sem.at[1])
        wait_bytes(part(land, 1), recv_sem.at[1])

    for k in (2, 3):
        wait_bytes(part(src, k), send_sem.at[k])
        wait_bytes(part(land, k), recv_sem.at[k])


def swap_order(rows_major, cols_major):
    count = rows_major * cols_major * 2
    row, col = iota((count, count), 0), iota((count, count), 1)
    p, q, c = row // (2 * cols_major), lax.rem(row // 2, cols_major), lax.rem(row, 2)
    return one_hot(col == q * (2 * rows_major) + p * 2 + c)


def norm_parts(values, live=None):
    mean = jnp.mean(values, axis=-1, keepdims=True)
    centered = values - mean
    variance = jnp.mean(centered * centered, axis=-1, keepdims=True)
    scale = lax.rsqrt(variance + EPS)
    if live is not None:
        scale = scale * live
    return centered * scale, scale


def norm_back(grad, hat, scale):
    first = jnp.mean(grad, axis=-1, keepdims=True)
    second = jnp.mean(grad * hat, axis=-1, keepdims=True)
    return scale * (grad - first - hat * second)


def silu_parts(values):
    gate = 0.5 * jnp.tanh(0.5 * values) + 0.5
    active = values * gate
    return active, gate + active * (1.0 - gate)


def put_flat(ref, piece, values):
    half = ref.shape[0] // 2
    for k in range(4):
        first = (k // 2) * half + piece * 1024 + (k % 2) * 512
        ref[first : first + 512, :] = values[:, 128 * k : 128 * (k + 1)]


def put_small(ref, first, values):
    for k in range(4):
        ref[first + k : first + k + 1, :] = values[:, 128 * k : 128 * (k + 1)]


def rows16(start, size):
    return pl.ds(pl.multiple_of(start, 16), size)


def pick(axis, values):
    return jnp.where(axis == 0, values[0], jnp.where(axis == 1, values[1], values[2]))


class Place:
    def __init__(self):
        self.b, self.t = position()
        self.core = lax.rem(self.b, 2)
        self.xyz = (self.b // 2, lax.rem(self.t, 4), self.t // 4)
        self.core_mate = (self.xyz[0] * 2 + (1 - self.core), self.t)

    def axis(self, k, stage):
        return lax.rem(self.core + (k + stage), 3)

    def own(self, k, stage):
        return pick(self.axis(k, stage), self.xyz)

    def mate(self, k, step):
        axis = self.axis(k, 0)
        other = lax.rem(pick(axis, self.xyz) + step, 4)
        ox, oy, oz = (jnp.where(axis == a, other, v) for a, v in enumerate(self.xyz))
        return ox * 2 + self.core, oz * 4 + oy

    def plane_mate(self, k, step):
        second, third = self.axis(k, 1), self.axis(k, 2)
        c2 = lax.rem(pick(second, self.xyz) + step // 4, 4)
        c3 = lax.rem(pick(third, self.xyz) + lax.rem(step, 4), 4)
        ox, oy, oz = (
            jnp.where(second == a, c2, jnp.where(third == a, c3, v)) for a, v in enumerate(self.xyz)
        )
        return c2 * 4 + c3, (ox * 2 + self.core, oz * 4 + oy)


class AllReduce:
    def __init__(self, place, parts, flat, result, half, land_c, land_a, land_p, mid, sems):
        self.at, self.parts, self.flat, self.result = place, parts, flat, result
        self.half, self.land_c, self.land_a, self.land_p, self.mid = half, land_c, land_a, land_p, mid
        self.gs, self.gr, self.cr, self.ar = sems
        self.units = [sum(parts[:k]) for k in range(len(parts))]
        self.base = place.core * (flat.shape[0] // 2)
        self.other_base = (1 - place.core) * (flat.shape[0] // 2)

    def core_send(self, k):
        size, first = 16 * self.parts[k], 64 * self.units[k]
        own = pick(lax.rem((1 - self.at.core) + k, 3), self.at.xyz)
        for step in (1, 2, 3, 0):
            start = first + lax.rem(own + step, 4) * size
            send(
                self.flat.at[rows16(self.other_base + start, size)],
                self.land_c.at[rows16(start, size)],
                self.gs.at[0, k],
                self.cr.at[k, step],
                self.at.core_mate,
            )

    def core_sum(self):
        for step in (1, 2, 3, 0):
            for k, s in enumerate(self.parts):
                size = 16 * s
                start = 64 * self.units[k] + lax.rem(self.at.own(k, 0) + step, 4) * size
                block = rows16(start, size)
                wait_bytes(self.land_c.at[block], self.cr.at[k, step])
                own = self.flat[rows16(self.base + start, size), :]
                self.half[block, :] = (own.astype(F32) + self.land_c[block, :].astype(F32)).astype(BF16)
                if step:
                    send(
                        self.half.at[block],
                        self.land_a.at[rows16(48 * self.units[k] + (step - 1) * size, size)],
                        self.gs.at[1, k],
                        self.gr.at[1, k],
                        self.at.mate(k, step),
                    )

    def axis_sum(self):
        for k, s in enumerate(self.parts):
            size, first, landed = 16 * s, 16 * self.units[k], 48 * self.units[k]
            wait_bytes(self.land_a.at[rows16(landed, 3 * size)], self.gr.at[1, k])
            own = rows16(64 * self.units[k] + self.at.own(k, 0) * size, size)
            total = self.half[own, :].astype(F32)
            for j in range(3):
                total = total + self.land_a[rows16(landed + j * size, size), :].astype(F32)
            self.mid[rows16(first, size), :] = total.astype(BF16)

            def plane_send(step, carry, k=k, s=s, first=first):
                block, device = self.at.plane_mate(k, step)
                send(
                    self.mid.at[rows16(first + block * s, s)],
                    self.land_p.at[rows16(15 * self.units[k] + (step - 1) * s, s)],
                    self.gs.at[2, k],
                    self.gr.at[2, k],
                    device,
                )
                return carry

            lax.fori_loop(1, 16, plane_send, 0)

    def plane_sum(self):
        for k, s in enumerate(self.parts):
            landed = 15 * self.units[k]
            wait_bytes(self.land_p.at[rows16(landed, 15 * s)], self.gr.at[2, k])
            own = self.at.own(k, 1) * 4 + self.at.own(k, 2)
            total = self.mid[rows16(16 * self.units[k] + own * s, s), :].astype(F32)
            for j in range(15):
                total = total + self.land_p[rows16(landed + j * s, s), :].astype(F32)
            mine = self.final(k, 3)
            self.result[mine, :] = total.astype(BF16)

            def plane_spread(step, carry, k=k, mine=mine):
                _, device = self.at.plane_mate(k, step)
                block = self.result.at[mine]
                send(block, block, self.gs.at[3, k], self.gr.at[3, k], device)
                return carry

            lax.fori_loop(1, 16, plane_spread, 0)

    def final(self, k, depth):
        start, size = self.base + 64 * self.units[k], 64 * self.parts[k]
        for stage in range(depth):
            size //= 4
            start = start + self.at.own(k, stage) * size
        return rows16(start, size)

    def to_core(self, k, block):
        send(block, block, self.gs.at[5, k], self.gr.at[5, k], self.at.core_mate)

    def back_plane(self):
        for k, s in enumerate(self.parts):
            wait_bytes(self.result.at[pl.ds(0, 15 * s)], self.gr.at[3, k])
            block = self.result.at[self.final(k, 1)]
            for step in range(1, 4):
                send(block, block, self.gs.at[4, k], self.ar.at[k, step - 1], self.at.mate(k, step))
            self.to_core(k, block)

    def back_axis(self):
        for step in (1, 3, 2):
            for k, s in enumerate(self.parts):
                size = 16 * s
                wait_bytes(self.result.at[pl.ds(0, size)], self.ar.at[k, step - 1])
                other = lax.rem(self.at.own(k, 0) + (4 - step), 4)
                start = self.base + 64 * self.units[k] + other * size
                self.to_core(k, self.result.at[rows16(start, size)])

    def copy_out(self, target, sems, part):
        half = self.flat.shape[0] // 2
        rows = rows16((self.base, self.other_base)[part], half)
        return pltpu.make_async_copy(self.result.at[rows], target.at[rows], sems.at[part])

    def finish(self, target, sems):
        self.copy_out(target, sems, 0).start()
        for k, s in enumerate(self.parts):
            wait_bytes(self.result.at[pl.ds(0, 64 * s)], self.gr.at[5, k])
        self.copy_out(target, sems, 1).start()
        for k, s in enumerate(self.parts):
            for j, rows in enumerate((64, 48, 15, 15, 48, 64)):
                wait_bytes(self.result.at[pl.ds(0, rows * s)], self.gs.at[j, k])


class SmallSum:
    def __init__(self, place, small, out, sums, land, ss, sr):
        self.at, self.small, self.out, self.sums, self.land = place, small, out, sums, land
        self.ss, self.sr = ss, sr

    def core_send(self):
        send(self.small, self.land.at[0], self.ss.at[0], self.sr.at[0], self.at.core_mate)

    def core_sum(self):
        wait_bytes(self.small, self.ss.at[0])
        wait_bytes(self.land.at[0], self.sr.at[0])
        self.sums[0] = self.small[...] + self.land[0]
        self.axis_send(0)

    def axis_send(self, stage):
        own = self.at.xyz[stage]
        for step in range(1, 4):
            other = lax.rem(own + step, 4)
            ox, oy, oz = (other if a == stage else v for a, v in enumerate(self.at.xyz))
            send(
                self.sums.at[stage],
                self.land.at[1 + 4 * stage + own],
                self.ss.at[1 + stage],
                self.sr.at[1 + stage],
                (ox * 2 + self.at.core, oz * 4 + oy),
            )

    def axis_sum(self, stage):
        first = 1 + 4 * stage
        self.land[first + self.at.xyz[stage]] = self.sums[stage]
        wait_bytes(self.land.at[pl.ds(0, 3)], self.sr.at[1 + stage])
        wait_bytes(self.land.at[pl.ds(0, 3)], self.ss.at[1 + stage])
        total = self.land[first] + self.land[first + 1] + self.land[first + 2] + self.land[first + 3]
        if stage < 2:
            self.sums[stage + 1] = total
            self.axis_send(stage + 1)
        else:
            self.out[...] = total


def step_kernel(
    count, halo_send_h, far_send_h, sidx_h, ridx_h, nodes_h, cot_nodes_h, eb_h, eg_h, nb_h, ng_h,
    edges_h, cot_edges_h, ewi_h, ewo_h, nwi_h, nwo_h,
    node_out_h, grad_nodes_h, edge_sum_h, node_sum_h, small_out_h, edge_out_h, grad_edges_h,
    halo_send, far_send, sidx, ridx, nodes, cot_nodes, eb, eg, nb, ng,
    edges, cots, ewi, ewo, nwi, nwo, rhs, rhs_far, ewoT, ewiT, nwoT, nwiT,
    first_s, active_s, slope_s, hat_s, scale_s, ohr_s,
    picks, order, gathered, g_in, g_out, g_bias, g_gain, totals, slots, small,
    out_s, table, land_1, far_2, edge_flat, node_flat,
    e_half, e_land_c, e_land_a, e_land_p, e_mid,
    n_half, n_land_c, n_land_a, n_land_p, n_mid,
    far_s, oht_s, node_pre, node_out, grad_nodes, edge_sum, node_sum, small_out,
    sm, sm_land, halo_back, land_1b, far_2b, land_2b,
    late_sems, early_sems, in_sems, cot_sems, w_sems, out_sems,
    hs, hr, s1, r1, s2, r2, bhs, bhr, bs1, br1, bs2, br2, ss, sr, egs, egr, ecr, ear, ngs, ngr, ncr, nar,
):
    at = Place()
    b, t = at.b, at.t
    early = [
        pltpu.make_async_copy(source, target, early_sems.at[k])
        for k, (source, target) in enumerate(
            (
                (nodes_h, nodes), (halo_send_h, halo_send), (far_send_h, far_send), (sidx_h, sidx), (ridx_h, ridx),
                (eb_h, eb), (eg_h, eg), (nb_h, nb), (ng_h, ng), (cot_nodes_h, cot_nodes),
            )
        )
    ]
    for copy in early:
        copy.start()
    greet(b, t)

    def block(ref, i):
        return ref.at[pl.ds(pl.multiple_of(i * CHUNK, CHUNK), CHUNK)]

    weights = [(ewi_h, ewi), (ewo_h, ewo), (nwi_h, nwi), (nwo_h, nwo)]

    def weight_copy(k):
        return pltpu.make_async_copy(weights[k][0], weights[k][1], w_sems.at[k])

    weight_copy(0).start()
    for i in range(CHUNKS):
        pltpu.make_async_copy(block(edges_h, i), block(edges, i), in_sems.at[i]).start()
    for k in range(1, 4):
        weight_copy(k).start()
    for i in range(CHUNKS):
        pltpu.make_async_copy(block(cot_edges_h, i), block(cots, i), cot_sems.at[i]).start()

    for copy in early:
        copy.wait()
    x = nodes[...]
    halo_list = jnp.concatenate([halo_send[0, k : k + 1, :] for k in range(4)], axis=1)
    picks[0:HALO, :] = one_hot_rows(index_columns(halo_list), 0, 2)
    for c in range(2):
        wanted = index_columns(far_send[0, c : c + 1, :])
        picks[HALO + 128 * c : HALO + 128 * (c + 1), :] = one_hot_rows(wanted, 0, 2)
    out_s[0:HALO, :] = nn(picks[0:HALO, :], x).astype(BF16)
    far_rows = nn(picks[HALO:TABLE, :], x).astype(BF16)
    row, col = iota((FAR, FAR), 0), iota((FAR, FAR), 1)
    peer = lax.rem(col, 128)
    order[...] = one_hot(
        (lax.rem(row, 2) == col // 128) & (lax.rem(row // 2, 8) == peer // 16) & (row // 16 == lax.rem(peer, 16))
    )
    out_s[HALO:TABLE, :] = nn(order[...], far_rows).astype(BF16)

    @pl.when(b == 0)
    def _():
        table[0:32, :] = jnp.zeros((32, D), BF16)

    @pl.when(b == 7)
    def _():
        table[32:64, :] = jnp.zeros((32, D), BF16)

    pl.semaphore_wait(pltpu.get_barrier_semaphore(), 22)
    for step in range(1, 16):
        peer = lax.rem(t + step, 16)
        send(
            out_s.at[rows16(HALO + peer * 16, 16)], land_1.at[rows16(t * 16, 16)], s1, r1, (b, peer)
        )
    halo_swap(out_s, table, b, t, hs, hr)
    land_1[rows16(t * 16, 16), :] = out_s[rows16(HALO + t * 16, 16), :]

    gathered[...] = jnp.zeros_like(gathered)
    g_in[...] = jnp.zeros_like(g_in)
    g_out[...] = jnp.zeros_like(g_out)
    g_bias[...] = jnp.zeros_like(g_bias)
    g_gain[...] = jnp.zeros_like(g_gain)

    weight_copy(0).wait()
    rhs[0:D, :] = ewi[0:D, :]
    rhs[D : D + N, :] = nn(x, ewi[D : 2 * D, :]).astype(BF16)
    rhs[D + N :, :] = nn(x, ewi[2 * D :, :]).astype(BF16)
    live = count[0]

    def rows_of(i):
        return pl.ds(pl.multiple_of(i * CHUNK, CHUNK), CHUNK)

    def live_mask(i):
        return jnp.where(iota((CHUNK, 1), 0) + i * CHUNK < live, 1.0, 0.0)

    def local_part(i, carry):
        rows = rows_of(i)
        pltpu.make_async_copy(block(edges_h, i), block(edges, i), in_sems.at[i]).wait()
        sent = index_columns(sidx[:, rows])
        own = one_hot_rows(sent, 0, 2)
        far_s[rows, :] = one_hot_rows(sent, N, 3)
        oht_s[0:SLOTS, rows] = one_hot(iota((SLOTS, CHUNK), 0) == sidx[:, rows])
        oht_s[SLOTS:, rows] = one_hot(iota((N, CHUNK), 0) == ridx[:, rows])
        ohr = one_hot_rows(index_columns(ridx[:, rows]), 0, 2)
        ohr_s[rows, :] = ohr
        first_s[rows, :] = nn(jnp.concatenate([edges[rows, :], own, ohr], axis=1), rhs[...]) + eb[...]
        return carry

    lax.fori_loop(0, CHUNKS // 2, local_part, 0)
    wait_bytes(land_1.at[pl.ds(0, 240)], r1)
    far_2[...] = nn(swap_order(8, 16), land_1[...]).astype(BF16)
    for step in range(1, 8):
        peer = lax.rem(b + step, 8)
        send(
            far_2.at[rows16(peer * 32, 32)],
            table.at[rows16(HALO + b * 32, 32)],
            s2,
            r2,
            (peer, t),
        )
    table[rows16(HALO + b * 32, 32), :] = far_2[rows16(b * 32, 32), :]
    lax.fori_loop(CHUNKS // 2, CHUNKS, local_part, 0)
    weight_copy(1).wait()
    ewoT[...] = ewo[...].T
    weight_copy(2).wait()
    weight_copy(3).wait()
    for k in range(2):
        nwiT[:, D * k : D * (k + 1)] = nwi[D * k : D * (k + 1), :].T
    nwoT[...] = nwo[...].T
    for k in range(3):
        ewiT[:, D * k : D * (k + 1)] = ewi[D * k : D * (k + 1), :].T
    node_pre[...] = nn(x, nwi[0:D, :]) + nb[...]
    halo_wait(out_s, table, b, hs, hr)
    wait_bytes(out_s.at[pl.ds(0, 240)], s1)
    wait_bytes(table.at[pl.ds(0, 224)], r2)
    wait_bytes(far_2.at[pl.ds(0, 224)], s2)
    rhs_far[...] = nn(table[...], ewi[D : 2 * D, :]).astype(BF16)

    def forward(i, carry):
        rows = rows_of(i)
        active, slope = silu_parts(first_s[rows, :] + nn(far_s[rows, :], rhs_far[...]))
        active = active.astype(BF16)
        active_s[rows, :] = active
        slope_s[rows, :] = slope.astype(BF16)
        hat, scale = norm_parts(nn(active, ewo[...]), live_mask(i))
        hat = hat.astype(BF16)
        hat_s[rows, :] = hat
        scale_s[rows, :] = scale
        gathered[...] += nn(oht_s[SLOTS:, rows], hat)
        return carry

    lax.fori_loop(0, CHUNKS, forward, 0)

    got = (gathered[...] * eg[...]).astype(BF16)
    first = node_pre[...] + nn(got, nwi[D:, :])
    active, slope = silu_parts(first)
    active = active.astype(BF16)
    hat, scale = norm_parts(nn(active, nwo[...]))
    node_out[...] = (x.astype(F32) + hat * ng[...]).astype(BF16)
    node_out_copy = pltpu.make_async_copy(node_out, node_out_h, late_sems.at[4])
    node_out_copy.start()
    cot = cot_nodes[...].astype(F32)
    put_small(small, 12, jnp.sum(cot * hat, axis=0, keepdims=True))
    d_second = norm_back(cot * ng[...], hat, scale).astype(BF16)
    d_first = nn(d_second, nwoT[...]) * slope
    put_small(small, 8, jnp.sum(d_first, axis=0, keepdims=True))
    d_first = d_first.astype(BF16)
    totals[...] = nn(d_first, nwiT[:, 0:D]) + cot
    from_gathered = nn(d_first, nwiT[:, D:]).astype(BF16)

    put_flat(node_flat, 2, tn(active, d_second).astype(BF16))
    put_flat(node_flat, 0, tn(x, d_first).astype(BF16))
    put_flat(node_flat, 1, tn(got, d_first).astype(BF16))
    node_ar = AllReduce(
        at, NODE_PARTS, node_flat, node_sum, n_half, n_land_c, n_land_a, n_land_p, n_mid,
        (ngs, ngr, ncr, nar),
    )
    edge_ar = AllReduce(
        at, EDGE_PARTS, edge_flat, edge_sum, e_half, e_land_c, e_land_a, e_land_p, e_mid,
        (egs, egr, ecr, ear),
    )
    small_ar = SmallSum(at, small, small_out, sm, sm_land, ss, sr)
    node_ar.core_send(0)
    node_ar.core_send(1)

    def backward_out(i, carry):
        rows = rows_of(i)
        pltpu.make_async_copy(block(cot_edges_h, i), block(cots, i), cot_sems.at[i]).wait()
        ce = cots[rows, :].astype(F32)
        hat = hat_s[rows, :].astype(F32)
        d_message = ce + nn(ohr_s[rows, :], from_gathered)
        g_gain[...] += jnp.sum(d_message * hat, axis=0, keepdims=True)
        d_second = norm_back(d_message * eg[...], hat, scale_s[rows, :]).astype(BF16)
        g_out[...] += tn(active_s[rows, :], d_second)
        active_s[rows, :] = d_second
        return carry

    lax.fori_loop(0, CHUNKS, backward_out, 0)
    put_flat(node_flat, 3, g_out[...].astype(BF16))
    node_ar.core_send(2)

    def backward_in(i, carry):
        rows = rows_of(i)
        d_first = nn(active_s[rows, :], ewoT[...]) * slope_s[rows, :].astype(F32)
        g_bias[...] += jnp.sum(d_first, axis=0, keepdims=True)
        d_first = d_first.astype(BF16)
        slope_s[rows, :] = d_first
        g_in[...] += tn(edges[rows, :], d_first)
        pl.when(i == 0)(node_ar.core_sum)
        return carry

    lax.fori_loop(0, CHUNKS, backward_in, 0)

    put_flat(edge_flat, 0, g_in[...].astype(BF16))
    edge_ar.core_send(0)
    gr_sum = nn(oht_s[SLOTS:, :], slope_s[...]).astype(BF16)
    put_flat(edge_flat, 2, tn(x, gr_sum).astype(BF16))
    edge_ar.core_send(2)
    gs = nn(oht_s[0:SLOTS, :], slope_s[...]).astype(BF16)
    put_flat(edge_flat, 1, (tn(x, gs[0:N, :]) + tn(table[...], gs[N:SLOTS, :])).astype(BF16))
    edge_ar.core_send(1)
    put_small(small, 0, g_bias[...])
    put_small(small, 4, g_gain[...])
    small_ar.core_send()

    slots[...] = nn(gs[N:SLOTS, :], ewiT[:, D : 2 * D]).astype(BF16)
    for step in range(1, 8):
        peer = lax.rem(b + step, 8)
        send(
            slots.at[rows16(HALO + peer * 32, 32)], land_1b.at[rows16(b * 32, 32)], bs1, br1, (peer, t)
        )
    halo_swap(slots, halo_back, b, t, bhs, bhr)
    land_1b[rows16(b * 32, 32), :] = slots[rows16(HALO + b * 32, 32), :]

    @pl.when(b == 0)
    def _():
        halo_back[0:32, :] = jnp.zeros((32, D), BF16)

    @pl.when(b == 7)
    def _():
        halo_back[32:64, :] = jnp.zeros((32, D), BF16)

    def edge_grad(i):
        rows = slice(i * CHUNK, (i + 1) * CHUNK)
        cots[rows, :] = (nn(slope_s[rows, :], ewiT[:, 0:D]) + cots[rows, :].astype(F32)).astype(BF16)
        pltpu.make_async_copy(block(cots, i), block(grad_edges_h, i), out_sems.at[1, i]).start()

    def edge_result(i):
        rows = slice(i * CHUNK, (i + 1) * CHUNK)
        message = hat_s[rows, :].astype(F32) * eg[...]
        edges[rows, :] = (edges[rows, :].astype(F32) + message).astype(BF16)
        pltpu.make_async_copy(block(edges, i), block(edge_out_h, i), out_sems.at[0, i]).start()

    edge_ar.core_sum()
    small_ar.core_sum()
    node_ar.axis_sum()
    for i in range(CHUNKS):
        edge_grad(i)
    totals[...] += nn(gs[0:N, :], ewiT[:, D : 2 * D]) + nn(gr_sum, ewiT[:, 2 * D :])
    wait_bytes(land_1b.at[pl.ds(0, 224)], br1)
    far_2b[...] = nn(swap_order(16, 8), land_1b[...]).astype(BF16)
    for step in range(1, 16):
        peer = lax.rem(t + step, 16)
        send(
            far_2b.at[rows16(peer * 16, 16)], land_2b.at[rows16(t * 16, 16)], bs2, br2, (b, peer)
        )
    land_2b[rows16(t * 16, 16), :] = far_2b[rows16(t * 16, 16), :]
    edge_ar.axis_sum()
    small_ar.axis_sum(0)
    node_ar.plane_sum()
    for i in range(CHUNKS):
        edge_result(i)
    small_ar.axis_sum(1)
    edge_ar.plane_sum()
    node_ar.back_plane()
    halo_wait(slots, halo_back, b, bhs, bhr)
    wait_bytes(slots.at[pl.ds(0, 224)], bs1)
    wait_bytes(land_2b.at[pl.ds(0, 240)], br2)
    wait_bytes(far_2b.at[pl.ds(0, 240)], bs2)
    far_back = tn(order[...], land_2b[...]).astype(BF16)
    returned = tn(picks[...], jnp.concatenate([halo_back[...], far_back], axis=0))
    grad_nodes[...] = (totals[...] + returned).astype(BF16)
    grad_nodes_copy = pltpu.make_async_copy(grad_nodes, grad_nodes_h, late_sems.at[5])
    grad_nodes_copy.start()
    small_ar.axis_sum(2)
    small_copy = pltpu.make_async_copy(small_out, small_out_h, late_sems.at[6])
    small_copy.start()
    edge_ar.back_plane()
    for i in range(CHUNKS):
        pltpu.make_async_copy(block(edges, i), block(edge_out_h, i), out_sems.at[0, i]).wait()
        pltpu.make_async_copy(block(cots, i), block(grad_edges_h, i), out_sems.at[1, i]).wait()
    node_out_copy.wait()
    node_ar.back_axis()
    node_late, edge_late = late_sems.at[pl.ds(0, 2)], late_sems.at[pl.ds(2, 2)]
    node_ar.finish(node_sum_h, node_late)
    edge_ar.back_axis()
    edge_ar.finish(edge_sum_h, edge_late)
    grad_nodes_copy.wait()
    small_copy.wait()
    for part in range(2):
        node_ar.copy_out(node_sum_h, node_late, part).wait()
        edge_ar.copy_out(edge_sum_h, edge_late, part).wait()


def final_kernel(
    edge_sum, node_sum, small, node_out, edge_out, grad_nodes, grad_edges,
    node_out_h, edge_out_h, grad_nodes_h, grad_edges_h, ewi_h, eb, ewo_h, eg, nwi_h, nb, nwo_h, ng,
    wide, parts, small_s, rows_s, through, in_sems, move_sems, sems,
):
    targets = [(nwi_h, 0, node_sum, 0), (nwi_h, 512, node_sum, 1), (nwo_h, 0, node_sum, 2)]
    targets += [(ewo_h, 0, node_sum, 3)]
    targets += [(ewi_h, 0, edge_sum, 0), (ewi_h, 512, edge_sum, 1), (ewi_h, 1024, edge_sum, 2)]

    def fetch(j):
        _, _, source, piece = targets[j]
        return pltpu.make_async_copy(source.at[:, piece], parts.at[j], in_sems.at[j])

    small_copy = pltpu.make_async_copy(small, small_s, in_sems.at[7])
    for j in range(len(targets)):
        fetch(j).start()
    small_copy.start()
    copies = []
    moves = [(node_out, node_out_h, 0, N), (grad_nodes, grad_nodes_h, 0, N)]
    moves += [(edge_out, edge_out_h, 0, EDGES), (grad_edges, grad_edges_h, 0, EDGES)]
    places = [sum(size for _, _, _, size in moves[:j]) for j in range(len(moves))]

    def move(j, inward):
        source, target, first, size = moves[j]
        near = through.at[pl.ds(places[j], size)]
        if inward:
            return pltpu.make_async_copy(source.at[pl.ds(first, size)], near, move_sems.at[0, j])
        return pltpu.make_async_copy(near, target.at[pl.ds(first, size)], move_sems.at[1, j])

    for j in range(len(moves)):
        move(j, True).start()
    for j in range(len(moves)):
        move(j, True).wait()
        move(j, False).start()
        copies.append(move(j, False))
    for j, (ref, out_first, _, _) in enumerate(targets):
        fetch(j).wait()
        for k in range(4):
            wide[512 * j : 512 * (j + 1), 128 * k : 128 * (k + 1)] = parts[j, k // 2, k % 2].astype(F32)
        copy = pltpu.make_async_copy(
            wide.at[pl.ds(512 * j, 512)], ref.at[pl.ds(out_first, 512)], sems.at[4 + j]
        )
        copy.start()
        copies.append(copy)
    small_copy.wait()
    for j, ref in enumerate((eb, eg, nb, ng)):
        for k in range(4):
            rows_s[j, :, 128 * k : 128 * (k + 1)] = small_s[4 * j + k : 4 * j + k + 1, :]
        copy = pltpu.make_async_copy(rows_s.at[j], ref, sems.at[11 + j])
        copy.start()
        copies.append(copy)
    for copy in copies:
        copy.wait()


def vmem(count):
    return [pl.BlockSpec(memory_space=pltpu.VMEM)] * count


def shape(rows, dtype=BF16, width=D):
    return jax.ShapeDtypeStruct((rows, width), dtype)


def reduce_scratch(total):
    v, half = pltpu.VMEM, total // 2
    return [
        v((half, 128), BF16),
        v((half, 128), BF16),
        v((half // 4 * 3, 128), BF16),
        v((half // 64 * 15, 128), BF16),
        v((half // 4, 128), BF16),
    ]


def step(*operands):
    dma = pltpu.SemaphoreType.DMA
    hbm = pl.BlockSpec(memory_space=pltpu.HBM)
    v = pltpu.VMEM
    wide = v((EDGES, D), BF16)
    square = v((D, D), BF16)
    total = v((D, D), F32)
    return pl.pallas_call(
        step_kernel,
        out_shape=(
            shape(N),
            shape(N),
            shape(4 * EDGE_ROWS, BF16, 128),
            shape(4 * NODE_ROWS, BF16, 128),
            shape(16, F32, 128),
            shape(EDGES),
            shape(EDGES),
        ),
        in_specs=[pl.BlockSpec(memory_space=pltpu.SMEM)] + [hbm] * 16,
        out_specs=(hbm,) * 7,
        scratch_shapes=[
            v((1, 4, 32), jnp.int32),
            v((1, 2, 128), jnp.int32),
            v((1, EDGES), jnp.int32),
            v((1, EDGES), jnp.int32),
            v((N, D), BF16),
            v((N, D), BF16),
            v((1, D), F32),
            v((1, D), F32),
            v((1, D), F32),
            v((1, D), F32),
            wide,
            wide,
            v((3 * D, D), BF16),
            square,
            v((2 * D, D), BF16),
            square,
            v((D + 2 * N, D), BF16),
            v((TABLE, D), BF16),
            square,
            v((D, 3 * D), BF16),
            square,
            v((D, 2 * D), BF16),
            v((EDGES, D), F32),
            wide,
            wide,
            wide,
            v((EDGES, 1), F32),
            v((EDGES, N), BF16),
            v((TABLE, N), BF16),
            v((FAR, FAR), BF16),
            v((N, D), F32),
            total,
            total,
            v((1, D), F32),
            v((1, D), F32),
            v((N, D), F32),
            v((TABLE, D), BF16),
            v((16, 128), F32),
            v((TABLE, D), BF16),
            v((TABLE, D), BF16),
            v((FAR, D), BF16),
            v((FAR, D), BF16),
            v((4 * EDGE_ROWS, 128), BF16),
            v((4 * NODE_ROWS, 128), BF16),
        ]
        + reduce_scratch(4 * EDGE_ROWS)
        + reduce_scratch(4 * NODE_ROWS)
        + [
            v((EDGES, TABLE), BF16),
            v((SLOTS + N, EDGES), BF16),
            v((N, D), F32),
            v((N, D), BF16),
            v((N, D), BF16),
            v((4 * EDGE_ROWS, 128), BF16),
            v((4 * NODE_ROWS, 128), BF16),
            v((16, 128), F32),
            v((3, 16, 128), F32),
            v((13, 16, 128), F32),
            v((HALO, D), BF16),
            v((FAR, D), BF16),
            v((FAR, D), BF16),
            v((FAR, D), BF16),
            dma((7,)),
            dma((10,)),
            dma((CHUNKS,)),
            dma((CHUNKS,)),
            dma((4,)),
            dma((2, CHUNKS)),
        ]
        + [dma((4,)), dma((4,)), dma(()), dma(()), dma(()), dma(())] * 2
        + [dma((4,)), dma((4,))]
        + [dma((6, 3)), dma((6, 3)), dma((3, 4)), dma((3, 3))] * 2,
        compiler_params=pltpu.CompilerParams(
            collective_id=0, has_side_effects=True, vmem_limit_bytes=VMEM_LIMIT
        ),
    )(*operands)


def final(edge_sum, node_sum, small, node_out, edge_out, grad_nodes, grad_edges):
    hbm = pl.BlockSpec(memory_space=pl.ANY)
    v, dma = pltpu.VMEM, pltpu.SemaphoreType.DMA
    return pl.pallas_call(
        final_kernel,
        out_shape=(
            shape(N), shape(EDGES), shape(N), shape(EDGES),
            shape(1536, F32), shape(1, F32), shape(512, F32), shape(1, F32),
            shape(1024, F32), shape(1, F32), shape(512, F32), shape(1, F32),
        ),
        in_specs=[hbm] * 7,
        out_specs=(hbm,) * 12,
        scratch_shapes=[
            v((3584, D), F32),
            v((7, 2, 2, 512, 128), BF16),
            v((16, 128), F32),
            v((4, 1, D), F32),
            v((2 * N + 2 * EDGES, D), BF16),
            dma((8,)),
            dma((2, 4)),
            dma((15,)),
        ],
        compiler_params=pltpu.CompilerParams(vmem_limit_bytes=VMEM_LIMIT),
    )(edge_sum.reshape(2, 3, 2, 512, 128), node_sum.reshape(2, 4, 2, 512, 128), small, node_out, edge_out, grad_nodes, grad_edges)


def shards(
    node_latents, edge_latents, edge_count, receiver, sender, halo_send, far_send,
    edge_weight_in, edge_bias, edge_weight_out, edge_gain,
    node_weight_in, node_bias, node_weight_out, node_gain, cot_nodes, cot_edges,
):
    node_out, grad_nodes, edge_sum, node_sum, small, edge_out, grad_edges = step(
        edge_count, halo_send, far_send.transpose(0, 2, 1), sender.reshape(1, EDGES), receiver.reshape(1, EDGES),
        node_latents, cot_nodes,
        edge_bias.reshape(1, D), edge_gain.reshape(1, D), node_bias.reshape(1, D), node_gain.reshape(1, D),
        edge_latents, cot_edges, edge_weight_in, edge_weight_out, node_weight_in, node_weight_out,
    )
    outs = final(edge_sum, node_sum, small, node_out, edge_out, grad_nodes, grad_edges)
    return tuple(out.reshape(D) if out.shape[0] == 1 else out for out in outs)


def solution(mesh):
    split = ("lat", "lon")
    rows, flat = P(split, None), P(split)
    cube, whole = P(split, None, None), P()
    return jax.shard_map(
        shards,
        mesh=mesh,
        in_specs=(rows, rows, flat, flat, flat, cube, cube) + (whole,) * 8 + (rows, rows),
        out_specs=(rows, rows, rows, rows) + (whole,) * 8,
        check_vma=False,
    )
```
